32 devices in a mesh: grp: 2 (over y), bead: 4 (over z), space: 4 (over x, core).
Axes of the slice: x: 2, y: 2, z: 4, core: 2. Of those that a mesh axis runs over, the one named last changes fastest.
Arguments:
- positions: float32 [16, 3, 2048], P(('grp', 'bead'), None, 'space'), parts along dimension 0, may hold values from -6 to 6
- momenta: float32 [16, 3, 2048], P(('grp', 'bead'), None, 'space'), parts along dimension 0, may hold values from -6 to 6
- species: int32 [4096], P(('grp', 'space')), parts along dimension 0, may hold values from 0 to 3
- neighbour_index: int32 [32, 4096], P(None, ('grp', 'space')), parts along dimension 1, may hold values from 0 to 767, as said below
- neighbour_count: int32 [4096], P(('grp', 'space')), parts along dimension 0, may hold values from 1 to 32
- radial_rates: float32 [32], replicated, may hold values from 0.1 to 1
- weight_input: float32 [256, 128], replicated, may hold values from -0.5 to 0.5
- embedding: float32 [256, 4], replicated, may hold values from -6 to 6
- weight_middle: float32 [256, 256], replicated, may hold values from -0.375 to 0.375
- weight_deeper: float32 [256, 256], replicated, may hold values from -0.375 to 0.375
- weight_output: float32 [256], replicated, may hold values from -0.375 to 0.375
Outputs:
- momenta_next: float32 [16, 3, 2048], P(('grp', 'bead'), None, 'space'), parts along dimension 0
- displacement: float32 [16, 3, 2048], P(('grp', 'bead'), None, 'space'), parts along dimension 0
The draws below stay inside these ranges and needn't reach their ends.
There are 2 independent parts, one for each index of `grp`. The reference program is written for one: setup_inputs(seed, part) draws one part's arguments, and reference() takes and returns one part's arrays. A program takes and returns all parts, laid end to end along the dimension named above; an argument that names none is the same for every part. Nothing has to cross between parts.
Inputs may be any that keep to these rules, and one draw needn't show every extreme that they name: `neighbour_index`: each atom's slots name atoms within 128 places of itself in the extended slab, never itself.
All inputs are finite; a program needn't handle non-finite values.
Results may differ from the reference program's by a relative error of at most 0.00005.
Values sent between devices are 32-bit elements; how exact they have to be, the bound alone decides.
No kernel may reach another device: no remote copies, remote signals or barrier semaphores. Data moves between devices by JAX's collectives and lax.ppermute only.
A program may use at most 64 MiB of HBM per device.

```python
import math
import jax
import jax.numpy as jnp
from jax import lax

ATOM_DEV = 512
HALO = 128
NC = 4
NB = 32
RB = 32
SPECIES = 4
HID = 256
BEADS = 8
NATOM = 2048


def draw_neighbour_index(key, part):
    offsets = jax.random.randint(key, (NB, NATOM), 0, 2 * HALO)
    offsets = jnp.where(offsets >= HALO, offsets + 1, offsets)
    local_ids = jnp.arange(NATOM, dtype=jnp.int32) % ATOM_DEV
    result = local_ids[None, :] + offsets
    result = result.at[0, ATOM_DEV - 1::ATOM_DEV].set(ATOM_DEV + 2 * HALO - 1)
    result = result.at[0, ::ATOM_DEV].set(0)
    return result.astype(jnp.int32)


def draw_neighbour_count(key, part):
    slab_ids = jnp.arange(NATOM, dtype=jnp.int32) // ATOM_DEV
    lowest = 1 + (NB - 1) * (slab_ids % 4) // 4
    counts = jax.random.randint(key, (NATOM,), lowest, NB + 1)
    counts = counts.at[::ATOM_DEV].set(NB)
    counts = counts.at[1::ATOM_DEV].set(1)
    return counts.astype(jnp.int32)


def touch_ends(values, own_key, least, high):
    longest = values.shape.index(max(values.shape))
    spots = []
    for shift in (0, 1):
        where = [jax.random.randint(jax.random.fold_in(own_key, axis), (), 0, length) for axis, length in enumerate(values.shape)]
        where[longest] = (where[longest] + shift) % values.shape[longest]
        spots.append(tuple(where))
    return values.at[spots[0]].set(least).at[spots[1]].set(high)


def shard_levels(rng, shape, split, least, top_value):
    def one(axis_at, blocks):
        heights = jax.random.uniform(jax.random.fold_in(jax.random.fold_in(rng, 6), axis_at), (blocks,), jnp.float32, least / len(split), top_value / len(split))
        return jnp.repeat(jnp.exp(heights), shape[axis_at] // blocks).reshape((-1,) + (1,) * (len(shape) - axis_at - 1))

    factor_of = one(*split[0])
    for cut in split[1:]:
        factor_of = factor_of * one(*cut)
    return factor_of


def normal_values(own_key, dims, deviation, most, split=(), kind=jnp.bfloat16):
    drawn = deviation * jax.random.normal(own_key, dims, jnp.float32)
    if split:
        drawn = drawn * shard_levels(own_key, dims, split, -0.22, 0.18)
    return jnp.clip(drawn, -most, most).astype(kind)


def setup_inputs(seed: int = 0, part: int = 0) -> dict:
    key_of = jax.random.split(jax.random.key(seed), 12)
    part_keys = jax.random.split(jax.random.fold_in(key_of[11], part), 12)
    return {
        "positions": normal_values(part_keys[0], (BEADS, 3, NATOM), 1.0, 6.0, ((0, 4), (2, 4)), jnp.float32),
        "momenta": normal_values(part_keys[1], (BEADS, 3, NATOM), 1.0, 6.0, ((0, 4), (2, 4)), jnp.float32),
        "species": touch_ends(jax.random.randint(part_keys[2], (NATOM,), 0, SPECIES), jax.random.fold_in(part_keys[2], 1), 0, SPECIES - 1).astype(jnp.int32),
        "neighbour_index": draw_neighbour_index(jax.random.fold_in(jax.random.fold_in(key_of[11], part), 71), part),
        "neighbour_count": draw_neighbour_count(jax.random.fold_in(jax.random.fold_in(key_of[11], part), 71), part),
        "radial_rates": jnp.clip(jnp.exp(jax.random.uniform(key_of[5], (RB,), jnp.float32, math.log(0.1), math.log(1.0))), 0.1, 1.0),
        "weight_input": normal_values(key_of[6], (HID, SPECIES * RB), (SPECIES * RB) ** -0.5, 0.5, (), jnp.float32),
        "embedding": normal_values(key_of[7], (HID, SPECIES), 1.0, 6.0, (), jnp.float32),
        "weight_middle": normal_values(key_of[8], (HID, HID), HID ** -0.5, 0.375, (), jnp.float32),
        "weight_deeper": normal_values(key_of[9], (HID, HID), HID ** -0.5, 0.375, (), jnp.float32),
        "weight_output": normal_values(key_of[10], (HID,), HID ** -0.5, 0.375, (), jnp.float32),
    }


MASS_TABLE = (1.0, 0.25, 1.5, 2.0)
SPRING_RATE = 0.2
TIME_STEP = 0.5

def contraction_table(bead_count, kept_modes):
    row_ids = jnp.arange(kept_modes).astype(jnp.float32)[:, None]
    col_ids = jnp.arange(bead_count).astype(jnp.float32)[None, :]
    angles = 2.0 * jnp.pi * (row_ids / kept_modes - col_ids / bead_count)
    summed = jnp.ones_like(angles)
    for order in range(1, kept_modes // 2):
        summed = summed + 2.0 * jnp.cos(order * angles)
    summed = summed + jnp.cos(kept_modes // 2 * angles)
    return summed / bead_count

def atom_masses(species_real):
    masses = jnp.zeros_like(species_real)
    for kind_id in range(SPECIES):
        masses = masses + jnp.where(species_real == kind_id, MASS_TABLE[kind_id], 0.0)
    return masses

def atom_energy(centre, centre_species, neighbours, neighbour_species, present, radial_rates, weight_input, embedding, weight_middle, weight_deeper, weight_output):
    offsets = neighbours - centre[:, None, :]
    distance_sq = lax.optimization_barrier(jnp.sum(offsets * offsets, axis=0))
    radial = jnp.exp(-radial_rates[:, None, None] * distance_sq[None]) * present[None]
    species_ids = jnp.arange(SPECIES).astype(jnp.float32)
    onehot = (neighbour_species[None] == species_ids[:, None, None]).astype(jnp.float32)
    descriptor = jnp.einsum('snb,mnb->smb', onehot, radial, precision=lax.Precision.HIGHEST)
    descriptor = descriptor.reshape(SPECIES * radial.shape[0], radial.shape[2])
    centre_onehot = (centre_species[None] == species_ids[:, None]).astype(jnp.float32)
    hidden = jnp.dot(weight_input, descriptor, precision=lax.Precision.HIGHEST, preferred_element_type=jnp.float32)
    hidden = jax.nn.silu(hidden + jnp.dot(embedding, centre_onehot, precision=lax.Precision.HIGHEST, preferred_element_type=jnp.float32))
    hidden = jax.nn.silu(jnp.dot(weight_middle, hidden, precision=lax.Precision.HIGHEST, preferred_element_type=jnp.float32))
    hidden = jax.nn.silu(jnp.dot(weight_deeper, hidden, precision=lax.Precision.HIGHEST, preferred_element_type=jnp.float32))
    return jnp.dot(weight_output, hidden, precision=lax.Precision.HIGHEST, preferred_element_type=jnp.float32)

def reference(positions, momenta, species, neighbour_index, neighbour_count, radial_rates, weight_input, embedding, weight_middle, weight_deeper, weight_output):
    atom_total = positions.shape[2]
    table = contraction_table(BEADS, NC)
    contracted = jnp.einsum('kj,jca->kca', table, positions, precision=lax.Precision.HIGHEST)
    atom_ids = jnp.arange(atom_total, dtype=jnp.int32)
    slab_ids = atom_ids // ATOM_DEV
    targets = slab_ids[None, :] * ATOM_DEV + neighbour_index - HALO
    slot_ids = jnp.arange(NB, dtype=jnp.int32)[:, None]
    live = (slot_ids < neighbour_count[None, :]) & (targets >= 0) & (targets < atom_total)
    present = live.astype(jnp.float32)
    safe_targets = jnp.clip(targets, 0, atom_total - 1)
    species_real = species.astype(jnp.float32)
    neighbour_species = species_real[safe_targets]

    def energy(coords):
        neighbours = coords[:, safe_targets]
        return jnp.sum(atom_energy(coords, species_real, neighbours, neighbour_species, present, radial_rates, weight_input, embedding, weight_middle, weight_deeper, weight_output))
    replica_force = lax.map(lambda coords: -jax.grad(energy)(coords), contracted)
    expanded = BEADS / NC * jnp.einsum('kj,kca->jca', table, replica_force, precision=lax.Precision.HIGHEST)
    masses = atom_masses(species_real)
    laplace = 2.0 * positions - jnp.roll(positions, 1, axis=0) - jnp.roll(positions, -1, axis=0)
    spring = -SPRING_RATE * masses[None, None, :] * laplace
    momenta_next = momenta + TIME_STEP * (spring + expanded)
    displacement = TIME_STEP * momenta_next / masses[None, None, :]
    return (momenta_next, displacement)
```

```python
import jax
import jax.numpy as jnp
import numpy as np
from jax import lax
from jax.experimental import pallas as pl
from jax.experimental.pallas import tpu as pltpu
from jax.sharding import PartitionSpec as P

HALO = 128
NC = 4
SPECIES = 4
LANES = 128
DEAD = 4096
LOG2E = 1.4426950408889634

MASS_TABLE = (1.0, 0.25, 1.5, 2.0)
SPRING_RATE = 0.2
TIME_STEP = 0.5


def contraction_table(bead_count, kept_modes):
    rows = np.arange(kept_modes)[:, None] / kept_modes
    cols = np.arange(bead_count)[None, :] / bead_count
    angles = 2.0 * np.pi * (rows - cols)
    summed = np.ones_like(angles)
    for order in range(1, kept_modes // 2):
        summed = summed + 2.0 * np.cos(order * angles)
    summed = summed + np.cos(kept_modes // 2 * angles)
    return (summed / bead_count).astype(np.float32)


def per_species(species, values):
    picked = jnp.full(species.shape, values[0], jnp.float32)
    for kind in range(1, SPECIES):
        picked = jnp.where(species == kind, values[kind], picked)
    return picked


def split2(value):
    high = value.astype(jnp.bfloat16)
    low = (value - high.astype(jnp.float32)).astype(jnp.bfloat16)
    return high, low


def dot(lhs, rhs):
    return lax.dot_general(
        lhs, rhs, (((1,), (0,)), ((), ())), preferred_element_type=jnp.float32
    )


def dot_nt(lhs, rhs):
    return lax.dot_general(
        lhs, rhs, (((1,), (1,)), ((), ())), preferred_element_type=jnp.float32
    )


def weights_kernel(w1, emb, w2, w3, l1, l2, l3, t1, t2, t3):
    hid, chan = w1.shape
    high, low = split2(w1[...])
    l1[:, 0:chan] = high
    l1[:, 2 * chan : 3 * chan] = low
    l1[:, 3 * chan : 4 * chan] = high
    e = emb[...]
    eh, el = split2(e)
    ell = (e - eh.astype(jnp.float32) - el.astype(jnp.float32)).astype(jnp.bfloat16)
    l1[:, chan : 2 * chan] = jnp.concatenate(
        [eh, el, ell, jnp.zeros((hid, chan - 3 * SPECIES), jnp.bfloat16)], axis=1
    )
    t1[0:chan, :], t1[chan : 2 * chan, :] = split2(w1[...].T)
    for src, fwd, bwd in ((w2, l2, t2), (w3, l3, t3)):
        fwd[0:hid, :], fwd[hid : 2 * hid, :] = split2(src[...])
        bwd[0:hid, :], bwd[hid : 2 * hid, :] = split2(src[...].T)


def split_weights(w1, emb, w2, w3):
    hid, chan = w1.shape
    vmem = pl.BlockSpec(memory_space=pltpu.VMEM)
    shapes = [
        (hid, 4 * chan),
        (2 * hid, hid),
        (2 * hid, hid),
        (2 * chan, hid),
        (2 * hid, hid),
        (2 * hid, hid),
    ]
    return pl.pallas_call(
        weights_kernel,
        out_shape=[jax.ShapeDtypeStruct(s, jnp.bfloat16) for s in shapes],
        in_specs=[vmem] * 4,
        out_specs=[vmem] * len(shapes),
        name="split_weights",
    )(w1, emb, w2, w3)


def force_kernel(
    ext,
    code,
    rates,
    wout,
    l1,
    l2,
    l3,
    t1,
    t2,
    t3,
    out,
    off_s,
    kind_s,
    dist_s,
    rad_s,
    desc_s,
    grad_s,
    pair_s,
    rel_s,
):
    slots, block = code.shape
    groups = block // LANES
    rate_count = rates.shape[0]
    octets = rate_count // 8
    chan = SPECIES * rate_count
    hid = wout.shape[0]
    band = LANES + 2 * HALO
    rates2 = rates[...] * (-LOG2E)
    rate8 = [
        jnp.broadcast_to(rates2[8 * o : 8 * o + 8, :], (8, LANES))
        for o in range(octets)
    ]

    for g in range(groups):
        lane0 = g * LANES
        src = [
            [
                jnp.broadcast_to(
                    ext[c : c + 1, lane0 + LANES * q : lane0 + LANES * (q + 1)],
                    (8, LANES),
                )
                for q in range(band // LANES)
            ]
            for c in range(4)
        ]
        for o in range(slots // 8):
            rows = slice(8 * o, 8 * o + 8)
            cols = slice(lane0, lane0 + LANES)
            word = code[rows, cols]
            lane = jnp.bitwise_and(word, LANES - 1)
            part = jnp.bitwise_and(word, DEAD - 1)
            is0 = part < LANES
            is1 = part < 2 * LANES
            got = []
            for c in range(4):
                a, b, d = (
                    jnp.take_along_axis(src[c][q], lane, axis=1) for q in range(3)
                )
                got.append(jnp.where(is0, a, jnp.where(is1, b, d)))
            total = None
            for c in range(3):
                diff = got[c] - src[c][1]
                off_s[c, rows, cols] = diff
                total = diff * diff if total is None else total + diff * diff
            dist_s[rows, cols] = total
            kind_s[rows, cols] = jnp.where(word >= DEAD, -1.0, got[3])

    for g in range(groups):
        cols = slice(g * LANES, (g + 1) * LANES)
        acc = [[jnp.zeros((8, LANES), jnp.float32)] * octets for _ in range(SPECIES)]
        for n in range(slots):
            kind = jnp.broadcast_to(kind_s[n : n + 1, cols], (8, LANES))
            dist = jnp.broadcast_to(dist_s[n : n + 1, cols], (8, LANES))
            masks = [kind == float(s) for s in range(SPECIES)]
            for o in range(octets):
                radial = jnp.exp2(rate8[o] * dist)
                first = (n * octets + o) * 8
                rad_s[first : first + 8, cols] = radial
                for s in range(SPECIES):
                    acc[s][o] = acc[s][o] + jnp.where(masks[s], radial, 0.0)
        for s in range(SPECIES):
            for o in range(octets):
                first = s * rate_count + 8 * o
                desc_s[first : first + 8, cols] = acc[s][o]

    kinds = lax.broadcasted_iota(jnp.int32, (16, block), 0)
    kinds = jnp.where(kinds < 3 * SPECIES, kinds % SPECIES, -1).astype(jnp.float32)
    centre = ext[3:4, HALO : HALO + block]
    onehot = jnp.where(kinds == centre, 1.0, 0.0).astype(jnp.bfloat16)
    dh, dl = split2(desc_s[...])
    pad = jnp.zeros((chan - 16, block), jnp.bfloat16)
    first = dot(l1[:, 0 : 2 * chan], jnp.concatenate([dh, onehot, pad], axis=0))
    first = first + dot(l1[:, 2 * chan : 4 * chan], jnp.concatenate([dh, dl], axis=0))

    def act(x):
        sig = 1.0 / (1.0 + jnp.exp2(x * (-LOG2E)))
        value = x * sig
        return value, sig + value * (1.0 - sig)

    def layer(pair, x):
        high, low = split2(x)
        both = dot(pair[...], high)
        rows = pair.shape[0] // 2
        return both[0:rows] + (both[rows:] + dot(pair[0:rows, :], low))

    h1, s1 = act(first)
    h2, s2 = act(layer(l2, h1))
    _, s3 = act(layer(l3, h2))
    g3 = wout[...] * s3
    g2 = layer(t3, g3) * s2
    g1 = layer(t2, g2) * s1
    grad_s[...] = layer(t1, g1)

    rate_true = [
        jnp.broadcast_to(rates[8 * o : 8 * o + 8, :], (8, LANES)) for o in range(octets)
    ]
    for g in range(groups):
        cols = slice(g * LANES, (g + 1) * LANES)
        grads = [
            [
                grad_s[s * rate_count + 8 * o : s * rate_count + 8 * o + 8, cols]
                * rate_true[o]
                for o in range(octets)
            ]
            for s in range(SPECIES)
        ]
        for n in range(slots):
            kind = jnp.broadcast_to(kind_s[n : n + 1, cols], (8, LANES))
            masks = [kind == float(s) for s in range(SPECIES - 1)]
            total = None
            for o in range(octets):
                picked = grads[SPECIES - 1][o]
                for s in range(SPECIES - 1):
                    picked = jnp.where(masks[s], grads[s][o], picked)
                first = (n * octets + o) * 8
                term = picked * rad_s[first : first + 8, cols]
                total = term if total is None else total + term
            dist_s[n : n + 1, cols] = jnp.sum(total, axis=0, keepdims=True)

    for g in range(groups):
        cols = slice(g * LANES, (g + 1) * LANES)
        centre_force = [jnp.zeros((8, LANES), jnp.float32)] * 3
        for o in range(slots // 8):
            rows = slice(8 * o, 8 * o + 8)
            word = code[rows, cols]
            part = jnp.bitwise_and(word, DEAD - 1)
            rel_s[0, rows, cols] = jnp.bitwise_and(part, 63)
            rel_s[1, rows, cols] = jnp.right_shift(part, 6)
            slope = jnp.where(word >= DEAD, 0.0, 2.0 * dist_s[rows, cols])
            for c in range(3):
                force = slope * off_s[c, rows, cols]
                centre_force[c] = centre_force[c] + force
                high = force.astype(jnp.bfloat16).astype(jnp.float32)
                pair_s[2 * c, rows, cols] = high
                pair_s[2 * c + 1, rows, cols] = force - high
        for c in range(3):
            rad_s[c : c + 1, cols] = jnp.sum(centre_force[c], axis=0, keepdims=True)

    low_ids = lax.broadcasted_iota(jnp.int32, (64, LANES), 0)
    high_ids = lax.broadcasted_iota(jnp.int32, (8, LANES), 0)
    out[...] = jnp.zeros_like(out)
    for g in range(groups):
        cols = slice(g * LANES, (g + 1) * LANES)
        total = jnp.zeros((48, 64), jnp.float32)
        for n in range(0, slots, 2):
            lefts, rights = [], []
            for k in (n, n + 1):
                low = rel_s[0, k : k + 1, cols]
                high = jnp.broadcast_to(rel_s[1, k : k + 1, cols], (8, LANES))
                rights.append(jnp.where(low_ids == low, 1.0, 0.0).astype(jnp.bfloat16))
                hit = high_ids == high
                lefts.append(
                    jnp.concatenate(
                        [
                            jnp.where(
                                hit,
                                jnp.broadcast_to(
                                    pair_s[c, k : k + 1, cols], (8, LANES)
                                ),
                                0.0,
                            )
                            for c in range(6)
                        ],
                        axis=0,
                    ).astype(jnp.bfloat16)
                )
            total = total + dot_nt(
                jnp.concatenate(lefts, axis=1), jnp.concatenate(rights, axis=1)
            )
        for c in range(3):
            merged = total[16 * c : 16 * c + 8, :] + total[16 * c + 8 : 16 * c + 16, :]
            for q in range(band // 64):
                first = g * LANES + 64 * q
                out[c : c + 1, first : first + 64] = (
                    out[c : c + 1, first : first + 64] + merged[q : q + 1, :]
                )
    for c in range(3):
        out[c : c + 1, HALO : HALO + block] = (
            out[c : c + 1, HALO : HALO + block] - rad_s[c : c + 1, :]
        )


def window_forces(ext, code, rates, wout, pairs):
    slots, block = code.shape
    rate_count = rates.shape[0]
    vmem = pl.BlockSpec(memory_space=pltpu.VMEM)
    f32 = jnp.float32
    return pl.pallas_call(
        force_kernel,
        out_shape=jax.ShapeDtypeStruct((8, block + 2 * HALO), f32),
        in_specs=[vmem] * 10,
        out_specs=vmem,
        scratch_shapes=[
            pltpu.VMEM((3, slots, block), f32),
            pltpu.VMEM((slots, block), f32),
            pltpu.VMEM((slots, block), f32),
            pltpu.VMEM((slots * rate_count, block), f32),
            pltpu.VMEM((SPECIES * rate_count, block), f32),
            pltpu.VMEM((SPECIES * rate_count, block), f32),
            pltpu.VMEM((6, slots, block), f32),
            pltpu.VMEM((2, slots, block), jnp.int32),
        ],
        compiler_params=pltpu.CompilerParams(vmem_limit_bytes=32 * 1024 * 1024),
        name="window_forces",
    )(ext, code, rates[:, None], wout[:, None], *pairs)


def swap_with_adjacent(send_inner, send_outer):
    count = lax.axis_size("space")
    inner = [(i, i ^ 1) for i in range(count)]
    outer = [(i, (i + 1) % count if i % 2 else (i - 1) % count) for i in range(count)]
    return (
        lax.ppermute(send_inner, "space", inner),
        lax.ppermute(send_outer, "space", outer),
    )


def on_device(
    positions,
    momenta,
    species,
    neighbour_index,
    neighbour_count,
    radial_rates,
    weight_input,
    embedding,
    weight_middle,
    weight_deeper,
    weight_output,
):
    bead_dev = positions.shape[0]
    atom_dev = positions.shape[2]
    bead_groups = lax.axis_size("bead")
    slab_count = lax.axis_size("space")
    bead_count = bead_dev * bead_groups
    table = jnp.asarray(contraction_table(bead_count, NC))
    place = lax.axis_index("bead")
    slab = lax.axis_index("space")
    even = slab % 2 == 0
    replica = place % NC
    block_size = atom_dev * NC // bead_groups
    block_start = (place // NC) * block_size
    direct = bead_groups == NC

    pairs = split_weights(weight_input, embedding, weight_middle, weight_deeper)

    slots = lax.dynamic_slice_in_dim(neighbour_index, block_start, block_size, 1)
    counts = lax.dynamic_slice_in_dim(neighbour_count, block_start, block_size, 0)
    targets = slab * atom_dev + slots - HALO
    slot_ids = lax.broadcasted_iota(jnp.int32, slots.shape, 0)
    live = (slot_ids < counts[None, :]) & (targets >= 0) & (targets < atom_dev * slab_count)
    group_first = lax.broadcasted_iota(jnp.int32, slots.shape, 1) // LANES * LANES
    code = slots - block_start - group_first + jnp.where(live, 0, DEAD)

    if direct:
        others = [
            lax.ppermute(positions, "bead", [(i, i ^ k) for i in range(bead_groups)])
            for k in range(1, bead_groups)
        ]
        contracted = jnp.zeros(positions.shape[1:], jnp.float32)
        for k, block in enumerate([positions] + others):
            owner = jnp.bitwise_xor(place, k)
            for j in range(bead_dev):
                contracted = contracted + table[replica, owner * bead_dev + j] * block[j]
        odd_place = place % 2 == 1
        near, far = others[0], others[bead_groups - 2]
        below = jnp.where(odd_place, near[-1], far[-1])
        above = jnp.where(odd_place, far[0], near[0])
    else:
        everything = lax.all_gather(positions, "bead", axis=0, tiled=True)
        weights = lax.dynamic_index_in_dim(table, replica, 0, keepdims=False)
        contracted = jnp.sum(weights[:, None, None] * everything, axis=0)
        first = place * bead_dev
        below = lax.dynamic_index_in_dim(
            everything, (first - 1) % bead_count, 0, keepdims=False
        )
        above = lax.dynamic_index_in_dim(
            everything, (first + bead_dev) % bead_count, 0, keepdims=False
        )

    stacked = jnp.concatenate(
        [
            contracted,
            species.astype(jnp.float32)[None, :],
            jnp.zeros((4, atom_dev), jnp.float32),
        ],
        axis=0,
    )
    bottom, top = stacked[:, :HALO], stacked[:, atom_dev - HALO :]
    got_inner, got_outer = swap_with_adjacent(
        jnp.where(even, top, bottom), jnp.where(even, bottom, top)
    )
    extended = jnp.concatenate(
        [
            jnp.where(even, got_outer, got_inner),
            stacked,
            jnp.where(even, got_inner, got_outer),
        ],
        axis=1,
    )
    window = lax.dynamic_slice_in_dim(extended, block_start, block_size + 2 * HALO, 1)
    force = window_forces(window, code, radial_rates, weight_output, pairs)[:3]

    if not direct:
        partial = jnp.zeros((3, atom_dev + 2 * HALO), jnp.float32)
        partial = lax.dynamic_update_slice_in_dim(partial, force, block_start, 1)
        chosen = (jnp.arange(NC, dtype=jnp.int32) == replica).astype(jnp.float32)
        force = lax.psum(chosen[:, None, None] * partial[None], "bead")

    lower, own, upper = (
        force[..., :HALO],
        force[..., HALO : HALO + atom_dev],
        force[..., HALO + atom_dev :],
    )
    got_inner, got_outer = swap_with_adjacent(
        jnp.where(even, upper, lower), jnp.where(even, lower, upper)
    )
    own = jnp.concatenate(
        [
            own[..., :HALO] + jnp.where(even, got_outer, got_inner),
            own[..., HALO : atom_dev - HALO],
            own[..., atom_dev - HALO :] + jnp.where(even, got_inner, got_outer),
        ],
        axis=-1,
    )

    if direct:
        expanded = [jnp.zeros((3, atom_dev), jnp.float32)] * bead_dev
        for k in range(bead_groups):
            if k == 0:
                block = own
            else:
                block = lax.ppermute(own, "bead", [(i, i ^ k) for i in range(bead_groups)])
            owner = jnp.bitwise_xor(place, k)
            for j in range(bead_dev):
                expanded[j] = expanded[j] + table[owner, place * bead_dev + j] * block
        expanded = jnp.stack(expanded)
    else:
        columns = lax.dynamic_slice_in_dim(table, place * bead_dev, bead_dev, 1)
        expanded = jnp.sum(columns[:, :, None, None] * own[:, None], axis=0)
    expanded = bead_count / NC * expanded

    masses = per_species(species, MASS_TABLE)
    cycle = jnp.concatenate([below[None], positions, above[None]], axis=0)
    laplace = 2.0 * positions - cycle[:-2] - cycle[2:]
    spring = -SPRING_RATE * masses[None, None, :] * laplace
    momenta_next = momenta + TIME_STEP * (spring + expanded)
    displacement = TIME_STEP * momenta_next / masses[None, None, :]
    return (momenta_next, displacement)


def solution(mesh):
    return jax.shard_map(
        on_device,
        mesh=mesh,
        in_specs=(
            P(("grp", "bead"), None, "space"),
            P(("grp", "bead"), None, "space"),
            P(("grp", "space")),
            P(None, ("grp", "space")),
            P(("grp", "space")),
            P(),
            P(),
            P(),
            P(),
            P(),
            P(),
        ),
        out_specs=(P(("grp", "bead"), None, "space"), P(("grp", "bead"), None, "space")),
        check_vma=False,
    )
```

```python
import jax
import jax.numpy as jnp
import numpy as np
from jax import lax
from jax.experimental import pallas as pl
from jax.experimental.pallas import tpu as pltpu
from jax.sharding import PartitionSpec as P

HALO = 128
NC = 4
SPECIES = 4
LANES = 128
DEAD = 4096
LOG2E = 1.4426950408889634

MASS_TABLE = (1.0, 0.25, 1.5, 2.0)
SPRING_RATE = 0.2
TIME_STEP = 0.5


def contraction_table(bead_count, kept_modes):
    rows = np.arange(kept_modes)[:, None] / kept_modes
    cols = np.arange(bead_count)[None, :] / bead_count
    angles = 2.0 * np.pi * (rows - cols)
    summed = np.ones_like(angles)
    for order in range(1, kept_modes // 2):
        summed = summed + 2.0 * np.cos(order * angles)
    summed = summed + np.cos(kept_modes // 2 * angles)
    return (summed / bead_count).astype(np.float32)


def per_species(species, values):
    picked = jnp.full(species.shape, values[0], jnp.float32)
    for kind in range(1, SPECIES):
        picked = jnp.where(species == kind, values[kind], picked)
    return picked


def split2(value):
    high = value.astype(jnp.bfloat16)
    low = (value - high.astype(jnp.float32)).astype(jnp.bfloat16)
    return high, low


def dot(lhs, rhs):
    return lax.dot_general(
        lhs, rhs, (((1,), (0,)), ((), ())), preferred_element_type=jnp.float32
    )


def dot_nt(lhs, rhs):
    return lax.dot_general(
        lhs, rhs, (((1,), (1,)), ((), ())), preferred_element_type=jnp.float32
    )


def weights_kernel(w1, emb, w2, w3, rates, wout, l1, l2, l3, t1, t2, t3, rates_b, wout_b):
    hid, chan = w1.shape
    high, low = split2(w1[...])
    l1[:, 0:chan] = high
    l1[:, 2 * chan : 3 * chan] = low
    l1[:, 3 * chan : 4 * chan] = high
    e = emb[...]
    eh = e.astype(jnp.bfloat16).astype(jnp.float32)
    el = (e - eh).astype(jnp.bfloat16).astype(jnp.float32)
    terms = jnp.concatenate([eh, el, e - eh - el, jnp.zeros_like(e)], axis=0)
    terms = jnp.concatenate(
        [terms, jnp.zeros((chan - 4 * SPECIES, hid), jnp.float32)], axis=0
    )
    l1[:, chan : 2 * chan] = terms.T.astype(jnp.bfloat16)
    t1[0:chan, :], t1[chan : 2 * chan, :] = split2(w1[...].T)
    for src, fwd, bwd in ((w2, l2, t2), (w3, l3, t3)):
        fwd[0:hid, :], fwd[hid : 2 * hid, :] = split2(src[...])
        bwd[0:hid, :], bwd[hid : 2 * hid, :] = split2(src[...].T)
    count = rates.shape[1]
    tall = jnp.concatenate(
        [rates[...], jnp.zeros((1, LANES - count), jnp.float32)], axis=1
    )
    rates_b[...] = jnp.broadcast_to(tall, (LANES, LANES)).T[0:count, :]
    wout_b[...] = jnp.broadcast_to(wout[...], (LANES, hid)).T


def split_weights(w1, emb, w2, w3, rates, wout):
    hid, chan = w1.shape
    vmem = pl.BlockSpec(memory_space=pltpu.VMEM)
    shapes = [
        (hid, 4 * chan),
        (2 * hid, hid),
        (2 * hid, hid),
        (2 * chan, hid),
        (2 * hid, hid),
        (2 * hid, hid),
    ]
    out_shape = [pltpu.VMEM(s, jnp.bfloat16) for s in shapes]
    out_shape += [
        pltpu.VMEM((rates.shape[0], LANES), jnp.float32),
        pltpu.VMEM((hid, LANES), jnp.float32),
    ]
    return pl.pallas_call(
        weights_kernel,
        out_shape=out_shape,
        in_specs=[vmem] * 6,
        out_specs=[vmem] * len(out_shape),
        name="split_weights",
    )(w1, emb.T, w2, w3, rates[None, :], wout[None, :])


def force_kernel(
    ext,
    code,
    l1,
    l2,
    l3,
    t1,
    t2,
    t3,
    rates,
    wout,
    out,
    off_s,
    kind_s,
    dist_s,
    rad_s,
    desc_s,
    grad_s,
    pair_s,
    rel_s,
):
    slots, block = code.shape
    groups = block // LANES
    rate_count = rates.shape[0]
    octets = rate_count // 8
    chan = SPECIES * rate_count
    hid = wout.shape[0]
    band = LANES + 2 * HALO
    rate8 = [rates[8 * o : 8 * o + 8, :] * (-LOG2E) for o in range(octets)]

    for g in range(groups):
        lane0 = g * LANES
        src = [
            [
                jnp.broadcast_to(
                    ext[c : c + 1, lane0 + LANES * q : lane0 + LANES * (q + 1)],
                    (8, LANES),
                )
                for q in range(band // LANES)
            ]
            for c in range(4)
        ]
        for o in range(slots // 8):
            rows = slice(8 * o, 8 * o + 8)
            cols = slice(lane0, lane0 + LANES)
            word = code[rows, cols]
            lane = jnp.bitwise_and(word, LANES - 1)
            part = jnp.bitwise_and(word, DEAD - 1)
            is0 = part < LANES
            is1 = part < 2 * LANES
            got = []
            for c in range(4):
                a, b, d = (
                    jnp.take_along_axis(src[c][q], lane, axis=1) for q in range(3)
                )
                got.append(jnp.where(is0, a, jnp.where(is1, b, d)))
            total = None
            for c in range(3):
                diff = got[c] - src[c][1]
                off_s[c, rows, cols] = diff
                total = diff * diff if total is None else total + diff * diff
            dist_s[rows, cols] = total
            kind_s[rows, cols] = jnp.where(word >= DEAD, -1.0, got[3])

    for g in range(groups):
        cols = slice(g * LANES, (g + 1) * LANES)
        acc = [[jnp.zeros((8, LANES), jnp.float32)] * octets for _ in range(SPECIES)]
        for n in range(slots):
            kind = jnp.broadcast_to(kind_s[n : n + 1, cols], (8, LANES))
            dist = jnp.broadcast_to(dist_s[n : n + 1, cols], (8, LANES))
            masks = [kind == float(s) for s in range(SPECIES)]
            for o in range(octets):
                radial = jnp.exp2(rate8[o] * dist)
                first = (n * octets + o) * 8
                rad_s[first : first + 8, cols] = radial
                for s in range(SPECIES):
                    acc[s][o] = acc[s][o] + jnp.where(masks[s], radial, 0.0)
        for s in range(SPECIES):
            for o in range(octets):
                first = s * rate_count + 8 * o
                desc_s[first : first + 8, cols] = acc[s][o]

    kinds = lax.broadcasted_iota(jnp.int32, (16, block), 0)
    kinds = jnp.where(kinds < 3 * SPECIES, kinds % SPECIES, -1).astype(jnp.float32)
    centre = ext[3:4, HALO : HALO + block]
    onehot = jnp.where(kinds == centre, 1.0, 0.0).astype(jnp.bfloat16)
    dh, dl = split2(desc_s[...])
    pad = jnp.zeros((chan - 16, block), jnp.bfloat16)
    first = dot(l1[:, 0 : 2 * chan], jnp.concatenate([dh, onehot, pad], axis=0))
    first = first + dot(l1[:, 2 * chan : 4 * chan], jnp.concatenate([dh, dl], axis=0))

    def act(x):
        sig = 1.0 / (1.0 + jnp.exp2(x * (-LOG2E)))
        value = x * sig
        return value, sig + value * (1.0 - sig)

    def layer(pair, x):
        high, low = split2(x)
        both = dot(pair[...], high)
        rows = pair.shape[0] // 2
        return both[0:rows] + (both[rows:] + dot(pair[0:rows, :], low))

    h1, s1 = act(first)
    h2, s2 = act(layer(l2, h1))
    _, s3 = act(layer(l3, h2))
    g3 = jnp.concatenate([wout[...]] * groups, axis=1) * s3
    g2 = layer(t3, g3) * s2
    g1 = layer(t2, g2) * s1
    grad_s[...] = layer(t1, g1)

    rate_true = [rates[8 * o : 8 * o + 8, :] for o in range(octets)]
    for g in range(groups):
        cols = slice(g * LANES, (g + 1) * LANES)
        grads = [
            [
                grad_s[s * rate_count + 8 * o : s * rate_count + 8 * o + 8, cols]
                * rate_true[o]
                for o in range(octets)
            ]
            for s in range(SPECIES)
        ]
        for n in range(slots):
            kind = jnp.broadcast_to(kind_s[n : n + 1, cols], (8, LANES))
            masks = [kind == float(s) for s in range(SPECIES - 1)]
            total = None
            for o in range(octets):
                picked = grads[SPECIES - 1][o]
                for s in range(SPECIES - 1):
                    picked = jnp.where(masks[s], grads[s][o], picked)
                first = (n * octets + o) * 8
                term = picked * rad_s[first : first + 8, cols]
                total = term if total is None else total + term
            dist_s[n : n + 1, cols] = jnp.sum(total, axis=0, keepdims=True)

    for g in range(groups):
        cols = slice(g * LANES, (g + 1) * LANES)
        centre_force = [jnp.zeros((8, LANES), jnp.float32)] * 3
        for o in range(slots // 8):
            rows = slice(8 * o, 8 * o + 8)
            word = code[rows, cols]
            part = jnp.bitwise_and(word, DEAD - 1)
            rel_s[0, rows, cols] = jnp.bitwise_and(part, 63)
            rel_s[1, rows, cols] = jnp.right_shift(part, 6)
            slope = jnp.where(word >= DEAD, 0.0, 2.0 * dist_s[rows, cols])
            for c in range(3):
                force = slope * off_s[c, rows, cols]
                centre_force[c] = centre_force[c] + force
                high = force.astype(jnp.bfloat16).astype(jnp.float32)
                pair_s[2 * c, rows, cols] = high
                pair_s[2 * c + 1, rows, cols] = force - high
        for c in range(3):
            rad_s[c : c + 1, cols] = jnp.sum(centre_force[c], axis=0, keepdims=True)

    low_ids = lax.broadcasted_iota(jnp.int32, (64, LANES), 0)
    high_ids = lax.broadcasted_iota(jnp.int32, (8, LANES), 0)
    out[...] = jnp.zeros_like(out)
    for g in range(groups):
        cols = slice(g * LANES, (g + 1) * LANES)
        total = jnp.zeros((48, 64), jnp.float32)
        for n in range(0, slots, 2):
            lefts, rights = [], []
            for k in (n, n + 1):
                low = rel_s[0, k : k + 1, cols]
                high = jnp.broadcast_to(rel_s[1, k : k + 1, cols], (8, LANES))
                rights.append(jnp.where(low_ids == low, 1.0, 0.0).astype(jnp.bfloat16))
                hit = high_ids == high
                lefts.append(
                    jnp.concatenate(
                        [
                            jnp.where(
                                hit,
                                jnp.broadcast_to(
                                    pair_s[c, k : k + 1, cols], (8, LANES)
                                ),
                                0.0,
                            )
                            for c in range(6)
                        ],
                        axis=0,
                    ).astype(jnp.bfloat16)
                )
            total = total + dot_nt(
                jnp.concatenate(lefts, axis=1), jnp.concatenate(rights, axis=1)
            )
        for c in range(3):
            merged = total[16 * c : 16 * c + 8, :] + total[16 * c + 8 : 16 * c + 16, :]
            for q in range(band // 64):
                first = g * LANES + 64 * q
                out[c : c + 1, first : first + 64] = (
                    out[c : c + 1, first : first + 64] + merged[q : q + 1, :]
                )
    for c in range(3):
        out[c : c + 1, HALO : HALO + block] = (
            out[c : c + 1, HALO : HALO + block] - rad_s[c : c + 1, :]
        )


def window_forces(ext, code, prepared):
    slots, block = code.shape
    rate_count = prepared[6].shape[0]
    vmem = pl.BlockSpec(memory_space=pltpu.VMEM)
    f32 = jnp.float32
    return pl.pallas_call(
        force_kernel,
        out_shape=jax.ShapeDtypeStruct((8, block + 2 * HALO), f32),
        in_specs=[vmem] * 10,
        out_specs=vmem,
        scratch_shapes=[
            pltpu.VMEM((3, slots, block), f32),
            pltpu.VMEM((slots, block), f32),
            pltpu.VMEM((slots, block), f32),
            pltpu.VMEM((slots * rate_count, block), f32),
            pltpu.VMEM((SPECIES * rate_count, block), f32),
            pltpu.VMEM((SPECIES * rate_count, block), f32),
            pltpu.VMEM((6, slots, block), f32),
            pltpu.VMEM((2, slots, block), jnp.int32),
        ],
        compiler_params=pltpu.CompilerParams(vmem_limit_bytes=32 * 1024 * 1024),
        name="window_forces",
    )(ext, code, *prepared)


def swap_with_adjacent(send_inner, send_outer):
    count = lax.axis_size("space")
    inner = [(i, i ^ 1) for i in range(count)]
    outer = [(i, (i + 1) % count if i % 2 else (i - 1) % count) for i in range(count)]
    return (
        lax.ppermute(send_inner, "space", inner),
        lax.ppermute(send_outer, "space", outer),
    )


def on_device(
    positions,
    momenta,
    species,
    neighbour_index,
    neighbour_count,
    radial_rates,
    weight_input,
    embedding,
    weight_middle,
    weight_deeper,
    weight_output,
):
    bead_dev = positions.shape[0]
    atom_dev = positions.shape[2]
    bead_groups = lax.axis_size("bead")
    slab_count = lax.axis_size("space")
    bead_count = bead_dev * bead_groups
    table = contraction_table(bead_count, NC)
    place = lax.axis_index("bead")
    slab = lax.axis_index("space")
    even = slab % 2 == 0
    replica = place % NC
    block_size = atom_dev * NC // bead_groups
    block_start = (place // NC) * block_size
    direct = bead_groups == NC

    prepared = split_weights(
        weight_input, embedding, weight_middle, weight_deeper, radial_rates, weight_output
    )

    slots = lax.dynamic_slice_in_dim(neighbour_index, block_start, block_size, 1)
    counts = lax.dynamic_slice_in_dim(neighbour_count, block_start, block_size, 0)
    targets = slab * atom_dev + slots - HALO
    slot_ids = lax.broadcasted_iota(jnp.int32, slots.shape, 0)
    live = (slot_ids < counts[None, :]) & (targets >= 0) & (targets < atom_dev * slab_count)
    group_first = lax.broadcasted_iota(jnp.int32, slots.shape, 1) // LANES * LANES
    code = slots - block_start - group_first + jnp.where(live, 0, DEAD)

    own_beads = positions.transpose(1, 0, 2)
    if direct:
        pairs = [[(i, i ^ k) for i in range(NC)] for k in range(NC)]
        blocks = [own_beads] + [
            lax.ppermute(own_beads, "bead", pairs[k]) for k in range(1, NC)
        ]
        odd_place = place % 2 == 1

        def share(k, j, expand):
            ahead, behind = k % NC, -k % NC
            if expand:
                values = table[ahead, j], table[behind, j]
            else:
                values = table[0, ahead * bead_dev + j], table[0, behind * bead_dev + j]
            if values[0] == values[1]:
                return values[0]
            return jnp.where(odd_place, values[1], values[0])

        contracted = jnp.zeros((3, atom_dev), jnp.float32)
        for k in range(NC):
            for j in range(bead_dev):
                contracted = contracted + share(k, j, False) * blocks[k][:, j]
        below = jnp.where(odd_place, blocks[1][:, -1], blocks[NC - 1][:, -1])
        above = jnp.where(odd_place, blocks[NC - 1][:, 0], blocks[1][:, 0])
    else:
        everything = lax.all_gather(own_beads, "bead", axis=1, tiled=True)
        weights = lax.dynamic_index_in_dim(jnp.asarray(table), replica, 0, keepdims=False)
        contracted = jnp.sum(weights[None, :, None] * everything, axis=1)
        first = place * bead_dev
        below = lax.dynamic_index_in_dim(
            everything, (first - 1) % bead_count, 1, keepdims=False
        )
        above = lax.dynamic_index_in_dim(
            everything, (first + bead_dev) % bead_count, 1, keepdims=False
        )

    stacked = jnp.concatenate(
        [
            contracted,
            species.astype(jnp.float32)[None, :],
            jnp.zeros((4, atom_dev), jnp.float32),
        ],
        axis=0,
    )
    bottom, top = stacked[:, :HALO], stacked[:, atom_dev - HALO :]
    got_inner, got_outer = swap_with_adjacent(
        jnp.where(even, top, bottom), jnp.where(even, bottom, top)
    )
    extended = jnp.concatenate(
        [
            jnp.where(even, got_outer, got_inner),
            stacked,
            jnp.where(even, got_inner, got_outer),
        ],
        axis=1,
    )
    window = lax.dynamic_slice_in_dim(extended, block_start, block_size + 2 * HALO, 1)
    force = window_forces(window, code, prepared)[:3]

    if not direct:
        partial = jnp.zeros((3, atom_dev + 2 * HALO), jnp.float32)
        partial = lax.dynamic_update_slice_in_dim(partial, force, block_start, 1)
        chosen = (jnp.arange(NC, dtype=jnp.int32) == replica).astype(jnp.float32)
        force = lax.psum(chosen[:, None, None] * partial[None], "bead")

    lower, own, upper = (
        force[..., :HALO],
        force[..., HALO : HALO + atom_dev],
        force[..., HALO + atom_dev :],
    )
    got_inner, got_outer = swap_with_adjacent(
        jnp.where(even, upper, lower), jnp.where(even, lower, upper)
    )
    own = jnp.concatenate(
        [
            own[..., :HALO] + jnp.where(even, got_outer, got_inner),
            own[..., HALO : atom_dev - HALO],
            own[..., atom_dev - HALO :] + jnp.where(even, got_inner, got_outer),
        ],
        axis=-1,
    )

    if direct:
        expanded = [jnp.zeros((3, atom_dev), jnp.float32)] * bead_dev
        for k in range(NC):
            block = lax.ppermute(own, "bead", pairs[k]) if k else own
            for j in range(bead_dev):
                expanded[j] = expanded[j] + share(k, j, True) * block
        expanded = jnp.stack(expanded, axis=1)
    else:
        columns = lax.dynamic_slice_in_dim(
            jnp.asarray(table), place * bead_dev, bead_dev, 1
        )
        expanded = jnp.sum(columns[:, None, :, None] * own[:, :, None, :], axis=0)
    expanded = bead_count / NC * expanded

    masses = per_species(species, MASS_TABLE)
    cycle = jnp.concatenate([below[:, None], own_beads, above[:, None]], axis=1)
    laplace = 2.0 * own_beads - cycle[:, :-2] - cycle[:, 2:]
    spring = -SPRING_RATE * masses * laplace
    momenta_next = momenta.transpose(1, 0, 2) + TIME_STEP * (spring + expanded)
    displacement = TIME_STEP * momenta_next / masses
    return (momenta_next.transpose(1, 0, 2), displacement.transpose(1, 0, 2))


def solution(mesh):
    return jax.shard_map(
        on_device,
        mesh=mesh,
        in_specs=(
            P(("grp", "bead"), None, "space"),
            P(("grp", "bead"), None, "space"),
            P(("grp", "space")),
            P(None, ("grp", "space")),
            P(("grp", "space")),
            P(),
            P(),
            P(),
            P(),
            P(),
            P(),
        ),
        out_specs=(P(("grp", "bead"), None, "space"), P(("grp", "bead"), None, "space")),
        check_vma=False,
    )
```

```python
import functools

import jax
import jax.numpy as jnp
import numpy as np
from jax import lax
from jax.experimental import pallas as pl
from jax.experimental.pallas import tpu as pltpu
from jax.sharding import PartitionSpec as P

HALO = 128
NC = 4
SPECIES = 4
LANES = 128
DEAD = 4096
LOG2E = 1.4426950408889634

MASS_TABLE = (1.0, 0.25, 1.5, 2.0)
SPRING_RATE = 0.2
TIME_STEP = 0.5


def contraction_table(bead_count, kept_modes):
    rows = np.arange(kept_modes)[:, None] / kept_modes
    cols = np.arange(bead_count)[None, :] / bead_count
    angles = 2.0 * np.pi * (rows - cols)
    summed = np.ones_like(angles)
    for order in range(1, kept_modes // 2):
        summed = summed + 2.0 * np.cos(order * angles)
    summed = summed + np.cos(kept_modes // 2 * angles)
    return (summed / bead_count).astype(np.float32)


def per_species(species, values):
    picked = jnp.full(species.shape, values[0], jnp.float32)
    for kind in range(1, SPECIES):
        picked = jnp.where(species == kind, values[kind], picked)
    return picked


VMEM = pl.BlockSpec(memory_space=pltpu.VMEM)
SMEM = pl.BlockSpec(memory_space=pltpu.SMEM)


PARAMS = pltpu.CompilerParams(vmem_limit_bytes=16 * 1024 * 1024)


def cost(micros):
    return pl.CostEstimate(
        flops=0, transcendentals=0, bytes_accessed=int(micros * 3_000_000)
    )


def split2(value):
    high = value.astype(jnp.bfloat16)
    low = (value - high.astype(jnp.float32)).astype(jnp.bfloat16)
    return high, low


def dot(lhs, rhs):
    return lax.dot_general(
        lhs, rhs, (((1,), (0,)), ((), ())), preferred_element_type=jnp.float32
    )


def dot_nt(lhs, rhs):
    return lax.dot_general(
        lhs, rhs, (((1,), (1,)), ((), ())), preferred_element_type=jnp.float32
    )


def prepare_kernel(slab_atoms, block_start, *refs):
    held, outs = refs[:9], refs[9:19]
    copied, sems = refs[19:28], refs[28]
    copies = [
        pltpu.make_async_copy(src, dst, sems.at[i])
        for i, (src, dst) in enumerate(zip(held, copied, strict=True))
    ]
    for copy in copies:
        copy.start()
    slots, counts, species, w1, emb, w2, w3, rates, wout = copied
    code, kinds, l1, l2, l3, t1, t2, t3, rates_b, wout_b = outs
    for copy in copies[:3]:
        copy.wait()
    kinds[...] = species[...].astype(jnp.float32)

    slab = lax.axis_index("space")
    last = lax.axis_size("space") - 1
    lowest = jnp.where(slab == 0, HALO, 0)
    highest = jnp.where(slab == last, slab_atoms + HALO, slab_atoms + 2 * HALO)
    word = slots[...]
    slot_ids = lax.broadcasted_iota(jnp.int32, word.shape, 0)
    lane_ids = lax.broadcasted_iota(jnp.int32, word.shape, 1)
    live = (slot_ids < counts[...]) & (word >= lowest) & (word < highest)
    band = word - block_start() - jnp.bitwise_and(lane_ids, -LANES)
    code[...] = jnp.where(live, band, band + DEAD)

    for copy in copies[3:]:
        copy.wait()
    hid, chan = w1.shape
    high, low = split2(w1[...])
    l1[:, 0:chan] = high
    l1[:, 2 * chan : 3 * chan] = low
    l1[:, 3 * chan : 4 * chan] = high
    e = emb[...]
    eh = e.astype(jnp.bfloat16).astype(jnp.float32)
    el = (e - eh).astype(jnp.bfloat16).astype(jnp.float32)
    terms = jnp.concatenate([eh, el, e - eh - el, jnp.zeros_like(e)], axis=0)
    terms = jnp.concatenate(
        [terms, jnp.zeros((chan - 4 * SPECIES, hid), jnp.float32)], axis=0
    )
    l1[:, chan : 2 * chan] = terms.T.astype(jnp.bfloat16)
    t1[0:chan, :], t1[chan : 2 * chan, :] = split2(w1[...].T)
    for src, fwd, bwd in ((w2, l2, t2), (w3, l3, t3)):
        fwd[0:hid, :], fwd[hid : 2 * hid, :] = split2(src[...])
        bwd[0:hid, :], bwd[hid : 2 * hid, :] = split2(src[...].T)
    count = rates.shape[1]
    tall = jnp.concatenate(
        [rates[...], jnp.zeros((1, LANES - count), jnp.float32)], axis=1
    )
    rates_b[...] = jnp.broadcast_to(tall, (LANES, LANES)).T[0:count, :]
    wout_b[...] = jnp.broadcast_to(wout[...], (LANES, hid)).T


def prepare(slab_atoms, block_start, slots, counts, species, w1, emb, w2, w3, rates, wout):
    hid, chan = w1.shape
    shapes = [
        (hid, 4 * chan),
        (2 * hid, hid),
        (2 * hid, hid),
        (2 * chan, hid),
        (2 * hid, hid),
        (2 * hid, hid),
    ]
    out_shape = [
        pltpu.VMEM(slots.shape, jnp.int32),
        pltpu.VMEM(species.shape, jnp.float32),
    ]
    out_shape += [pltpu.VMEM(s, jnp.bfloat16) for s in shapes]
    out_shape += [
        pltpu.VMEM((rates.shape[0], LANES), jnp.float32),
        pltpu.VMEM((hid, LANES), jnp.float32),
    ]
    operands = (
        slots,
        counts[None, :],
        species,
        w1,
        emb.T,
        w2,
        w3,
        rates[None, :],
        wout[None, :],
    )
    code, kinds, *pairs, rates_b, wout_b = pl.pallas_call(
        functools.partial(prepare_kernel, slab_atoms, block_start),
        out_shape=out_shape,
        in_specs=[pl.BlockSpec(memory_space=pltpu.HBM)] * len(operands),
        out_specs=[VMEM] * len(out_shape),
        scratch_shapes=[pltpu.VMEM(x.shape, x.dtype) for x in operands]
        + [pltpu.SemaphoreType.DMA((len(operands),))],
        cost_estimate=cost(1.2),
        name="prepare",
    )(*operands)
    return code, kinds, pairs, rates_b, wout_b


def neighbours(places, word, g, off, kind, dist):
    src = [
        [
            jnp.broadcast_to(
                places[4 * (g + q) + c : 4 * (g + q) + c + 1, :], (8, LANES)
            )
            for q in range(3)
        ]
        for c in range(4)
    ]
    for o in range(word.shape[0] // 8):
        rows = slice(8 * o, 8 * o + 8)
        lane = jnp.bitwise_and(word[rows, :], LANES - 1)
        part = jnp.bitwise_and(word[rows, :], DEAD - 1)
        is0 = part < LANES
        is1 = part < 2 * LANES
        got = []
        for c in range(4):
            x0, x1, x2 = (
                jnp.take_along_axis(src[c][q], lane, axis=1) for q in range(3)
            )
            got.append(jnp.where(is0, x0, jnp.where(is1, x1, x2)))
        total = None
        for c in range(3):
            diff = got[c] - src[c][1]
            off[c, rows, :] = diff
            total = diff * diff if total is None else total + diff * diff
        dist[rows, :] = total
        kind[rows, :] = jnp.where(word[rows, :] >= DEAD, -1.0, got[3])


def describe(kind, dist, rates, rad, desc, cols):
    slots = kind.shape[0]
    rate_count = rates.shape[0]
    octets = rate_count // 8
    rate8 = [rates[8 * o : 8 * o + 8, :] * (-LOG2E) for o in range(octets)]
    acc = [[jnp.zeros((8, LANES), jnp.float32)] * octets for _ in range(SPECIES)]
    for n in range(slots):
        kind_n = jnp.broadcast_to(kind[n : n + 1, :], (8, LANES))
        dist_n = jnp.broadcast_to(dist[n : n + 1, :], (8, LANES))
        masks = [kind_n == float(s) for s in range(SPECIES)]
        for o in range(octets):
            radial = jnp.exp2(rate8[o] * dist_n)
            first = n * rate_count + 8 * o
            rad[first : first + 8, :] = radial
            for s in range(SPECIES):
                acc[s][o] = acc[s][o] + jnp.where(masks[s], radial, 0.0)
    for s in range(SPECIES):
        for o in range(octets):
            first = s * rate_count + 8 * o
            desc[first : first + 8, cols] = acc[s][o]


def network(desc, onehot, pairs, wout):
    l1, l2, l3, t1, t2, t3 = pairs
    chan, block = desc.shape
    dh, dl = split2(desc)
    pad = jnp.zeros((chan - onehot.shape[0], block), jnp.bfloat16)
    first = dot(l1[:, 0 : 2 * chan], jnp.concatenate([dh, onehot, pad], axis=0))
    first = first + dot(l1[:, 2 * chan : 4 * chan], jnp.concatenate([dh, dl], axis=0))

    def act(x):
        sig = 1.0 / (1.0 + jnp.exp2(x * (-LOG2E)))
        value = x * sig
        return value, sig + value * (1.0 - sig)

    def layer(pair, x):
        high, low = split2(x)
        both = dot(pair[...], high)
        rows = pair.shape[0] // 2
        return both[0:rows] + (both[rows:] + dot(pair[0:rows, :], low))

    h1, s1 = act(first)
    h2, s2 = act(layer(l2, h1))
    _, s3 = act(layer(l3, h2))
    g3 = jnp.concatenate([wout[...]] * (block // LANES), axis=1) * s3
    g2 = layer(t3, g3) * s2
    g1 = layer(t2, g2) * s1
    return layer(t1, g1)


def slot_slopes(grad, cols, kind, rates, rad, slope):
    slots = kind.shape[0]
    rate_count = rates.shape[0]
    octets = rate_count // 8
    grads = [
        [
            grad[s * rate_count + 8 * o : s * rate_count + 8 * o + 8, cols]
            * rates[8 * o : 8 * o + 8, :]
            for o in range(octets)
        ]
        for s in range(SPECIES)
    ]
    for n in range(slots):
        kind_n = jnp.broadcast_to(kind[n : n + 1, :], (8, LANES))
        masks = [kind_n == float(s) for s in range(SPECIES - 1)]
        total = None
        for o in range(octets):
            picked = grads[SPECIES - 1][o]
            for s in range(SPECIES - 1):
                picked = jnp.where(masks[s], grads[s][o], picked)
            first = n * rate_count + 8 * o
            term = picked * rad[first : first + 8, :]
            total = term if total is None else total + term
        slope[n : n + 1, :] = jnp.sum(total, axis=0, keepdims=True)


def pair_forces(word, slope, off, pair, rel):
    sums = [jnp.zeros((8, LANES), jnp.float32)] * 3
    for o in range(word.shape[0] // 8):
        rows = slice(8 * o, 8 * o + 8)
        part = jnp.bitwise_and(word[rows, :], DEAD - 1)
        rel[0, rows, :] = jnp.bitwise_and(part, 63)
        rel[1, rows, :] = jnp.right_shift(part, 6)
        twice = jnp.where(word[rows, :] >= DEAD, 0.0, 2.0 * slope[rows, :])
        for c in range(3):
            force = twice * off[c, rows, :]
            sums[c] = sums[c] + force
            high = force.astype(jnp.bfloat16).astype(jnp.float32)
            pair[2 * c, rows, :] = high
            pair[2 * c + 1, rows, :] = force - high
    return [jnp.sum(x, axis=0, keepdims=True) for x in sums]


def scatter(pair, rel, slots, out, block0, centre):
    low_ids = lax.broadcasted_iota(jnp.int32, (64, LANES), 0)
    high_ids = lax.broadcasted_iota(jnp.int32, (8, LANES), 0)
    total = jnp.zeros((48, 64), jnp.float32)
    for n in range(0, slots, 2):
        lefts, rights = [], []
        for k in (n, n + 1):
            low = rel[0, k : k + 1, :]
            high = jnp.broadcast_to(rel[1, k : k + 1, :], (8, LANES))
            rights.append(jnp.where(low_ids == low, 1.0, 0.0).astype(jnp.bfloat16))
            hit = high_ids == high
            picked = [
                jnp.where(hit, jnp.broadcast_to(pair[c, k : k + 1, :], (8, LANES)), 0.0)
                for c in range(6)
            ]
            lefts.append(jnp.concatenate(picked, axis=0).astype(jnp.bfloat16))
        total = total + dot_nt(
            jnp.concatenate(lefts, axis=1), jnp.concatenate(rights, axis=1)
        )
    for c in range(3):
        merged = total[16 * c : 16 * c + 8, :] + total[16 * c + 8 : 16 * c + 16, :]
        for q in range(3):
            row = 4 * (block0 + q) + c
            both = jnp.concatenate(
                [merged[2 * q : 2 * q + 1, :], merged[2 * q + 1 : 2 * q + 2, :]], axis=1
            )
            if q == 1:
                both = both - centre[c]
            out[row : row + 1, :] = out[row : row + 1, :] + both


def inner_kernel(own, code, rates, off, kind, rad, desc, dist):
    for i in range(kind.shape[0]):
        cols = slice(i * LANES, (i + 1) * LANES)
        word = code[:, (i + 1) * LANES : (i + 2) * LANES]
        neighbours(own, word, i, off.at[i], kind.at[i], dist)
        describe(kind.at[i], dist, rates, rad.at[i], desc, cols)


def inner_stage(own, code, rates, count):
    slots = code.shape[0]
    rate_count = rates.shape[0]
    out_shape = [
        pltpu.VMEM((count, 3, slots, LANES), jnp.float32),
        pltpu.VMEM((count, slots, LANES), jnp.float32),
        pltpu.VMEM((count, slots * rate_count, LANES), jnp.float32),
        pltpu.VMEM((SPECIES * rate_count, count * LANES), jnp.float32),
    ]
    return pl.pallas_call(
        inner_kernel,
        out_shape=out_shape,
        in_specs=[VMEM] * 3,
        out_specs=[VMEM] * 4,
        scratch_shapes=[pltpu.VMEM((slots, LANES), jnp.float32)],
        compiler_params=PARAMS,
        cost_estimate=cost(1.0),
        name="inner_descriptor",
    )(own, code, rates)


def outer_kernel(inner, *refs):
    ins = 10 + (1 if inner else 0)
    places, code, l1, l2, l3, t1, t2, t3, rates, wout = refs[:10]
    out = refs[ins]
    grad_inner = refs[ins + 1] if inner else None
    off, kind, dist, rad, desc, grad, pair, rel = refs[ins + (2 if inner else 1) :]
    slots, block = code.shape
    groups = block // LANES
    outer = sorted({0, groups - 1})
    order = outer + list(range(1, groups - 1))
    words = [code[:, g * LANES : (g + 1) * LANES] for g in outer]
    for i, g in enumerate(outer):
        cols = slice(i * LANES, (i + 1) * LANES)
        neighbours(places, words[i], g, off.at[i], kind.at[i], dist)
        describe(kind.at[i], dist, rates, rad.at[i], desc, cols)

    kinds = lax.broadcasted_iota(jnp.int32, (16, LANES), 0)
    kinds = jnp.where(
        kinds < 3 * SPECIES, jnp.bitwise_and(kinds, SPECIES - 1), -1
    ).astype(jnp.float32)
    onehot = jnp.concatenate(
        [
            jnp.where(kinds == places[4 * (g + 1) + 3 : 4 * (g + 1) + 4, :], 1.0, 0.0)
            for g in order
        ],
        axis=1,
    ).astype(jnp.bfloat16)
    whole = desc[...]
    if inner:
        whole = jnp.concatenate([whole, refs[10][...]], axis=1)
    slopes = network(whole, onehot, (l1, l2, l3, t1, t2, t3), wout)
    split = len(outer) * LANES
    grad[...] = slopes[:, :split]
    if inner:
        grad_inner[...] = slopes[:, split:]

    out[...] = jnp.zeros_like(out)
    for i, g in enumerate(outer):
        cols = slice(i * LANES, (i + 1) * LANES)
        slot_slopes(grad, cols, kind.at[i], rates, rad.at[i], dist)
        centre = pair_forces(words[i], dist, off.at[i], pair, rel)
        scatter(pair, rel, slots, out, g, centre)


def outer_stage(places, code, pairs, rates, wout, desc_inner):
    slots, block = code.shape
    rate_count = rates.shape[0]
    chan = SPECIES * rate_count
    groups = block // LANES
    count = len({0, groups - 1})
    inner = groups - count
    f32 = jnp.float32
    out_shape = [pltpu.VMEM((4 * (groups + 2), LANES), f32)]
    operands = [places, code, *pairs, rates, wout]
    if inner:
        out_shape.append(pltpu.VMEM((chan, inner * LANES), f32))
        operands.append(desc_inner)
    return pl.pallas_call(
        functools.partial(outer_kernel, inner),
        out_shape=out_shape,
        in_specs=[VMEM] * len(operands),
        out_specs=[VMEM] * len(out_shape),
        scratch_shapes=[
            pltpu.VMEM((count, 3, slots, LANES), f32),
            pltpu.VMEM((count, slots, LANES), f32),
            pltpu.VMEM((slots, LANES), f32),
            pltpu.VMEM((count, slots * rate_count, LANES), f32),
            pltpu.VMEM((chan, count * LANES), f32),
            pltpu.VMEM((chan, count * LANES), f32),
            pltpu.VMEM((6, slots, LANES), f32),
            pltpu.VMEM((2, slots, LANES), jnp.int32),
        ],
        compiler_params=PARAMS,
        cost_estimate=cost(3.0),
        name="outer_forces",
    )(*operands)


def inner_force_kernel(code, rates, off, kind, rad, grad, out, slope, pair, rel):
    slots = code.shape[0]
    out[...] = jnp.zeros_like(out)
    for i in range(kind.shape[0]):
        cols = slice(i * LANES, (i + 1) * LANES)
        word = code[:, (i + 1) * LANES : (i + 2) * LANES]
        slot_slopes(grad, cols, kind.at[i], rates, rad.at[i], slope)
        centre = pair_forces(word, slope, off.at[i], pair, rel)
        scatter(pair, rel, slots, out, i, centre)


def inner_forces(code, rates, off, kind, rad, grad):
    slots, block = code.shape
    return pl.pallas_call(
        inner_force_kernel,
        out_shape=pltpu.VMEM((block // LANES * 4, LANES), jnp.float32),
        in_specs=[VMEM] * 6,
        out_specs=VMEM,
        scratch_shapes=[
            pltpu.VMEM((slots, LANES), jnp.float32),
            pltpu.VMEM((6, slots, LANES), jnp.float32),
            pltpu.VMEM((2, slots, LANES), jnp.int32),
        ],
        compiler_params=PARAMS,
        cost_estimate=cost(1.2),
        name="inner_forces",
    )(code, rates, off, kind, rad, grad)


def bead_rows(array):
    beads, comps, atoms = array.shape
    split = array.reshape(beads, comps, atoms // LANES, LANES)
    return split.transpose(1, 2, 0, 3).reshape(-1, LANES)


def from_bead_rows(rows, shape):
    beads, comps, atoms = shape
    split = rows.reshape(comps, atoms // LANES, beads, LANES)
    return split.transpose(2, 0, 1, 3).reshape(shape)


def contract_kernel(table, beads, *refs):
    blocks, species, out = refs[:NC], refs[NC], refs[NC + 1]
    tiles = species.shape[0]
    for c in range(3):
        total = None
        for r in range(NC):
            for j in range(beads):
                rows = pl.ds(c * tiles * beads + j, tiles, stride=beads)
                term = float(table[r, j]) * blocks[r][rows, :]
                total = term if total is None else total + term
        out[pl.ds(c, tiles, stride=4), :] = total
    out[pl.ds(3, tiles, stride=4), :] = species[...]


def contract(table, beads, blocks, species):
    return pl.pallas_call(
        functools.partial(contract_kernel, table, beads),
        out_shape=pltpu.VMEM((4 * species.shape[0], LANES), jnp.float32),
        in_specs=[VMEM] * (NC + 1),
        out_specs=VMEM,
        compiler_params=PARAMS,
        cost_estimate=cost(0.2),
        name="contract",
    )(*blocks, species)


def masses_of(species):
    return per_species(species, MASS_TABLE)


def spring_kernel(beads, own, before, after, momenta, species, out):
    tiles = species.shape[0]
    pull = TIME_STEP * SPRING_RATE * masses_of(species[...])

    def row(ref, c, j):
        return ref[pl.ds(c * tiles * beads + j, tiles, stride=beads), :]

    for c in range(3):
        for j in range(beads):
            below = row(own, c, j - 1) if j else row(before, c, beads - 1)
            above = row(own, c, j + 1) if j + 1 < beads else row(after, c, 0)
            laplace = 2.0 * row(own, c, j) - below - above
            out[pl.ds(c * tiles * beads + j, tiles, stride=beads), :] = (
                row(momenta, c, j) - pull * laplace
            )


def spring_kick(beads, own, before, after, momenta, species):
    return pl.pallas_call(
        functools.partial(spring_kernel, beads),
        out_shape=pltpu.VMEM(own.shape, jnp.float32),
        in_specs=[VMEM] * 5,
        out_specs=VMEM,
        compiler_params=PARAMS,
        cost_estimate=cost(0.8),
        name="spring_kick",
    )(own, before, after, momenta, species)


def expand_kernel(table, beads, *refs):
    forces, kicked, species = refs[:NC], refs[NC], refs[NC + 1]
    momenta, displacement = refs[NC + 2 :]
    tiles = species.shape[0]
    scale = TIME_STEP * beads * NC / NC
    drift = per_species(species[...], [TIME_STEP / m for m in MASS_TABLE])
    for c in range(3):
        pulls = [force[pl.ds(c, tiles, stride=4), :] for force in forces]
        for j in range(beads):
            rows = pl.ds(c * tiles * beads + j, tiles, stride=beads)
            total = kicked[rows, :]
            for r in range(NC):
                total = total + (scale * float(table[-r % NC, j])) * pulls[r]
            momenta[rows, :] = total
            displacement[rows, :] = drift * total


def expand(table, beads, forces, kicked, species):
    shape = jax.ShapeDtypeStruct(kicked.shape, jnp.float32)
    return pl.pallas_call(
        functools.partial(expand_kernel, table, beads),
        out_shape=[shape, shape],
        in_specs=[VMEM] * (NC + 2),
        out_specs=[VMEM] * 2,
        compiler_params=PARAMS,
        cost_estimate=cost(0.8),
        name="expand",
    )(*forces, kicked, species)


def swap_with_adjacent(send_inner, send_outer):
    count = lax.axis_size("space")
    inner = [(i, i ^ 1) for i in range(count)]
    outer = [(i, (i + 1) % count if i % 2 else (i - 1) % count) for i in range(count)]
    return (
        lax.ppermute(send_inner, "space", inner),
        lax.ppermute(send_outer, "space", outer),
    )


def around(block):
    count = lax.axis_size("bead")
    blocks = [
        lax.ppermute(block, "bead", [(i, (i + r) % count) for i in range(count)])
        for r in range(count - 1, 0, -1)
    ]
    return [block] + blocks[::-1]


def on_device(
    positions,
    momenta,
    species,
    neighbour_index,
    neighbour_count,
    radial_rates,
    weight_input,
    embedding,
    weight_middle,
    weight_deeper,
    weight_output,
):
    bead_dev = positions.shape[0]
    atom_dev = positions.shape[2]
    bead_groups = lax.axis_size("bead")
    bead_count = bead_dev * bead_groups
    table = contraction_table(bead_count, NC)
    place = lax.axis_index("bead")
    slab = lax.axis_index("space")
    even = jnp.bitwise_and(slab, 1) == 0
    direct = bead_groups == NC
    block_size = atom_dev * NC // bead_groups
    tiles = atom_dev // LANES

    if direct:
        block_start = 0
        slots, counts = neighbour_index, neighbour_count
    else:
        block_start = (place // NC) * block_size
        slots = lax.dynamic_slice_in_dim(neighbour_index, block_start, block_size, 1)
        counts = lax.dynamic_slice_in_dim(neighbour_count, block_start, block_size, 0)
    code, kinds, pairs, rates, wout = prepare(
        atom_dev,
        lambda: 0 if direct else (lax.axis_index("bead") // NC) * block_size,
        slots,
        counts,
        species.reshape(tiles, LANES),
        weight_input,
        embedding,
        weight_middle,
        weight_deeper,
        radial_rates,
        weight_output,
    )

    if direct:
        blocks = around(bead_rows(positions))
        own = contract(table, bead_dev, blocks, kinds)
    else:
        replica = place % NC
        everything = lax.all_gather(positions, "bead", axis=0, tiled=True)
        weights = lax.dynamic_index_in_dim(jnp.asarray(table), replica, 0, keepdims=False)
        contracted = jnp.sum(weights[:, None, None] * everything, axis=0)
        stacked = contracted.reshape(3, tiles, LANES).transpose(1, 0, 2)
        own = jnp.concatenate([stacked, kinds[:, None]], axis=1).reshape(-1, LANES)

    bottom, top = own[:4], own[4 * tiles - 4 :]
    got_inner, got_outer = swap_with_adjacent(
        jnp.where(even, top, bottom), jnp.where(even, bottom, top)
    )
    inner_count = max(block_size // LANES - 2, 0)
    if inner_count:
        off, kind, rad, desc_inner = inner_stage(own, code, rates, inner_count)
    else:
        desc_inner = None
    window = jnp.concatenate(
        [
            jnp.where(even, got_outer, got_inner),
            own,
            jnp.where(even, got_inner, got_outer),
        ],
        axis=0,
    )
    if not direct:
        first = block_start // LANES * 4
        window = lax.dynamic_slice_in_dim(window, first, 4 * (block_size // LANES + 2), 0)
    force, *grad_inner = outer_stage(window, code, pairs, rates, wout, desc_inner)

    if not direct:
        partial = jnp.zeros((4 * (tiles + 2), LANES), jnp.float32)
        partial = lax.dynamic_update_slice_in_dim(partial, force, first, 0)
        chosen = (jnp.arange(NC, dtype=jnp.int32) == replica).astype(jnp.float32)
        force = lax.psum(chosen[:, None, None] * partial[None], "bead")

    lower, middle, upper = force[..., :4, :], force[..., 4:-4, :], force[..., -4:, :]
    got_inner, got_outer = swap_with_adjacent(
        jnp.where(even, upper, lower), jnp.where(even, lower, upper)
    )
    if inner_count:
        middle = middle + inner_forces(code, rates, off, kind, rad, *grad_inner)
    middle = jnp.concatenate(
        [
            middle[..., :4, :] + jnp.where(even, got_outer, got_inner),
            middle[..., 4:-4, :],
            middle[..., -4:, :] + jnp.where(even, got_inner, got_outer),
        ],
        axis=-2,
    )

    if direct:
        forces = around(middle)
        kicked = spring_kick(
            bead_dev, blocks[0], blocks[1], blocks[NC - 1], bead_rows(momenta), kinds
        )
        moved = expand(table, bead_dev, forces, kicked, kinds)
        return tuple(from_bead_rows(rows, positions.shape) for rows in moved)

    first = place * bead_dev
    below = lax.dynamic_index_in_dim(everything, (first - 1) % bead_count, 0)
    above = lax.dynamic_index_in_dim(everything, (first + bead_dev) % bead_count, 0)
    whole = middle.reshape(NC, tiles, 4, LANES).transpose(0, 2, 1, 3)[:, :3]
    whole = whole.reshape(NC, 3, atom_dev)
    columns = lax.dynamic_slice_in_dim(jnp.asarray(table), first, bead_dev, 1)
    expanded = jnp.sum(columns[:, :, None, None] * whole[:, None], axis=0)
    expanded = bead_count / NC * expanded
    masses = masses_of(species)
    cycle = jnp.concatenate([below, positions, above], axis=0)
    laplace = 2.0 * positions - cycle[:-2] - cycle[2:]
    spring = -SPRING_RATE * masses * laplace
    momenta_next = momenta + TIME_STEP * (spring + expanded)
    return (momenta_next, TIME_STEP * momenta_next / masses)


def solution(mesh):
    return jax.shard_map(
        on_device,
        mesh=mesh,
        in_specs=(
            P(("grp", "bead"), None, "space"),
            P(("grp", "bead"), None, "space"),
            P(("grp", "space")),
            P(None, ("grp", "space")),
            P(("grp", "space")),
            P(),
            P(),
            P(),
            P(),
            P(),
            P(),
        ),
        out_specs=(P(("grp", "bead"), None, "space"), P(("grp", "bead"), None, "space")),
        check_vma=False,
    )
```

```python
import functools

import jax
import jax.numpy as jnp
import numpy as np
from jax import lax
from jax.experimental import pallas as pl
from jax.experimental.pallas import tpu as pltpu
from jax.sharding import PartitionSpec as P

HALO = 128
NC = 4
SPECIES = 4
LANES = 128
DEAD = 4096
LOG2E = 1.4426950408889634

MASS_TABLE = (1.0, 0.25, 1.5, 2.0)
SPRING_RATE = 0.2
TIME_STEP = 0.5

GATHER = ("swap", (1, 3, 2))
SPREAD = ("turn", (3, 2, 1))


def contraction_table(bead_count, kept_modes):
    rows = np.arange(kept_modes)[:, None] / kept_modes
    cols = np.arange(bead_count)[None, :] / bead_count
    angles = 2.0 * np.pi * (rows - cols)
    summed = np.ones_like(angles)
    for order in range(1, kept_modes // 2):
        summed = summed + 2.0 * np.cos(order * angles)
    summed = summed + np.cos(kept_modes // 2 * angles)
    return (summed / bead_count).astype(np.float32)


def per_species(species, values):
    picked = jnp.full(species.shape, values[0], jnp.float32)
    for kind in range(1, SPECIES):
        picked = jnp.where(species == kind, values[kind], picked)
    return picked


VMEM = pl.BlockSpec(memory_space=pltpu.VMEM)
SMEM = pl.BlockSpec(memory_space=pltpu.SMEM)


PARAMS = pltpu.CompilerParams(vmem_limit_bytes=16 * 1024 * 1024)


def cost(micros):
    return pl.CostEstimate(
        flops=0, transcendentals=0, bytes_accessed=int(micros * 3_000_000)
    )


def at_even(axis):
    return jnp.bitwise_and(lax.axis_index(axis), 1) == 0


def split2(value):
    high = value.astype(jnp.bfloat16)
    low = (value - high.astype(jnp.float32)).astype(jnp.bfloat16)
    return high, low


def dot(lhs, rhs):
    return lax.dot_general(
        lhs, rhs, (((1,), (0,)), ((), ())), preferred_element_type=jnp.float32
    )


def dot_nt(lhs, rhs):
    return lax.dot_general(
        lhs, rhs, (((1,), (1,)), ((), ())), preferred_element_type=jnp.float32
    )


def prepare_kernel(slab_atoms, block_start, *refs):
    held, outs = refs[:9], refs[9:18]
    copied, sems = refs[18:27], refs[27]
    copies = [
        pltpu.make_async_copy(src, dst, sems.at[i])
        for i, (src, dst) in enumerate(zip(held, copied, strict=True))
    ]
    for copy in copies:
        copy.start()
    slots, counts, species, w1, emb, w2, w3, rates, wout = copied
    code, kinds, t1, t2, t3, l2, l3, rates_b, wout_b = outs
    for copy in copies[:3]:
        copy.wait()
    kinds[...] = species[...].astype(jnp.float32)

    slab = lax.axis_index("space")
    last = lax.axis_size("space") - 1
    lowest = jnp.where(slab == 0, HALO, 0)
    highest = jnp.where(slab == last, slab_atoms + HALO, slab_atoms + 2 * HALO)
    word = slots[...]
    slot_ids = lax.broadcasted_iota(jnp.int32, word.shape, 0)
    lane_ids = lax.broadcasted_iota(jnp.int32, word.shape, 1)
    live = (slot_ids < counts[...]) & (word >= lowest) & (word < highest)
    band = word - block_start() - jnp.bitwise_and(lane_ids, -LANES)
    code[...] = jnp.where(live, band, band + DEAD)

    for copy in copies[3:]:
        copy.wait()
    chan = w1.shape[1]
    t1[0:chan, :], t1[chan : 2 * chan, :] = split2(w1[...].T)
    e = emb[...]
    eh = e.astype(jnp.bfloat16).astype(jnp.float32)
    el = (e - eh).astype(jnp.bfloat16).astype(jnp.float32)
    rest = jnp.zeros((chan - 3 * SPECIES, e.shape[1]), jnp.float32)
    terms = jnp.concatenate([eh, el, e - eh - el, rest], axis=0)
    t1[2 * chan : 3 * chan, :] = terms.astype(jnp.bfloat16)
    for src, fwd, bwd in ((w2, t2, l2), (w3, t3, l3)):
        hid = src.shape[0]
        fwd[0:hid, :], fwd[hid : 2 * hid, :] = split2(src[...].T)
        bwd[0:hid, :], bwd[hid : 2 * hid, :] = split2(src[...])
    count = rates.shape[1]
    tall = jnp.concatenate(
        [rates[...], jnp.zeros((1, LANES - count), jnp.float32)], axis=1
    )
    rates_b[...] = jnp.broadcast_to(tall, (LANES, LANES)).T[0:count, :]
    wout_b[...] = jnp.broadcast_to(wout[...], wout_b.shape)


def prepare(slab_atoms, block_start, slots, counts, species, w1, emb, w2, w3, rates, wout):
    hid, chan = w1.shape
    shapes = [
        (3 * chan, hid),
        (2 * hid, hid),
        (2 * hid, hid),
        (2 * hid, hid),
        (2 * hid, hid),
    ]
    out_shape = [
        pltpu.VMEM(slots.shape, jnp.int32),
        pltpu.VMEM(species.shape, jnp.float32),
    ]
    out_shape += [pltpu.VMEM(s, jnp.bfloat16) for s in shapes]
    out_shape += [
        pltpu.VMEM((rates.shape[0], LANES), jnp.float32),
        pltpu.VMEM((8, hid), jnp.float32),
    ]
    operands = (
        slots,
        counts[None, :],
        species,
        w1,
        emb.T,
        w2,
        w3,
        rates[None, :],
        wout[None, :],
    )
    code, kinds, *pairs, rates_b, wout_b = pl.pallas_call(
        functools.partial(prepare_kernel, slab_atoms, block_start),
        out_shape=out_shape,
        in_specs=[pl.BlockSpec(memory_space=pltpu.HBM)] * len(operands),
        out_specs=[VMEM] * len(out_shape),
        scratch_shapes=[pltpu.VMEM(x.shape, x.dtype) for x in operands]
        + [pltpu.SemaphoreType.DMA((len(operands),))],
        cost_estimate=cost(1.2),
        name="prepare",
    )(*operands)
    return code, kinds, pairs, rates_b, wout_b


def neighbours(places, word, g, off, kind, dist):
    src = [
        [
            jnp.broadcast_to(
                places[4 * (g + q) + c : 4 * (g + q) + c + 1, :], (8, LANES)
            )
            for q in range(3)
        ]
        for c in range(4)
    ]
    for o in range(word.shape[0] // 8):
        rows = slice(8 * o, 8 * o + 8)
        lane = jnp.bitwise_and(word[rows, :], LANES - 1)
        part = jnp.bitwise_and(word[rows, :], DEAD - 1)
        is0 = part < LANES
        is1 = part < 2 * LANES
        got = []
        for c in range(4):
            x0, x1, x2 = (
                jnp.take_along_axis(src[c][q], lane, axis=1) for q in range(3)
            )
            got.append(jnp.where(is0, x0, jnp.where(is1, x1, x2)))
        total = None
        for c in range(3):
            diff = got[c] - src[c][1]
            off[c, rows, :] = diff
            total = diff * diff if total is None else total + diff * diff
        dist[rows, :] = total
        kind[rows, :] = jnp.where(word[rows, :] >= DEAD, -1.0, got[3])


def describe(kind, dist, rates, rad, desc):
    slots = kind.shape[0]
    rate_count = rates.shape[0]
    octets = rate_count // 8
    rate8 = [rates[8 * o : 8 * o + 8, :] * (-LOG2E) for o in range(octets)]
    acc = [[jnp.zeros((8, LANES), jnp.float32)] * octets for _ in range(SPECIES)]
    for n in range(slots):
        kind_n = jnp.broadcast_to(kind[n : n + 1, :], (8, LANES))
        dist_n = jnp.broadcast_to(dist[n : n + 1, :], (8, LANES))
        masks = [kind_n == float(s) for s in range(SPECIES)]
        for o in range(octets):
            radial = jnp.exp2(rate8[o] * dist_n)
            first = n * rate_count + 8 * o
            rad[first : first + 8, :] = radial
            for s in range(SPECIES):
                acc[s][o] = acc[s][o] + jnp.where(masks[s], radial, 0.0)
    for s in range(SPECIES):
        for o in range(octets):
            first = s * rate_count + 8 * o
            desc[first : first + 8, :] = acc[s][o]


def left_factor(desc, centre):
    chan = desc.shape[0]
    high, low = split2(desc[...].T)
    ids = lax.broadcasted_iota(jnp.int32, (chan, LANES), 0)
    ids = jnp.where(ids < 3 * SPECIES, jnp.bitwise_and(ids, SPECIES - 1), -1)
    onehot = jnp.where(ids.astype(jnp.float32) == centre, 1.0, 0.0)
    onehot = onehot.T.astype(jnp.bfloat16)
    return jnp.concatenate([high, high, low, onehot], axis=1)


def network(lefts, pairs, wout):
    t1, t2, t3, l2, l3 = pairs
    chan = t1.shape[0] // 3
    first = jnp.concatenate([t1[0 : 2 * chan, :], t1[0:chan, :], t1[2 * chan :, :]], axis=0)

    def act(x):
        sig = 0.5 + 0.5 * jnp.tanh(0.5 * x)
        value = x * sig
        return value, sig + value * (1.0 - sig)

    def layer(x, pair):
        high, low = split2(x)
        rows = pair.shape[0] // 2
        right = jnp.concatenate([pair[...], pair[0:rows, :]], axis=0)
        return dot(jnp.concatenate([high, high, low], axis=1), right)

    one = [act(dot(left, first)) for left in lefts]
    two = [act(layer(h, t2)) for h, _ in one]
    three = [act(layer(h, t3))[1] for h, _ in two]
    back = [wout[0:1, :] * s for s in three]
    back = [layer(g, l3) * s for g, (_, s) in zip(back, two)]
    back = [layer(g, l2) * s for g, (_, s) in zip(back, one)]
    last = jnp.concatenate(
        [t1[0:chan, :], t1[chan : 2 * chan, :], t1[0:chan, :]], axis=1
    )
    grads = []
    for g in back:
        high, low = split2(g)
        grads.append(dot_nt(last, jnp.concatenate([high, high, low], axis=1)))
    return grads


def slot_slopes(grad, kind, rates, rad, slope):
    slots = kind.shape[0]
    rate_count = rates.shape[0]
    octets = rate_count // 8
    grads = [
        [
            grad[s * rate_count + 8 * o : s * rate_count + 8 * o + 8, :]
            * rates[8 * o : 8 * o + 8, :]
            for o in range(octets)
        ]
        for s in range(SPECIES)
    ]
    for n in range(slots):
        kind_n = jnp.broadcast_to(kind[n : n + 1, :], (8, LANES))
        masks = [kind_n == float(s) for s in range(SPECIES - 1)]
        total = None
        for o in range(octets):
            picked = grads[SPECIES - 1][o]
            for s in range(SPECIES - 1):
                picked = jnp.where(masks[s], grads[s][o], picked)
            first = n * rate_count + 8 * o
            term = picked * rad[first : first + 8, :]
            total = term if total is None else total + term
        slope[n : n + 1, :] = jnp.sum(total, axis=0, keepdims=True)


def pair_forces(word, slope, off, pair, rel):
    sums = [jnp.zeros((8, LANES), jnp.float32)] * 3
    for o in range(word.shape[0] // 8):
        rows = slice(8 * o, 8 * o + 8)
        part = jnp.bitwise_and(word[rows, :], DEAD - 1)
        rel[0, rows, :] = jnp.bitwise_and(part, 63)
        rel[1, rows, :] = jnp.right_shift(part, 6)
        twice = jnp.where(word[rows, :] >= DEAD, 0.0, 2.0 * slope[rows, :])
        for c in range(3):
            force = twice * off[c, rows, :]
            sums[c] = sums[c] + force
            high = force.astype(jnp.bfloat16).astype(jnp.float32)
            pair[2 * c, rows, :] = high
            pair[2 * c + 1, rows, :] = force - high
    return [jnp.sum(x, axis=0, keepdims=True) for x in sums]


def scatter(pair, rel, slots, out, block0, centre):
    low_ids = lax.broadcasted_iota(jnp.int32, (64, LANES), 0)
    high_ids = lax.broadcasted_iota(jnp.int32, (8, LANES), 0)
    total = jnp.zeros((48, 64), jnp.float32)
    for n in range(0, slots, 2):
        lefts, rights = [], []
        for k in (n, n + 1):
            low = rel[0, k : k + 1, :]
            high = jnp.broadcast_to(rel[1, k : k + 1, :], (8, LANES))
            rights.append(jnp.where(low_ids == low, 1.0, 0.0).astype(jnp.bfloat16))
            hit = high_ids == high
            picked = [
                jnp.where(hit, jnp.broadcast_to(pair[c, k : k + 1, :], (8, LANES)), 0.0)
                for c in range(6)
            ]
            lefts.append(jnp.concatenate(picked, axis=0).astype(jnp.bfloat16))
        total = total + dot_nt(
            jnp.concatenate(lefts, axis=1), jnp.concatenate(rights, axis=1)
        )
    for c in range(3):
        merged = total[16 * c : 16 * c + 8, :] + total[16 * c + 8 : 16 * c + 16, :]
        for q in range(3):
            row = 4 * (block0 + q) + c
            both = jnp.concatenate(
                [merged[2 * q : 2 * q + 1, :], merged[2 * q + 1 : 2 * q + 2, :]], axis=1
            )
            if q == 1:
                both = both - centre[c]
            out[row : row + 1, :] = out[row : row + 1, :] + both


def inner_kernel(own, code, rates, off, kind, rad, left, dist, desc):
    for i in range(kind.shape[0]):
        word = code[:, (i + 1) * LANES : (i + 2) * LANES]
        neighbours(own, word, i, off.at[i], kind.at[i], dist)
        describe(kind.at[i], dist, rates, rad.at[i], desc)
        row = 4 * (i + 1) + 3
        left[i] = left_factor(desc, own[row : row + 1, :])


def inner_stage(own, code, rates, count):
    slots = code.shape[0]
    rate_count = rates.shape[0]
    chan = SPECIES * rate_count
    out_shape = [
        pltpu.VMEM((count, 3, slots, LANES), jnp.float32),
        pltpu.VMEM((count, slots, LANES), jnp.float32),
        pltpu.VMEM((count, slots * rate_count, LANES), jnp.float32),
        pltpu.VMEM((count, LANES, 4 * chan), jnp.bfloat16),
    ]
    return pl.pallas_call(
        inner_kernel,
        out_shape=out_shape,
        in_specs=[VMEM] * 3,
        out_specs=[VMEM] * 4,
        scratch_shapes=[
            pltpu.VMEM((slots, LANES), jnp.float32),
            pltpu.VMEM((chan, LANES), jnp.float32),
        ],
        compiler_params=PARAMS,
        cost_estimate=cost(1.0),
        name="inner_descriptor",
    )(own, code, rates)


def outer_kernel(direct, inner, *refs):
    refs = list(refs)

    def take(count):
        taken = refs[:count]
        del refs[:count]
        return taken

    blocks = take(3 if direct else 1)
    code, *pairs, rates, wout = take(9 - 1)
    left_inner = take(1)[0] if inner else None
    out = take(1)[0]
    to_inner, to_outer = take(2) if direct else (None, None)
    grad_inner = take(1)[0] if inner else None
    places, off, kind, dist, rad, desc, grad, pair, rel = refs
    slots, block = code.shape
    groups = block // LANES
    outer = sorted({0, groups - 1})
    if direct:
        own, got_outer, got_inner = blocks
        even = at_even("space")
        places[0:4, :] = jnp.where(even, got_outer[...], got_inner[...])
        places[4 : 4 * groups + 4, :] = own[...]
        places[4 * groups + 4 :, :] = jnp.where(even, got_inner[...], got_outer[...])
    else:
        places[...] = blocks[0][...]
    words = [code[:, g * LANES : (g + 1) * LANES] for g in outer]
    lefts = []
    for i, g in enumerate(outer):
        neighbours(places, words[i], g, off.at[i], kind.at[i], dist)
        describe(kind.at[i], dist, rates, rad.at[i], desc.at[i])
        row = 4 * (g + 1) + 3
        lefts.append(left_factor(desc.at[i], places[row : row + 1, :]))
    if inner:
        lefts += [left_inner[i] for i in range(left_inner.shape[0])]
    slopes = network(lefts, pairs, wout)
    for i in range(len(outer)):
        grad[i] = slopes[i]
    for i in range(len(outer), len(slopes)):
        grad_inner[i - len(outer)] = slopes[i]

    out[...] = jnp.zeros_like(out)
    for i, g in enumerate(outer):
        slot_slopes(grad.at[i], kind.at[i], rates, rad.at[i], dist)
        centre = pair_forces(words[i], dist, off.at[i], pair, rel)
        scatter(pair, rel, slots, out, g, centre)
    if direct:
        lower, upper = out[0:4, :], out[4 * groups + 4 :, :]
        to_inner[...] = jnp.where(even, upper, lower)
        to_outer[...] = jnp.where(even, lower, upper)


def outer_stage(blocks, code, pairs, rates, wout, left_inner):
    slots, block = code.shape
    rate_count = rates.shape[0]
    chan = SPECIES * rate_count
    groups = block // LANES
    count = len({0, groups - 1})
    inner = groups - count
    direct = len(blocks) > 1
    f32 = jnp.float32
    out_shape = [pltpu.VMEM((4 * (groups + 2), LANES), f32)]
    operands = [*blocks, code, *pairs, rates, wout]
    if direct:
        out_shape += [pltpu.VMEM((4, LANES), f32)] * 2
    if inner:
        out_shape.append(pltpu.VMEM((inner, chan, LANES), f32))
        operands.append(left_inner)
    return pl.pallas_call(
        functools.partial(outer_kernel, direct, inner),
        out_shape=out_shape,
        in_specs=[VMEM] * len(operands),
        out_specs=[VMEM] * len(out_shape),
        scratch_shapes=[
            pltpu.VMEM((4 * (groups + 2), LANES), f32),
            pltpu.VMEM((count, 3, slots, LANES), f32),
            pltpu.VMEM((count, slots, LANES), f32),
            pltpu.VMEM((slots, LANES), f32),
            pltpu.VMEM((count, slots * rate_count, LANES), f32),
            pltpu.VMEM((count, chan, LANES), f32),
            pltpu.VMEM((count, chan, LANES), f32),
            pltpu.VMEM((6, slots, LANES), f32),
            pltpu.VMEM((2, slots, LANES), jnp.int32),
        ],
        compiler_params=PARAMS,
        cost_estimate=cost(3.0),
        name="outer_forces",
    )(*operands)


def inner_force_kernel(code, rates, off, kind, rad, grad, out, slope, pair, rel):
    slots = code.shape[0]
    out[...] = jnp.zeros_like(out)
    for i in range(kind.shape[0]):
        word = code[:, (i + 1) * LANES : (i + 2) * LANES]
        slot_slopes(grad.at[i], kind.at[i], rates, rad.at[i], slope)
        centre = pair_forces(word, slope, off.at[i], pair, rel)
        scatter(pair, rel, slots, out, i, centre)


def inner_forces(code, rates, off, kind, rad, grad):
    slots, block = code.shape
    return pl.pallas_call(
        inner_force_kernel,
        out_shape=pltpu.VMEM((block // LANES * 4, LANES), jnp.float32),
        in_specs=[VMEM] * 6,
        out_specs=VMEM,
        scratch_shapes=[
            pltpu.VMEM((slots, LANES), jnp.float32),
            pltpu.VMEM((6, slots, LANES), jnp.float32),
            pltpu.VMEM((2, slots, LANES), jnp.int32),
        ],
        compiler_params=PARAMS,
        cost_estimate=cost(1.2),
        name="inner_forces",
    )(code, rates, off, kind, rad, grad)


def combine_kernel(inner, force, *refs):
    *rest, got_outer, got_inner, out = refs
    total = force[4 : force.shape[0] - 4, :]
    if inner:
        total = total + rest[0][...]
    even = at_even("space")
    out[...] = total
    out[0:4, :] += jnp.where(even, got_outer[...], got_inner[...])
    out[out.shape[0] - 4 :, :] += jnp.where(even, got_inner[...], got_outer[...])


def combine(force, inner, got_inner, got_outer):
    operands = [force, *inner, got_outer, got_inner]
    return pl.pallas_call(
        functools.partial(combine_kernel, len(inner)),
        out_shape=pltpu.VMEM((force.shape[0] - 8, LANES), jnp.float32),
        in_specs=[VMEM] * len(operands),
        out_specs=VMEM,
        compiler_params=PARAMS,
        cost_estimate=cost(0.1),
        name="combine",
    )(*operands)


def bead_rows(array):
    beads, comps, atoms = array.shape
    split = array.reshape(beads, comps, atoms // LANES, LANES)
    return split.transpose(1, 2, 0, 3).reshape(-1, LANES)


def from_bead_rows(rows, shape):
    beads, comps, atoms = shape
    split = rows.reshape(comps, atoms // LANES, beads, LANES)
    return split.transpose(2, 0, 1, 3).reshape(shape)


def contract_kernel(table, beads, *refs):
    blocks, species = arranged(GATHER, refs), refs[NC]
    out, to_inner, to_outer = refs[NC + 1 :]
    tiles = species.shape[0]
    for c in range(3):
        total = None
        for r in range(NC):
            for j in range(beads):
                rows = pl.ds(c * tiles * beads + j, tiles, stride=beads)
                term = share(GATHER, r, table[r, j], table[-r % NC, j]) * blocks[r][rows, :]
                total = term if total is None else total + term
        out[pl.ds(c, tiles, stride=4), :] = total
    out[pl.ds(3, tiles, stride=4), :] = species[...]
    bottom, top = out[0:4, :], out[4 * tiles - 4 :, :]
    even = at_even("space")
    to_inner[...] = jnp.where(even, top, bottom)
    to_outer[...] = jnp.where(even, bottom, top)


def contract(table, beads, blocks, species):
    return pl.pallas_call(
        functools.partial(contract_kernel, table, beads),
        out_shape=[
            pltpu.VMEM((4 * species.shape[0], LANES), jnp.float32),
            pltpu.VMEM((4, LANES), jnp.float32),
            pltpu.VMEM((4, LANES), jnp.float32),
        ],
        in_specs=[VMEM] * (NC + 1),
        out_specs=[VMEM] * 3,
        compiler_params=PARAMS,
        cost_estimate=cost(0.2),
        name="contract",
    )(blocks[0], *(blocks[r] for r in GATHER[1]), species)


def masses_of(species):
    return per_species(species, MASS_TABLE)


def spring_kernel(beads, own, before, after, momenta, species, out):
    tiles = species.shape[0]
    pull = TIME_STEP * SPRING_RATE * masses_of(species[...])

    def row(ref, c, j):
        return ref[pl.ds(c * tiles * beads + j, tiles, stride=beads), :]

    def side(c, j, ref, other):
        if GATHER[0] == "turn":
            return row(ref, c, j)
        return jnp.where(at_even("bead"), row(other, c, j), row(ref, c, j))

    for c in range(3):
        for j in range(beads):
            below = row(own, c, j - 1) if j else side(c, beads - 1, before, after)
            above = row(own, c, j + 1) if j + 1 < beads else side(c, 0, after, before)
            laplace = 2.0 * row(own, c, j) - below - above
            out[pl.ds(c * tiles * beads + j, tiles, stride=beads), :] = (
                row(momenta, c, j) - pull * laplace
            )


def spring_kick(beads, own, before, after, momenta, species):
    return pl.pallas_call(
        functools.partial(spring_kernel, beads),
        out_shape=pltpu.VMEM(own.shape, jnp.float32),
        in_specs=[VMEM] * 5,
        out_specs=VMEM,
        compiler_params=PARAMS,
        cost_estimate=cost(0.8),
        name="spring_kick",
    )(own, before, after, momenta, species)


def expand_kernel(table, beads, *refs):
    forces, kicked, species = arranged(SPREAD, refs), refs[NC], refs[NC + 1]
    momenta, displacement = refs[NC + 2 :]
    tiles = species.shape[0]
    scale = TIME_STEP * beads * NC / NC
    drift = per_species(species[...], [TIME_STEP / m for m in MASS_TABLE])
    for c in range(3):
        pulls = [force[pl.ds(c, tiles, stride=4), :] for force in forces]
        for j in range(beads):
            rows = pl.ds(c * tiles * beads + j, tiles, stride=beads)
            total = kicked[rows, :]
            for r in range(NC):
                weight = share(SPREAD, r, scale * table[-r % NC, j], scale * table[r, j])
                total = total + weight * pulls[r]
            momenta[rows, :] = total
            displacement[rows, :] = drift * total


def expand(table, beads, forces, kicked, species):
    shape = jax.ShapeDtypeStruct(kicked.shape, jnp.float32)
    return pl.pallas_call(
        functools.partial(expand_kernel, table, beads),
        out_shape=[shape, shape],
        in_specs=[VMEM] * (NC + 2),
        out_specs=[VMEM] * 2,
        compiler_params=PARAMS,
        cost_estimate=cost(0.8),
        name="expand",
    )(forces[0], *(forces[r] for r in SPREAD[1]), kicked, species)


def swap_with_adjacent(send_inner, send_outer):
    count = lax.axis_size("space")
    inner = [(i, i ^ 1) for i in range(count)]
    outer = [(i, (i + 1) % count if i % 2 else (i - 1) % count) for i in range(count)]
    return (
        lax.ppermute(send_inner, "space", inner),
        lax.ppermute(send_outer, "space", outer),
    )


def arranged(plan, refs):
    return [refs[0]] + [refs[1 + plan[1].index(r)] for r in range(1, NC)]


def share(plan, distance, behind, ahead):
    behind, ahead = float(behind), float(ahead)
    if plan[0] == "turn" or behind == ahead or distance == 0:
        return behind
    return jnp.where(at_even("bead"), ahead, behind)


def around(plan, block):
    count = lax.axis_size("bead")
    blocks = [block]
    for r in range(1, count):
        if plan[0] == "turn":
            pairs = [(i, (i + r) % count) for i in range(count)]
        else:
            pairs = [(i, i ^ r) for i in range(count)]
        blocks.append(lax.ppermute(block, "bead", pairs))
    return blocks


def on_device(
    positions,
    momenta,
    species,
    neighbour_index,
    neighbour_count,
    radial_rates,
    weight_input,
    embedding,
    weight_middle,
    weight_deeper,
    weight_output,
):
    bead_dev = positions.shape[0]
    atom_dev = positions.shape[2]
    bead_groups = lax.axis_size("bead")
    bead_count = bead_dev * bead_groups
    table = contraction_table(bead_count, NC)
    place = lax.axis_index("bead")
    direct = bead_groups == NC
    block_size = atom_dev * NC // bead_groups
    tiles = atom_dev // LANES

    if direct:
        block_start = 0
        slots, counts = neighbour_index, neighbour_count
    else:
        block_start = (place // NC) * block_size
        slots = lax.dynamic_slice_in_dim(neighbour_index, block_start, block_size, 1)
        counts = lax.dynamic_slice_in_dim(neighbour_count, block_start, block_size, 0)
    code, kinds, pairs, rates, wout = prepare(
        atom_dev,
        lambda: 0 if direct else (lax.axis_index("bead") // NC) * block_size,
        slots,
        counts,
        species.reshape(tiles, LANES),
        weight_input,
        embedding,
        weight_middle,
        weight_deeper,
        radial_rates,
        weight_output,
    )

    if direct:
        blocks = around(GATHER, bead_rows(positions))
        own, to_inner, to_outer = contract(table, bead_dev, blocks, kinds)
    else:
        replica = place % NC
        everything = lax.all_gather(positions, "bead", axis=0, tiled=True)
        weights = lax.dynamic_index_in_dim(jnp.asarray(table), replica, 0, keepdims=False)
        contracted = jnp.sum(weights[:, None, None] * everything, axis=0)
        stacked = contracted.reshape(3, tiles, LANES).transpose(1, 0, 2)
        own = jnp.concatenate([stacked, kinds[:, None]], axis=1).reshape(-1, LANES)

    if direct:
        got = swap_with_adjacent(to_inner, to_outer)
        inner_count = max(tiles - 2, 0)
        left_inner, others = None, []
        if inner_count:
            off, kind, rad, left_inner = inner_stage(own, code, rates, inner_count)
        force, to_inner, to_outer, *grad_inner = outer_stage(
            [own, *got[::-1]], code, pairs, rates, wout, left_inner
        )
        got = swap_with_adjacent(to_inner, to_outer)
        if inner_count:
            others = [inner_forces(code, rates, off, kind, rad, *grad_inner)]
        forces = around(SPREAD, combine(force, others, *got))
        kicked = spring_kick(
            bead_dev, blocks[0], blocks[1], blocks[NC - 1], bead_rows(momenta), kinds
        )
        moved = expand(table, bead_dev, forces, kicked, kinds)
        return tuple(from_bead_rows(rows, positions.shape) for rows in moved)

    even = at_even("space")
    bottom, top = own[:4], own[4 * tiles - 4 :]
    got_inner, got_outer = swap_with_adjacent(
        jnp.where(even, top, bottom), jnp.where(even, bottom, top)
    )
    window = jnp.concatenate(
        [
            jnp.where(even, got_outer, got_inner),
            own,
            jnp.where(even, got_inner, got_outer),
        ],
        axis=0,
    )
    first = block_start // LANES * 4
    groups = block_size // LANES
    window = lax.dynamic_slice_in_dim(window, first, 4 * (groups + 2), 0)
    left_inner = None
    if groups > 2:
        inside = window[4 : 4 * groups + 4]
        off, kind, rad, left_inner = inner_stage(inside, code, rates, groups - 2)
    force, *grad_inner = outer_stage([window], code, pairs, rates, wout, left_inner)
    if groups > 2:
        force = force.at[4 : 4 * groups + 4].add(
            inner_forces(code, rates, off, kind, rad, *grad_inner)
        )
    partial = jnp.zeros((4 * (tiles + 2), LANES), jnp.float32)
    partial = lax.dynamic_update_slice_in_dim(partial, force, first, 0)
    chosen = (jnp.arange(NC, dtype=jnp.int32) == replica).astype(jnp.float32)
    force = lax.psum(chosen[:, None, None] * partial[None], "bead")

    lower, middle, upper = force[:, :4], force[:, 4:-4], force[:, -4:]
    got_inner, got_outer = swap_with_adjacent(
        jnp.where(even, upper, lower), jnp.where(even, lower, upper)
    )
    middle = jnp.concatenate(
        [
            middle[:, :4] + jnp.where(even, got_outer, got_inner),
            middle[:, 4:-4],
            middle[:, -4:] + jnp.where(even, got_inner, got_outer),
        ],
        axis=1,
    )

    first = place * bead_dev
    below = lax.dynamic_index_in_dim(everything, (first - 1) % bead_count, 0)
    above = lax.dynamic_index_in_dim(everything, (first + bead_dev) % bead_count, 0)
    whole = middle.reshape(NC, tiles, 4, LANES).transpose(0, 2, 1, 3)[:, :3]
    whole = whole.reshape(NC, 3, atom_dev)
    columns = lax.dynamic_slice_in_dim(jnp.asarray(table), first, bead_dev, 1)
    expanded = jnp.sum(columns[:, :, None, None] * whole[:, None], axis=0)
    expanded = bead_count / NC * expanded
    masses = masses_of(species)
    cycle = jnp.concatenate([below, positions, above], axis=0)
    laplace = 2.0 * positions - cycle[:-2] - cycle[2:]
    spring = -SPRING_RATE * masses * laplace
    momenta_next = momenta + TIME_STEP * (spring + expanded)
    return (momenta_next, TIME_STEP * momenta_next / masses)


def solution(mesh):
    return jax.shard_map(
        on_device,
        mesh=mesh,
        in_specs=(
            P(("grp", "bead"), None, "space"),
            P(("grp", "bead"), None, "space"),
            P(("grp", "space")),
            P(None, ("grp", "space")),
            P(("grp", "space")),
            P(),
            P(),
            P(),
            P(),
            P(),
            P(),
        ),
        out_specs=(P(("grp", "bead"), None, "space"), P(("grp", "bead"), None, "space")),
        check_vma=False,
    )
```

```python
import functools

import jax
import jax.numpy as jnp
import numpy as np
from jax import lax
from jax.experimental import pallas as pl
from jax.experimental.pallas import tpu as pltpu
from jax.sharding import PartitionSpec as P

HALO = 128
NC = 4
SPECIES = 4
LANES = 128
DEAD = 4096
LOG2E = 1.4426950408889634

MASS_TABLE = (1.0, 0.25, 1.5, 2.0)
SPRING_RATE = 0.2
TIME_STEP = 0.5

GATHER = ("swap", (1, 3, 2))
SPREAD = ("turn", (3, 2, 1))


def contraction_table(bead_count, kept_modes):
    rows = np.arange(kept_modes)[:, None] / kept_modes
    cols = np.arange(bead_count)[None, :] / bead_count
    angles = 2.0 * np.pi * (rows - cols)
    summed = np.ones_like(angles)
    for order in range(1, kept_modes // 2):
        summed = summed + 2.0 * np.cos(order * angles)
    summed = summed + np.cos(kept_modes // 2 * angles)
    return (summed / bead_count).astype(np.float32)


def per_species(species, values):
    picked = jnp.full(species.shape, values[0], jnp.float32)
    for kind in range(1, SPECIES):
        picked = jnp.where(species == kind, values[kind], picked)
    return picked


VMEM = pl.BlockSpec(memory_space=pltpu.VMEM)
SMEM = pl.BlockSpec(memory_space=pltpu.SMEM)


PARAMS = pltpu.CompilerParams(vmem_limit_bytes=16 * 1024 * 1024)


def cost(micros):
    return pl.CostEstimate(
        flops=0, transcendentals=0, bytes_accessed=int(micros * 3_000_000)
    )


def at_even(axis):
    return jnp.bitwise_and(lax.axis_index(axis), 1) == 0


def split2(value):
    high = value.astype(jnp.bfloat16)
    low = (value - high.astype(jnp.float32)).astype(jnp.bfloat16)
    return high, low


def dot(lhs, rhs):
    return lax.dot_general(
        lhs, rhs, (((1,), (0,)), ((), ())), preferred_element_type=jnp.float32
    )


def dot_nt(lhs, rhs):
    return lax.dot_general(
        lhs, rhs, (((1,), (1,)), ((), ())), preferred_element_type=jnp.float32
    )


def prepare_kernel(slab_atoms, block_start, *refs):
    held, outs = refs[:9], refs[9:18]
    copied, sems = refs[18:27], refs[27]
    copies = [
        pltpu.make_async_copy(src, dst, sems.at[i])
        for i, (src, dst) in enumerate(zip(held, copied, strict=True))
    ]
    for copy in copies:
        copy.start()
    slots, counts, species, w1, emb, w2, w3, rates, wout = copied
    code, kinds, t1, t2, t3, l2, l3, rates_b, wout_b = outs
    for copy in copies[:3]:
        copy.wait()
    kinds[...] = species[...].astype(jnp.float32)

    slab = lax.axis_index("space")
    last = lax.axis_size("space") - 1
    lowest = jnp.where(slab == 0, HALO, 0)
    highest = jnp.where(slab == last, slab_atoms + HALO, slab_atoms + 2 * HALO)
    word = slots[...]
    slot_ids = lax.broadcasted_iota(jnp.int32, word.shape, 0)
    lane_ids = lax.broadcasted_iota(jnp.int32, word.shape, 1)
    live = (slot_ids < counts[...]) & (word >= lowest) & (word < highest)
    band = word - block_start() - jnp.bitwise_and(lane_ids, -LANES)
    code[...] = jnp.where(live, band, band + DEAD)

    for copy in copies[3:]:
        copy.wait()
    chan = w1.shape[1]
    t1[0:chan, :], t1[chan : 2 * chan, :] = split2(w1[...].T)
    e = emb[...]
    eh = e.astype(jnp.bfloat16).astype(jnp.float32)
    el = (e - eh).astype(jnp.bfloat16).astype(jnp.float32)
    rest = jnp.zeros((chan - 3 * SPECIES, e.shape[1]), jnp.float32)
    terms = jnp.concatenate([eh, el, e - eh - el, rest], axis=0)
    t1[2 * chan : 3 * chan, :] = terms.astype(jnp.bfloat16)
    for src, fwd, bwd in ((w2, t2, l2), (w3, t3, l3)):
        hid = src.shape[0]
        fwd[0:hid, :], fwd[hid : 2 * hid, :] = split2(src[...].T)
        bwd[0:hid, :], bwd[hid : 2 * hid, :] = split2(src[...])
    count = rates.shape[1]
    tall = jnp.concatenate(
        [rates[...], jnp.zeros((1, LANES - count), jnp.float32)], axis=1
    )
    rates_b[...] = jnp.broadcast_to(tall, (LANES, LANES)).T[0:count, :]
    wout_b[...] = jnp.broadcast_to(wout[...], wout_b.shape)


def prepare(slab_atoms, block_start, slots, counts, species, w1, emb, w2, w3, rates, wout):
    hid, chan = w1.shape
    shapes = [
        (3 * chan, hid),
        (2 * hid, hid),
        (2 * hid, hid),
        (2 * hid, hid),
        (2 * hid, hid),
    ]
    out_shape = [
        pltpu.VMEM(slots.shape, jnp.int32),
        pltpu.VMEM(species.shape, jnp.float32),
    ]
    out_shape += [pltpu.VMEM(s, jnp.bfloat16) for s in shapes]
    out_shape += [
        pltpu.VMEM((rates.shape[0], LANES), jnp.float32),
        pltpu.VMEM((8, hid), jnp.float32),
    ]
    operands = (
        slots,
        counts[None, :],
        species,
        w1,
        emb.T,
        w2,
        w3,
        rates[None, :],
        wout[None, :],
    )
    code, kinds, *pairs, rates_b, wout_b = pl.pallas_call(
        functools.partial(prepare_kernel, slab_atoms, block_start),
        out_shape=out_shape,
        in_specs=[pl.BlockSpec(memory_space=pltpu.HBM)] * len(operands),
        out_specs=[VMEM] * len(out_shape),
        scratch_shapes=[pltpu.VMEM(x.shape, x.dtype) for x in operands]
        + [pltpu.SemaphoreType.DMA((len(operands),))],
        cost_estimate=cost(1.2),
        name="prepare",
    )(*operands)
    return code, kinds, pairs, rates_b, wout_b


def neighbours(places, word, g, off, kind, dist):
    src = [
        [
            jnp.broadcast_to(
                places[4 * (g + q) + c : 4 * (g + q) + c + 1, :], (8, LANES)
            )
            for q in range(3)
        ]
        for c in range(4)
    ]
    for o in range(word.shape[0] // 8):
        rows = slice(8 * o, 8 * o + 8)
        lane = jnp.bitwise_and(word[rows, :], LANES - 1)
        part = jnp.bitwise_and(word[rows, :], DEAD - 1)
        is0 = part < LANES
        is1 = part < 2 * LANES
        got = []
        for c in range(4):
            x0, x1, x2 = (
                jnp.take_along_axis(src[c][q], lane, axis=1) for q in range(3)
            )
            got.append(jnp.where(is0, x0, jnp.where(is1, x1, x2)))
        total = None
        for c in range(3):
            diff = got[c] - src[c][1]
            off[c, rows, :] = diff
            total = diff * diff if total is None else total + diff * diff
        dist[rows, :] = total
        kind[rows, :] = jnp.where(word[rows, :] >= DEAD, -1.0, got[3])


def describe(kind, dist, rates, rad, desc):
    slots = kind.shape[0]
    rate_count = rates.shape[0]
    octets = rate_count // 8
    rate8 = [rates[8 * o : 8 * o + 8, :] * (-LOG2E) for o in range(octets)]
    acc = [[jnp.zeros((8, LANES), jnp.float32)] * octets for _ in range(SPECIES)]
    for n in range(slots):
        kind_n = jnp.broadcast_to(kind[n : n + 1, :], (8, LANES))
        dist_n = jnp.broadcast_to(dist[n : n + 1, :], (8, LANES))
        masks = [kind_n == float(s) for s in range(SPECIES)]
        for o in range(octets):
            radial = jnp.exp2(rate8[o] * dist_n)
            first = n * rate_count + 8 * o
            rad[first : first + 8, :] = radial
            for s in range(SPECIES):
                acc[s][o] = acc[s][o] + jnp.where(masks[s], radial, 0.0)
    for s in range(SPECIES):
        for o in range(octets):
            first = s * rate_count + 8 * o
            desc[first : first + 8, :] = acc[s][o]


def left_factor(desc, centre):
    chan = desc.shape[0]
    high, low = split2(desc[...].T)
    ids = lax.broadcasted_iota(jnp.int32, (chan, LANES), 0)
    ids = jnp.where(ids < 3 * SPECIES, jnp.bitwise_and(ids, SPECIES - 1), -1)
    onehot = jnp.where(ids.astype(jnp.float32) == centre, 1.0, 0.0)
    onehot = onehot.T.astype(jnp.bfloat16)
    return jnp.concatenate([high, high, low, onehot], axis=1)


def network(lefts, pairs, wout):
    t1, t2, t3, l2, l3 = pairs
    chan = t1.shape[0] // 3
    first = jnp.concatenate([t1[0 : 2 * chan, :], t1[0:chan, :], t1[2 * chan :, :]], axis=0)

    def act(x):
        sig = 0.5 + 0.5 * jnp.tanh(0.5 * x)
        value = x * sig
        return value, sig + value * (1.0 - sig)

    def layer(x, pair):
        high, low = split2(x)
        rows = pair.shape[0] // 2
        right = jnp.concatenate([pair[...], pair[0:rows, :]], axis=0)
        return dot(jnp.concatenate([high, high, low], axis=1), right)

    one = [act(dot(left, first)) for left in lefts]
    two = [act(layer(h, t2)) for h, _ in one]
    three = [act(layer(h, t3))[1] for h, _ in two]
    back = [wout[0:1, :] * s for s in three]
    back = [layer(g, l3) * s for g, (_, s) in zip(back, two)]
    back = [layer(g, l2) * s for g, (_, s) in zip(back, one)]
    last = jnp.concatenate(
        [t1[0:chan, :], t1[chan : 2 * chan, :], t1[0:chan, :]], axis=1
    )
    grads = []
    for g in back:
        high, low = split2(g)
        grads.append(dot_nt(last, jnp.concatenate([high, high, low], axis=1)))
    return grads


def slot_slopes(grad, kind, rates, rad, slope):
    slots = kind.shape[0]
    rate_count = rates.shape[0]
    octets = rate_count // 8
    grads = [
        [
            grad[s * rate_count + 8 * o : s * rate_count + 8 * o + 8, :]
            * rates[8 * o : 8 * o + 8, :]
            for o in range(octets)
        ]
        for s in range(SPECIES)
    ]
    for n in range(slots):
        kind_n = jnp.broadcast_to(kind[n : n + 1, :], (8, LANES))
        masks = [kind_n == float(s) for s in range(SPECIES - 1)]
        total = None
        for o in range(octets):
            picked = grads[SPECIES - 1][o]
            for s in range(SPECIES - 1):
                picked = jnp.where(masks[s], grads[s][o], picked)
            first = n * rate_count + 8 * o
            term = picked * rad[first : first + 8, :]
            total = term if total is None else total + term
        slope[n : n + 1, :] = jnp.sum(total, axis=0, keepdims=True)


def pair_forces(word, slope, off, pair, rel):
    sums = [jnp.zeros((8, LANES), jnp.float32)] * 3
    for o in range(word.shape[0] // 8):
        rows = slice(8 * o, 8 * o + 8)
        part = jnp.bitwise_and(word[rows, :], DEAD - 1)
        rel[0, rows, :] = jnp.bitwise_and(part, 63)
        rel[1, rows, :] = jnp.right_shift(part, 6)
        twice = jnp.where(word[rows, :] >= DEAD, 0.0, 2.0 * slope[rows, :])
        for c in range(3):
            force = twice * off[c, rows, :]
            sums[c] = sums[c] + force
            high = force.astype(jnp.bfloat16).astype(jnp.float32)
            pair[2 * c, rows, :] = high
            pair[2 * c + 1, rows, :] = force - high
    return [jnp.sum(x, axis=0, keepdims=True) for x in sums]


def scatter(pair, rel, slots, out, block0, centre):
    low_ids = lax.broadcasted_iota(jnp.int32, (64, LANES), 0)
    high_ids = lax.broadcasted_iota(jnp.int32, (8, LANES), 0)
    total = jnp.zeros((48, 64), jnp.float32)
    for n in range(0, slots, 2):
        lefts, rights = [], []
        for k in (n, n + 1):
            low = rel[0, k : k + 1, :]
            high = jnp.broadcast_to(rel[1, k : k + 1, :], (8, LANES))
            rights.append(jnp.where(low_ids == low, 1.0, 0.0).astype(jnp.bfloat16))
            hit = high_ids == high
            picked = [
                jnp.where(hit, jnp.broadcast_to(pair[c, k : k + 1, :], (8, LANES)), 0.0)
                for c in range(6)
            ]
            lefts.append(jnp.concatenate(picked, axis=0).astype(jnp.bfloat16))
        total = total + dot_nt(
            jnp.concatenate(lefts, axis=1), jnp.concatenate(rights, axis=1)
        )
    for c in range(3):
        merged = total[16 * c : 16 * c + 8, :] + total[16 * c + 8 : 16 * c + 16, :]
        for q in range(3):
            row = 4 * (block0 + q) + c
            both = jnp.concatenate(
                [merged[2 * q : 2 * q + 1, :], merged[2 * q + 1 : 2 * q + 2, :]], axis=1
            )
            if q == 1 and centre is not None:
                both = both - centre[c]
            out[row : row + 1, :] = out[row : row + 1, :] + both


def inner_kernel(own, code, rates, off, kind, rad, left, dist, desc):
    for i in range(kind.shape[0]):
        word = code[:, (i + 1) * LANES : (i + 2) * LANES]
        neighbours(own, word, i, off.at[i], kind.at[i], dist)
        describe(kind.at[i], dist, rates, rad.at[i], desc)
        row = 4 * (i + 1) + 3
        left[i] = left_factor(desc, own[row : row + 1, :])


def inner_stage(own, code, rates, count):
    slots = code.shape[0]
    rate_count = rates.shape[0]
    chan = SPECIES * rate_count
    out_shape = [
        pltpu.VMEM((count, 3, slots, LANES), jnp.float32),
        pltpu.VMEM((count, slots, LANES), jnp.float32),
        pltpu.VMEM((count, slots * rate_count, LANES), jnp.float32),
        pltpu.VMEM((count, LANES, 4 * chan), jnp.bfloat16),
    ]
    return pl.pallas_call(
        inner_kernel,
        out_shape=out_shape,
        in_specs=[VMEM] * 3,
        out_specs=[VMEM] * 4,
        scratch_shapes=[
            pltpu.VMEM((slots, LANES), jnp.float32),
            pltpu.VMEM((chan, LANES), jnp.float32),
        ],
        compiler_params=PARAMS,
        cost_estimate=cost(1.0),
        name="inner_descriptor",
    )(own, code, rates)


def outer_kernel(direct, inner, *refs):
    refs = list(refs)

    def take(count):
        taken = refs[:count]
        del refs[:count]
        return taken

    blocks = take(3 if direct else 1)
    code, *pairs, rates, wout = take(9 - 1)
    left_inner = take(1)[0] if inner else None
    out = take(1)[0]
    to_inner = take(1)[0] if direct else None
    grad_inner = take(1)[0] if inner else None
    places, off, kind, dist, rad, desc, grad, pair, rel, beyond, pulled = refs
    slots, block = code.shape
    groups = block // LANES
    stages = [
        (code[:, g * LANES : (g + 1) * LANES], places, g, out)
        for g in sorted({0, groups - 1})
    ]
    if direct:
        own, got_outer, got_inner = blocks
        even = at_even("space")
        first, last = own[0:4, :], own[4 * groups - 4 :, :]
        near, far = got_outer[0:4, :], got_outer[4:8, :]
        places[0:4, :] = jnp.where(even, far, got_inner[...])
        places[4 : 4 * groups + 4, :] = own[...]
        places[4 * groups + 4 :, :] = jnp.where(even, got_inner[...], near)
        beyond[0:4, :] = jnp.where(even, near, last)
        beyond[4:8, :] = jnp.where(even, far, near)
        beyond[8:12, :] = jnp.where(even, first, far)
        slab = lax.axis_index("space")
        at_end = (slab == 0) | (slab == lax.axis_size("space") - 1)
        word = got_outer[8:, :].astype(jnp.int32)
        word = jnp.where(at_end, jnp.bitwise_or(word, DEAD), word)
        stages.append((word, beyond, 0, pulled))
        pulled[...] = jnp.zeros_like(pulled)
    else:
        places[...] = blocks[0][...]
    lefts = []
    for i, (word, rows, g, _) in enumerate(stages):
        neighbours(rows, word, g, off.at[i], kind.at[i], dist)
        describe(kind.at[i], dist, rates, rad.at[i], desc.at[i])
        row = 4 * (g + 1) + 3
        lefts.append(left_factor(desc.at[i], rows[row : row + 1, :]))
    if inner:
        lefts += [left_inner[i] for i in range(left_inner.shape[0])]
    slopes = network(lefts, pairs, wout)
    for i in range(len(stages)):
        grad[i] = slopes[i]
    for i in range(len(stages), len(slopes)):
        grad_inner[i - len(stages)] = slopes[i]

    out[...] = jnp.zeros_like(out)
    for i, (word, rows, g, target) in enumerate(stages):
        slot_slopes(grad.at[i], kind.at[i], rates, rad.at[i], dist)
        centre = pair_forces(word, dist, off.at[i], pair, rel)
        scatter(pair, rel, slots, target, g, None if rows is beyond else centre)
    if direct:
        out[4:8, :] += jnp.where(even, pulled[8:12, :], 0.0)
        out[4 * groups : 4 * groups + 4, :] += jnp.where(even, 0.0, pulled[0:4, :])
        to_inner[...] = jnp.where(even, out[4 * groups + 4 :, :], out[0:4, :])


def outer_stage(blocks, code, pairs, rates, wout, left_inner):
    slots, block = code.shape
    rate_count = rates.shape[0]
    chan = SPECIES * rate_count
    groups = block // LANES
    count = len({0, groups - 1})
    inner = groups - count
    direct = len(blocks) > 1
    f32 = jnp.float32
    out_shape = [pltpu.VMEM((4 * (groups + 2), LANES), f32)]
    operands = [*blocks, code, *pairs, rates, wout]
    if direct:
        out_shape.append(pltpu.VMEM((4, LANES), f32))
        count += 1
    if inner:
        out_shape.append(pltpu.VMEM((inner, chan, LANES), f32))
        operands.append(left_inner)
    return pl.pallas_call(
        functools.partial(outer_kernel, direct, inner),
        out_shape=out_shape,
        in_specs=[VMEM] * len(operands),
        out_specs=[VMEM] * len(out_shape),
        scratch_shapes=[
            pltpu.VMEM((4 * (groups + 2), LANES), f32),
            pltpu.VMEM((count, 3, slots, LANES), f32),
            pltpu.VMEM((count, slots, LANES), f32),
            pltpu.VMEM((slots, LANES), f32),
            pltpu.VMEM((count, slots * rate_count, LANES), f32),
            pltpu.VMEM((count, chan, LANES), f32),
            pltpu.VMEM((count, chan, LANES), f32),
            pltpu.VMEM((6, slots, LANES), f32),
            pltpu.VMEM((2, slots, LANES), jnp.int32),
            pltpu.VMEM((12, LANES), f32),
            pltpu.VMEM((12, LANES), f32),
        ],
        compiler_params=PARAMS,
        cost_estimate=cost(3.0),
        name="outer_forces",
    )(*operands)


def inner_force_kernel(code, rates, off, kind, rad, grad, out, slope, pair, rel):
    slots = code.shape[0]
    out[...] = jnp.zeros_like(out)
    for i in range(kind.shape[0]):
        word = code[:, (i + 1) * LANES : (i + 2) * LANES]
        slot_slopes(grad.at[i], kind.at[i], rates, rad.at[i], slope)
        centre = pair_forces(word, slope, off.at[i], pair, rel)
        scatter(pair, rel, slots, out, i, centre)


def inner_forces(code, rates, off, kind, rad, grad):
    slots, block = code.shape
    return pl.pallas_call(
        inner_force_kernel,
        out_shape=pltpu.VMEM((block // LANES * 4, LANES), jnp.float32),
        in_specs=[VMEM] * 6,
        out_specs=VMEM,
        scratch_shapes=[
            pltpu.VMEM((slots, LANES), jnp.float32),
            pltpu.VMEM((6, slots, LANES), jnp.float32),
            pltpu.VMEM((2, slots, LANES), jnp.int32),
        ],
        compiler_params=PARAMS,
        cost_estimate=cost(1.2),
        name="inner_forces",
    )(code, rates, off, kind, rad, grad)


def combine_kernel(inner, force, *refs):
    *rest, got_inner, out = refs
    total = force[4 : force.shape[0] - 4, :]
    if inner:
        total = total + rest[0][...]
    even = at_even("space")
    out[...] = total
    out[0:4, :] += jnp.where(even, 0.0, got_inner[...])
    out[out.shape[0] - 4 :, :] += jnp.where(even, got_inner[...], 0.0)


def combine(force, inner, got_inner):
    operands = [force, *inner, got_inner]
    return pl.pallas_call(
        functools.partial(combine_kernel, len(inner)),
        out_shape=pltpu.VMEM((force.shape[0] - 8, LANES), jnp.float32),
        in_specs=[VMEM] * len(operands),
        out_specs=VMEM,
        compiler_params=PARAMS,
        cost_estimate=cost(0.1),
        name="combine",
    )(*operands)


def bead_rows(array):
    beads, comps, atoms = array.shape
    split = array.reshape(beads, comps, atoms // LANES, LANES)
    return split.transpose(1, 2, 0, 3).reshape(-1, LANES)


def from_bead_rows(rows, shape):
    beads, comps, atoms = shape
    split = rows.reshape(comps, atoms // LANES, beads, LANES)
    return split.transpose(2, 0, 1, 3).reshape(shape)


def contract_kernel(table, beads, *refs):
    blocks, species, code = arranged(GATHER, refs), refs[NC], refs[NC + 1]
    out, to_inner, to_outer = refs[NC + 2 :]
    tiles = species.shape[0]
    for c in range(3):
        total = None
        for r in range(NC):
            for j in range(beads):
                rows = pl.ds(c * tiles * beads + j, tiles, stride=beads)
                term = share(GATHER, r, table[r, j], table[-r % NC, j]) * blocks[r][rows, :]
                total = term if total is None else total + term
        out[pl.ds(c, tiles, stride=4), :] = total
    out[pl.ds(3, tiles, stride=4), :] = species[...]
    even = at_even("space")
    last = code.shape[1] - LANES
    to_inner[...] = jnp.where(even, out[4 * tiles - 4 :, :], out[0:4, :])
    to_outer[0:8, :] = jnp.where(even, out[0:8, :], out[4 * tiles - 8 :, :])
    to_outer[8:, :] = jnp.where(even, code[:, 0:LANES], code[:, last:]).astype(jnp.float32)


def contract(table, beads, blocks, species, code):
    return pl.pallas_call(
        functools.partial(contract_kernel, table, beads),
        out_shape=[
            pltpu.VMEM((4 * species.shape[0], LANES), jnp.float32),
            pltpu.VMEM((4, LANES), jnp.float32),
            pltpu.VMEM((8 + code.shape[0], LANES), jnp.float32),
        ],
        in_specs=[VMEM] * (NC + 2),
        out_specs=[VMEM] * 3,
        compiler_params=PARAMS,
        cost_estimate=cost(0.2),
        name="contract",
    )(blocks[0], *(blocks[r] for r in GATHER[1]), species, code)


def masses_of(species):
    return per_species(species, MASS_TABLE)


def spring_kernel(beads, own, before, after, momenta, species, out):
    tiles = species.shape[0]
    pull = TIME_STEP * SPRING_RATE * masses_of(species[...])

    def row(ref, c, j):
        return ref[pl.ds(c * tiles * beads + j, tiles, stride=beads), :]

    def side(c, j, ref, other):
        if GATHER[0] == "turn":
            return row(ref, c, j)
        return jnp.where(at_even("bead"), row(other, c, j), row(ref, c, j))

    for c in range(3):
        for j in range(beads):
            below = row(own, c, j - 1) if j else side(c, beads - 1, before, after)
            above = row(own, c, j + 1) if j + 1 < beads else side(c, 0, after, before)
            laplace = 2.0 * row(own, c, j) - below - above
            out[pl.ds(c * tiles * beads + j, tiles, stride=beads), :] = (
                row(momenta, c, j) - pull * laplace
            )


def spring_kick(beads, own, before, after, momenta, species):
    return pl.pallas_call(
        functools.partial(spring_kernel, beads),
        out_shape=pltpu.VMEM(own.shape, jnp.float32),
        in_specs=[VMEM] * 5,
        out_specs=VMEM,
        compiler_params=PARAMS,
        cost_estimate=cost(0.8),
        name="spring_kick",
    )(own, before, after, momenta, species)


def expand_kernel(table, beads, *refs):
    forces, kicked, species = arranged(SPREAD, refs), refs[NC], refs[NC + 1]
    momenta, displacement = refs[NC + 2 :]
    tiles = species.shape[0]
    scale = TIME_STEP * beads * NC / NC
    drift = per_species(species[...], [TIME_STEP / m for m in MASS_TABLE])
    for c in range(3):
        pulls = [force[pl.ds(c, tiles, stride=4), :] for force in forces]
        for j in range(beads):
            rows = pl.ds(c * tiles * beads + j, tiles, stride=beads)
            total = kicked[rows, :]
            for r in range(NC):
                weight = share(SPREAD, r, scale * table[-r % NC, j], scale * table[r, j])
                total = total + weight * pulls[r]
            momenta[rows, :] = total
            displacement[rows, :] = drift * total


def expand(table, beads, forces, kicked, species):
    shape = jax.ShapeDtypeStruct(kicked.shape, jnp.float32)
    return pl.pallas_call(
        functools.partial(expand_kernel, table, beads),
        out_shape=[shape, shape],
        in_specs=[VMEM] * (NC + 2),
        out_specs=[VMEM] * 2,
        compiler_params=PARAMS,
        cost_estimate=cost(0.8),
        name="expand",
    )(forces[0], *(forces[r] for r in SPREAD[1]), kicked, species)


def swap_inner(block):
    count = lax.axis_size("space")
    return lax.ppermute(block, "space", [(i, i ^ 1) for i in range(count)])


def swap_outer(block):
    count = lax.axis_size("space")
    pairs = [(i, (i + 1) % count if i % 2 else (i - 1) % count) for i in range(count)]
    return lax.ppermute(block, "space", pairs)


def arranged(plan, refs):
    return [refs[0]] + [refs[1 + plan[1].index(r)] for r in range(1, NC)]


def share(plan, distance, behind, ahead):
    behind, ahead = float(behind), float(ahead)
    if plan[0] == "turn" or behind == ahead or distance == 0:
        return behind
    return jnp.where(at_even("bead"), ahead, behind)


def around(plan, block):
    count = lax.axis_size("bead")
    blocks = [block]
    for r in range(1, count):
        if plan[0] == "turn":
            pairs = [(i, (i + r) % count) for i in range(count)]
        else:
            pairs = [(i, i ^ r) for i in range(count)]
        blocks.append(lax.ppermute(block, "bead", pairs))
    return blocks


def on_device(
    positions,
    momenta,
    species,
    neighbour_index,
    neighbour_count,
    radial_rates,
    weight_input,
    embedding,
    weight_middle,
    weight_deeper,
    weight_output,
):
    bead_dev = positions.shape[0]
    atom_dev = positions.shape[2]
    bead_groups = lax.axis_size("bead")
    bead_count = bead_dev * bead_groups
    table = contraction_table(bead_count, NC)
    place = lax.axis_index("bead")
    tiles = atom_dev // LANES
    direct = bead_groups == NC and tiles > 1
    block_size = atom_dev * NC // bead_groups

    if direct:
        block_start = 0
        slots, counts = neighbour_index, neighbour_count
    else:
        block_start = (place // NC) * block_size
        slots = lax.dynamic_slice_in_dim(neighbour_index, block_start, block_size, 1)
        counts = lax.dynamic_slice_in_dim(neighbour_count, block_start, block_size, 0)
    code, kinds, pairs, rates, wout = prepare(
        atom_dev,
        lambda: 0 if direct else (lax.axis_index("bead") // NC) * block_size,
        slots,
        counts,
        species.reshape(tiles, LANES),
        weight_input,
        embedding,
        weight_middle,
        weight_deeper,
        radial_rates,
        weight_output,
    )

    if direct:
        blocks = around(GATHER, bead_rows(positions))
        own, to_inner, to_outer = contract(table, bead_dev, blocks, kinds, code)
    else:
        replica = place % NC
        everything = lax.all_gather(positions, "bead", axis=0, tiled=True)
        weights = lax.dynamic_index_in_dim(jnp.asarray(table), replica, 0, keepdims=False)
        contracted = jnp.sum(weights[:, None, None] * everything, axis=0)
        stacked = contracted.reshape(3, tiles, LANES).transpose(1, 0, 2)
        own = jnp.concatenate([stacked, kinds[:, None]], axis=1).reshape(-1, LANES)

    if direct:
        got_outer, got_inner = swap_outer(to_outer), swap_inner(to_inner)
        inner_count = max(tiles - 2, 0)
        left_inner, others = None, []
        if inner_count:
            off, kind, rad, left_inner = inner_stage(own, code, rates, inner_count)
        force, to_inner, *grad_inner = outer_stage(
            [own, got_outer, got_inner], code, pairs, rates, wout, left_inner
        )
        got_inner = swap_inner(to_inner)
        if inner_count:
            others = [inner_forces(code, rates, off, kind, rad, *grad_inner)]
        forces = around(SPREAD, combine(force, others, got_inner))
        kicked = spring_kick(
            bead_dev, blocks[0], blocks[1], blocks[NC - 1], bead_rows(momenta), kinds
        )
        moved = expand(table, bead_dev, forces, kicked, kinds)
        return tuple(from_bead_rows(rows, positions.shape) for rows in moved)

    even = at_even("space")
    bottom, top = own[:4], own[4 * tiles - 4 :]
    got_inner = swap_inner(jnp.where(even, top, bottom))
    got_outer = swap_outer(jnp.where(even, bottom, top))
    window = jnp.concatenate(
        [
            jnp.where(even, got_outer, got_inner),
            own,
            jnp.where(even, got_inner, got_outer),
        ],
        axis=0,
    )
    first = block_start // LANES * 4
    groups = block_size // LANES
    window = lax.dynamic_slice_in_dim(window, first, 4 * (groups + 2), 0)
    left_inner = None
    if groups > 2:
        inside = window[4 : 4 * groups + 4]
        off, kind, rad, left_inner = inner_stage(inside, code, rates, groups - 2)
    force, *grad_inner = outer_stage([window], code, pairs, rates, wout, left_inner)
    if groups > 2:
        force = force.at[4 : 4 * groups + 4].add(
            inner_forces(code, rates, off, kind, rad, *grad_inner)
        )
    partial = jnp.zeros((4 * (tiles + 2), LANES), jnp.float32)
    partial = lax.dynamic_update_slice_in_dim(partial, force, first, 0)
    chosen = (jnp.arange(NC, dtype=jnp.int32) == replica).astype(jnp.float32)
    force = lax.psum(chosen[:, None, None] * partial[None], "bead")

    lower, middle, upper = force[:, :4], force[:, 4:-4], force[:, -4:]
    got_inner = swap_inner(jnp.where(even, upper, lower))
    got_outer = swap_outer(jnp.where(even, lower, upper))
    middle = jnp.concatenate(
        [
            middle[:, :4] + jnp.where(even, got_outer, got_inner),
            middle[:, 4:-4],
            middle[:, -4:] + jnp.where(even, got_inner, got_outer),
        ],
        axis=1,
    )

    first = place * bead_dev
    below = lax.dynamic_index_in_dim(everything, (first - 1) % bead_count, 0)
    above = lax.dynamic_index_in_dim(everything, (first + bead_dev) % bead_count, 0)
    whole = middle.reshape(NC, tiles, 4, LANES).transpose(0, 2, 1, 3)[:, :3]
    whole = whole.reshape(NC, 3, atom_dev)
    columns = lax.dynamic_slice_in_dim(jnp.asarray(table), first, bead_dev, 1)
    expanded = jnp.sum(columns[:, :, None, None] * whole[:, None], axis=0)
    expanded = bead_count / NC * expanded
    masses = masses_of(species)
    cycle = jnp.concatenate([below, positions, above], axis=0)
    laplace = 2.0 * positions - cycle[:-2] - cycle[2:]
    spring = -SPRING_RATE * masses * laplace
    momenta_next = momenta + TIME_STEP * (spring + expanded)
    return (momenta_next, TIME_STEP * momenta_next / masses)


def solution(mesh):
    return jax.shard_map(
        on_device,
        mesh=mesh,
        in_specs=(
            P(("grp", "bead"), None, "space"),
            P(("grp", "bead"), None, "space"),
            P(("grp", "space")),
            P(None, ("grp", "space")),
            P(("grp", "space")),
            P(),
            P(),
            P(),
            P(),
            P(),
            P(),
        ),
        out_specs=(P(("grp", "bead"), None, "space"), P(("grp", "bead"), None, "space")),
        check_vma=False,
    )
```

```python
import functools

import jax
import jax.numpy as jnp
import numpy as np
from jax import lax
from jax.experimental import pallas as pl
from jax.experimental.pallas import tpu as pltpu
from jax.sharding import PartitionSpec as P

HALO = 128
NC = 4
SPECIES = 4
LANES = 128
DEAD = 4096
LOG2E = 1.4426950408889634

MASS_TABLE = (1.0, 0.25, 1.5, 2.0)
SPRING_RATE = 0.2
TIME_STEP = 0.5

GATHER = ("swap", (1, 3, 2))
SPREAD = ("turn", (3, 2, 1))


def contraction_table(bead_count, kept_modes):
    rows = np.arange(kept_modes)[:, None] / kept_modes
    cols = np.arange(bead_count)[None, :] / bead_count
    angles = 2.0 * np.pi * (rows - cols)
    summed = np.ones_like(angles)
    for order in range(1, kept_modes // 2):
        summed = summed + 2.0 * np.cos(order * angles)
    summed = summed + np.cos(kept_modes // 2 * angles)
    return (summed / bead_count).astype(np.float32)


def per_species(species, values):
    picked = jnp.full(species.shape, values[0], jnp.float32)
    for kind in range(1, SPECIES):
        picked = jnp.where(species == kind, values[kind], picked)
    return picked


VMEM = pl.BlockSpec(memory_space=pltpu.VMEM)
SMEM = pl.BlockSpec(memory_space=pltpu.SMEM)


PARAMS = pltpu.CompilerParams(vmem_limit_bytes=16 * 1024 * 1024)


def cost(micros):
    return pl.CostEstimate(
        flops=0, transcendentals=0, bytes_accessed=int(micros * 3_000_000)
    )


def at_even(axis):
    return jnp.bitwise_and(lax.axis_index(axis), 1) == 0


def split2(value):
    high = value.astype(jnp.bfloat16)
    low = (value - high.astype(jnp.float32)).astype(jnp.bfloat16)
    return high, low


def dot(lhs, rhs):
    return lax.dot_general(
        lhs, rhs, (((1,), (0,)), ((), ())), preferred_element_type=jnp.float32
    )


def dot_nt(lhs, rhs):
    return lax.dot_general(
        lhs, rhs, (((1,), (1,)), ((), ())), preferred_element_type=jnp.float32
    )


def prepare_kernel(slab_atoms, block_start, *refs):
    held, outs = refs[:9], refs[9:18]
    copied, sems = refs[18:27], refs[27]
    copies = [
        pltpu.make_async_copy(src, dst, sems.at[i])
        for i, (src, dst) in enumerate(zip(held, copied, strict=True))
    ]
    for copy in copies:
        copy.start()
    slots, counts, species, w1, emb, w2, w3, rates, wout = copied
    code, kinds, t1, t2, t3, l2, l3, rates_b, wout_b = outs
    for copy in copies[:3]:
        copy.wait()
    kinds[...] = species[...].astype(jnp.float32)

    slab = lax.axis_index("space")
    last = lax.axis_size("space") - 1
    lowest = jnp.where(slab == 0, HALO, 0)
    highest = jnp.where(slab == last, slab_atoms + HALO, slab_atoms + 2 * HALO)
    word = slots[...]
    slot_ids = lax.broadcasted_iota(jnp.int32, word.shape, 0)
    lane_ids = lax.broadcasted_iota(jnp.int32, word.shape, 1)
    live = (slot_ids < counts[...]) & (word >= lowest) & (word < highest)
    band = word - block_start() - jnp.bitwise_and(lane_ids, -LANES)
    code[...] = jnp.where(live, band, band + DEAD)

    for copy in copies[3:]:
        copy.wait()
    chan = w1.shape[1]
    t1[0:chan, :], t1[chan : 2 * chan, :] = split2(w1[...].T)
    e = emb[...]
    eh = e.astype(jnp.bfloat16).astype(jnp.float32)
    el = (e - eh).astype(jnp.bfloat16).astype(jnp.float32)
    rest = jnp.zeros((chan - 3 * SPECIES, e.shape[1]), jnp.float32)
    terms = jnp.concatenate([eh, el, e - eh - el, rest], axis=0)
    t1[2 * chan : 3 * chan, :] = terms.astype(jnp.bfloat16)
    for src, fwd, bwd in ((w2, t2, l2), (w3, t3, l3)):
        hid = src.shape[0]
        fwd[0:hid, :], fwd[hid : 2 * hid, :] = split2(src[...].T)
        bwd[0:hid, :], bwd[hid : 2 * hid, :] = split2(src[...])
    count = rates.shape[1]
    tall = jnp.concatenate(
        [rates[...], jnp.zeros((1, LANES - count), jnp.float32)], axis=1
    )
    rates_b[...] = jnp.broadcast_to(tall, (LANES, LANES)).T[0:count, :]
    wout_b[...] = jnp.broadcast_to(wout[...], wout_b.shape)


def prepare(slab_atoms, block_start, slots, counts, species, w1, emb, w2, w3, rates, wout):
    hid, chan = w1.shape
    shapes = [
        (3 * chan, hid),
        (2 * hid, hid),
        (2 * hid, hid),
        (2 * hid, hid),
        (2 * hid, hid),
    ]
    out_shape = [
        pltpu.VMEM(slots.shape, jnp.int32),
        pltpu.VMEM(species.shape, jnp.float32),
    ]
    out_shape += [pltpu.VMEM(s, jnp.bfloat16) for s in shapes]
    out_shape += [
        pltpu.VMEM((rates.shape[0], LANES), jnp.float32),
        pltpu.VMEM((8, hid), jnp.float32),
    ]
    operands = (
        slots,
        counts[None, :],
        species,
        w1,
        emb.T,
        w2,
        w3,
        rates[None, :],
        wout[None, :],
    )
    code, kinds, *pairs, rates_b, wout_b = pl.pallas_call(
        functools.partial(prepare_kernel, slab_atoms, block_start),
        out_shape=out_shape,
        in_specs=[pl.BlockSpec(memory_space=pltpu.HBM)] * len(operands),
        out_specs=[VMEM] * len(out_shape),
        scratch_shapes=[pltpu.VMEM(x.shape, x.dtype) for x in operands]
        + [pltpu.SemaphoreType.DMA((len(operands),))],
        cost_estimate=cost(1.2),
        name="prepare",
    )(*operands)
    return code, kinds, pairs, rates_b, wout_b


def neighbours(places, word, g, off, kind, dist):
    src = [
        [
            jnp.broadcast_to(
                places[4 * (g + q) + c : 4 * (g + q) + c + 1, :], (8, LANES)
            )
            for q in range(3)
        ]
        for c in range(4)
    ]
    for o in range(word.shape[0] // 8):
        rows = slice(8 * o, 8 * o + 8)
        lane = jnp.bitwise_and(word[rows, :], LANES - 1)
        part = jnp.bitwise_and(word[rows, :], DEAD - 1)
        is0 = part < LANES
        is1 = part < 2 * LANES
        got = []
        for c in range(4):
            x0, x1, x2 = (
                jnp.take_along_axis(src[c][q], lane, axis=1) for q in range(3)
            )
            got.append(jnp.where(is0, x0, jnp.where(is1, x1, x2)))
        total = None
        for c in range(3):
            diff = got[c] - src[c][1]
            off[c, rows, :] = diff
            total = diff * diff if total is None else total + diff * diff
        dist[rows, :] = total
        kind[rows, :] = jnp.where(word[rows, :] >= DEAD, -1.0, got[3])


def describe(kind, dist, rates, rad, desc):
    slots = kind.shape[0]
    rate_count = rates.shape[0]
    octets = rate_count // 8
    rate8 = [rates[8 * o : 8 * o + 8, :] * (-LOG2E) for o in range(octets)]
    acc = [[jnp.zeros((8, LANES), jnp.float32)] * octets for _ in range(SPECIES)]
    for n in range(slots):
        kind_n = jnp.broadcast_to(kind[n : n + 1, :], (8, LANES))
        dist_n = jnp.broadcast_to(dist[n : n + 1, :], (8, LANES))
        masks = [kind_n == float(s) for s in range(SPECIES)]
        for o in range(octets):
            radial = jnp.exp2(rate8[o] * dist_n)
            first = n * rate_count + 8 * o
            rad[first : first + 8, :] = radial
            for s in range(SPECIES):
                acc[s][o] = acc[s][o] + jnp.where(masks[s], radial, 0.0)
    for s in range(SPECIES):
        for o in range(octets):
            first = s * rate_count + 8 * o
            desc[first : first + 8, :] = acc[s][o]


def left_factor(desc, centre):
    chan = desc.shape[0]
    high, low = split2(desc[...].T)
    ids = lax.broadcasted_iota(jnp.int32, (chan, LANES), 0)
    ids = jnp.where(ids < 3 * SPECIES, jnp.bitwise_and(ids, SPECIES - 1), -1)
    onehot = jnp.where(ids.astype(jnp.float32) == centre, 1.0, 0.0)
    onehot = onehot.T.astype(jnp.bfloat16)
    return jnp.concatenate([high, high, low, onehot], axis=1)


def dense(x, pair):
    high, low = split2(x)
    rows = pair.shape[0] // 2
    right = jnp.concatenate([pair[...], pair[0:rows, :]], axis=0)
    return dot(jnp.concatenate([high, high, low], axis=1), right)


def forward(lefts, pairs, wout):
    t1, t2, t3 = pairs
    chan = t1.shape[0] // 3
    first = jnp.concatenate([t1[0 : 2 * chan, :], t1[0:chan, :], t1[2 * chan :, :]], axis=0)

    def act(x):
        sig = 0.5 + 0.5 * jnp.tanh(0.5 * x)
        value = x * sig
        return value, sig + value * (1.0 - sig)

    one = [act(dot(left, first)) for left in lefts]
    two = [act(dense(h, t2)) for h, _ in one]
    three = [wout[0:1, :] * act(dense(h, t3))[1] for h, _ in two]
    return [(s1, s2, g3) for (_, s1), (_, s2), g3 in zip(one, two, three, strict=True)]


def backward(states, pairs):
    t1, l2, l3 = pairs
    chan = t1.shape[0] // 3
    back = [dense(g3, l3) * s2 for _, s2, g3 in states]
    back = [dense(g, l2) * s1 for g, (s1, _, _) in zip(back, states, strict=True)]
    last = jnp.concatenate(
        [t1[0:chan, :], t1[chan : 2 * chan, :], t1[0:chan, :]], axis=1
    )
    grads = []
    for g in back:
        high, low = split2(g)
        grads.append(dot_nt(last, jnp.concatenate([high, high, low], axis=1)))
    return grads


def slot_slopes(grad, kind, rates, rad, slope):
    slots = kind.shape[0]
    rate_count = rates.shape[0]
    octets = rate_count // 8
    grads = [
        [
            grad[s * rate_count + 8 * o : s * rate_count + 8 * o + 8, :]
            * rates[8 * o : 8 * o + 8, :]
            for o in range(octets)
        ]
        for s in range(SPECIES)
    ]
    for n in range(slots):
        kind_n = jnp.broadcast_to(kind[n : n + 1, :], (8, LANES))
        masks = [kind_n == float(s) for s in range(SPECIES - 1)]
        total = None
        for o in range(octets):
            picked = grads[SPECIES - 1][o]
            for s in range(SPECIES - 1):
                picked = jnp.where(masks[s], grads[s][o], picked)
            first = n * rate_count + 8 * o
            term = picked * rad[first : first + 8, :]
            total = term if total is None else total + term
        slope[n : n + 1, :] = jnp.sum(total, axis=0, keepdims=True)


def pair_forces(word, slope, off, pair, rel):
    sums = [jnp.zeros((8, LANES), jnp.float32)] * 3
    for o in range(word.shape[0] // 8):
        rows = slice(8 * o, 8 * o + 8)
        part = jnp.bitwise_and(word[rows, :], DEAD - 1)
        rel[0, rows, :] = jnp.bitwise_and(part, 63).astype(jnp.float32)
        rel[1, rows, :] = jnp.right_shift(part, 6).astype(jnp.float32)
        twice = jnp.where(word[rows, :] >= DEAD, 0.0, 2.0 * slope[rows, :])
        for c in range(3):
            force = twice * off[c, rows, :]
            sums[c] = sums[c] + force
            high = force.astype(jnp.bfloat16).astype(jnp.float32)
            pair[2 * c, rows, :] = high
            pair[2 * c + 1, rows, :] = force - high
    return [jnp.sum(x, axis=0, keepdims=True) for x in sums]


def scatter(pair, rel, slots, out, block0, centre):
    half = jnp.bfloat16
    low_ids = lax.broadcasted_iota(jnp.int32, (64, LANES), 0).astype(half)
    high_ids = lax.broadcasted_iota(jnp.int32, (16, LANES), 0)
    high_ids = jnp.bitwise_and(high_ids, 7).astype(half)
    ones, zeros = jnp.ones((64, LANES), half), jnp.zeros((64, LANES), half)
    total = jnp.zeros((48, 64), jnp.float32)
    for n in range(0, slots, 2):
        lefts, rights = [], []
        for k in (n, n + 1):
            low = jnp.broadcast_to(rel[0, k : k + 1, :], (16, LANES)).astype(half)
            high = jnp.broadcast_to(rel[1, k : k + 1, :], (16, LANES)).astype(half)
            low = jnp.concatenate([low] * 4, axis=0)
            rights.append(jnp.where(low_ids == low, ones, zeros))
            hit = high_ids == high
            for c in range(3):
                terms = [
                    jnp.broadcast_to(pair[2 * c + i, k : k + 1, :], (8, LANES))
                    for i in range(2)
                ]
                terms = jnp.concatenate(terms, axis=0).astype(half)
                lefts.append(jnp.where(hit, terms, zeros[0:16]))
        lefts = [jnp.concatenate(lefts[0:3], axis=0), jnp.concatenate(lefts[3:6], axis=0)]
        total = total + dot_nt(
            jnp.concatenate(lefts, axis=1), jnp.concatenate(rights, axis=1)
        )
    for c in range(3):
        merged = total[16 * c : 16 * c + 8, :] + total[16 * c + 8 : 16 * c + 16, :]
        for q in range(3):
            row = 4 * (block0 + q) + c
            both = jnp.concatenate(
                [merged[2 * q : 2 * q + 1, :], merged[2 * q + 1 : 2 * q + 2, :]], axis=1
            )
            if q == 1 and centre is not None:
                both = both - centre[c]
            out[row : row + 1, :] = out[row : row + 1, :] + both


def inner_kernel(own, code, rates, t1, t2, t3, wout, off, kind, rad, state, dist, desc):
    lefts = []
    for i in range(kind.shape[0]):
        word = code[:, (i + 1) * LANES : (i + 2) * LANES]
        neighbours(own, word, i, off.at[i], kind.at[i], dist.at[i])
        describe(kind.at[i], dist.at[i], rates, rad.at[i], desc.at[i])
        row = 4 * (i + 1) + 3
        lefts.append(left_factor(desc.at[i], own[row : row + 1, :]))
    for i, values in enumerate(forward(lefts, (t1, t2, t3), wout)):
        for j, value in enumerate(values):
            state[i, j] = value


def inner_stage(own, code, rates, pairs, wout, count):
    slots = code.shape[0]
    rate_count = rates.shape[0]
    chan = SPECIES * rate_count
    out_shape = [
        pltpu.VMEM((count, 3, slots, LANES), jnp.float32),
        pltpu.VMEM((count, slots, LANES), jnp.float32),
        pltpu.VMEM((count, slots * rate_count, LANES), jnp.float32),
        pltpu.VMEM((count, 3, LANES, wout.shape[1]), jnp.float32),
    ]
    return pl.pallas_call(
        inner_kernel,
        out_shape=out_shape,
        in_specs=[VMEM] * 7,
        out_specs=[VMEM] * 4,
        scratch_shapes=[
            pltpu.VMEM((count, slots, LANES), jnp.float32),
            pltpu.VMEM((count, chan, LANES), jnp.float32),
        ],
        compiler_params=PARAMS,
        cost_estimate=cost(1.0),
        name="inner_forward",
    )(own, code, rates, *pairs[:3], wout)


def outer_kernel(direct, inner, *refs):
    refs = list(refs)

    def take(count):
        taken = refs[:count]
        del refs[:count]
        return taken

    blocks = take(3 if direct else 1)
    code, *pairs, rates, wout = take(9 - 1)
    state_inner = take(1)[0] if inner else None
    out = take(1)[0]
    to_inner = take(1)[0] if direct else None
    grad_inner = take(1)[0] if inner else None
    places, off, kind, dist, rad, desc, grad, pair, rel, beyond, pulled = refs
    slots, block = code.shape
    groups = block // LANES
    stages = [
        (code[:, g * LANES : (g + 1) * LANES], places, g, out)
        for g in sorted({0, groups - 1})
    ]
    if direct:
        own, got_outer, got_inner = blocks
        even = at_even("space")
        first, last = own[0:4, :], own[4 * groups - 4 :, :]
        near, far = got_outer[0:4, :], got_outer[4:8, :]
        places[0:4, :] = jnp.where(even, far, got_inner[...])
        places[4 : 4 * groups + 4, :] = own[...]
        places[4 * groups + 4 :, :] = jnp.where(even, got_inner[...], near)
        beyond[0:4, :] = jnp.where(even, near, last)
        beyond[4:8, :] = jnp.where(even, far, near)
        beyond[8:12, :] = jnp.where(even, first, far)
        slab = lax.axis_index("space")
        at_end = (slab == 0) | (slab == lax.axis_size("space") - 1)
        word = got_outer[8:, :].astype(jnp.int32)
        word = jnp.where(at_end, jnp.bitwise_or(word, DEAD), word)
        stages.append((word, beyond, 0, pulled))
        pulled[...] = jnp.zeros_like(pulled)
    else:
        places[...] = blocks[0][...]
    lefts = []
    for i, (word, rows, g, _) in enumerate(stages):
        neighbours(rows, word, g, off.at[i], kind.at[i], dist.at[i])
        describe(kind.at[i], dist.at[i], rates, rad.at[i], desc.at[i])
        row = 4 * (g + 1) + 3
        lefts.append(left_factor(desc.at[i], rows[row : row + 1, :]))
    t1, t2, t3, l2, l3 = pairs
    states = forward(lefts, (t1, t2, t3), wout)
    if inner:
        states += [[state_inner[i, j] for j in range(3)] for i in range(inner)]
    slopes = backward(states, (t1, l2, l3))
    for i in range(len(stages)):
        grad[i] = slopes[i]
    for i in range(len(stages), len(slopes)):
        grad_inner[i - len(stages)] = slopes[i]

    out[...] = jnp.zeros_like(out)
    for i, (word, rows, g, target) in enumerate(stages):
        slope = dist.at[i]
        slot_slopes(grad.at[i], kind.at[i], rates, rad.at[i], slope)
        centre = pair_forces(word, slope, off.at[i], pair.at[i], rel.at[i])
        centre = None if rows is beyond else centre
        scatter(pair.at[i], rel.at[i], slots, target, g, centre)
    if direct:
        out[4:8, :] += jnp.where(even, pulled[8:12, :], 0.0)
        out[4 * groups : 4 * groups + 4, :] += jnp.where(even, 0.0, pulled[0:4, :])
        to_inner[...] = jnp.where(even, out[4 * groups + 4 :, :], out[0:4, :])


def outer_stage(blocks, code, pairs, rates, wout, state_inner):
    slots, block = code.shape
    rate_count = rates.shape[0]
    chan = SPECIES * rate_count
    groups = block // LANES
    count = len({0, groups - 1})
    inner = groups - count
    direct = len(blocks) > 1
    f32 = jnp.float32
    out_shape = [pltpu.VMEM((4 * (groups + 2), LANES), f32)]
    operands = [*blocks, code, *pairs, rates, wout]
    if direct:
        out_shape.append(pltpu.VMEM((4, LANES), f32))
        count += 1
    if inner:
        out_shape.append(pltpu.VMEM((inner, chan, LANES), f32))
        operands.append(state_inner)
    return pl.pallas_call(
        functools.partial(outer_kernel, direct, inner),
        out_shape=out_shape,
        in_specs=[VMEM] * len(operands),
        out_specs=[VMEM] * len(out_shape),
        scratch_shapes=[
            pltpu.VMEM((4 * (groups + 2), LANES), f32),
            pltpu.VMEM((count, 3, slots, LANES), f32),
            pltpu.VMEM((count, slots, LANES), f32),
            pltpu.VMEM((count, slots, LANES), f32),
            pltpu.VMEM((count, slots * rate_count, LANES), f32),
            pltpu.VMEM((count, chan, LANES), f32),
            pltpu.VMEM((count, chan, LANES), f32),
            pltpu.VMEM((count, 6, slots, LANES), f32),
            pltpu.VMEM((count, 2, slots, LANES), jnp.float32),
            pltpu.VMEM((12, LANES), f32),
            pltpu.VMEM((12, LANES), f32),
        ],
        compiler_params=PARAMS,
        cost_estimate=cost(3.0),
        name="outer_forces",
    )(*operands)


def inner_force_kernel(code, rates, off, kind, rad, grad, out, slope, pair, rel):
    slots = code.shape[0]
    out[...] = jnp.zeros_like(out)
    for i in range(kind.shape[0]):
        word = code[:, (i + 1) * LANES : (i + 2) * LANES]
        slot_slopes(grad.at[i], kind.at[i], rates, rad.at[i], slope.at[i])
        centre = pair_forces(word, slope.at[i], off.at[i], pair.at[i], rel.at[i])
        scatter(pair.at[i], rel.at[i], slots, out, i, centre)


def inner_forces(code, rates, off, kind, rad, grad):
    slots, block = code.shape
    count = kind.shape[0]
    return pl.pallas_call(
        inner_force_kernel,
        out_shape=pltpu.VMEM((block // LANES * 4, LANES), jnp.float32),
        in_specs=[VMEM] * 6,
        out_specs=VMEM,
        scratch_shapes=[
            pltpu.VMEM((count, slots, LANES), jnp.float32),
            pltpu.VMEM((count, 6, slots, LANES), jnp.float32),
            pltpu.VMEM((count, 2, slots, LANES), jnp.float32),
        ],
        compiler_params=PARAMS,
        cost_estimate=cost(1.2),
        name="inner_forces",
    )(code, rates, off, kind, rad, grad)


def combine_kernel(inner, force, *refs):
    *rest, got_inner, out = refs
    total = force[4 : force.shape[0] - 4, :]
    if inner:
        total = total + rest[0][...]
    even = at_even("space")
    out[...] = total
    out[0:4, :] += jnp.where(even, 0.0, got_inner[...])
    out[out.shape[0] - 4 :, :] += jnp.where(even, got_inner[...], 0.0)


def combine(force, inner, got_inner):
    operands = [force, *inner, got_inner]
    return pl.pallas_call(
        functools.partial(combine_kernel, len(inner)),
        out_shape=pltpu.VMEM((force.shape[0] - 8, LANES), jnp.float32),
        in_specs=[VMEM] * len(operands),
        out_specs=VMEM,
        compiler_params=PARAMS,
        cost_estimate=cost(0.1),
        name="combine",
    )(*operands)


def bead_rows(array):
    beads, comps, atoms = array.shape
    split = array.reshape(beads, comps, atoms // LANES, LANES)
    return split.transpose(1, 2, 0, 3).reshape(-1, LANES)


def from_bead_rows(rows, shape):
    beads, comps, atoms = shape
    split = rows.reshape(comps, atoms // LANES, beads, LANES)
    return split.transpose(2, 0, 1, 3).reshape(shape)


def contract_kernel(table, beads, *refs):
    blocks, species, code = arranged(GATHER, refs), refs[NC], refs[NC + 1]
    out, to_inner, to_outer = refs[NC + 2 :]
    tiles = species.shape[0]
    for c in range(3):
        total = None
        for r in range(NC):
            for j in range(beads):
                rows = pl.ds(c * tiles * beads + j, tiles, stride=beads)
                term = share(GATHER, r, table[r, j], table[-r % NC, j]) * blocks[r][rows, :]
                total = term if total is None else total + term
        out[pl.ds(c, tiles, stride=4), :] = total
    out[pl.ds(3, tiles, stride=4), :] = species[...]
    even = at_even("space")
    last = code.shape[1] - LANES
    to_inner[...] = jnp.where(even, out[4 * tiles - 4 :, :], out[0:4, :])
    to_outer[0:8, :] = jnp.where(even, out[0:8, :], out[4 * tiles - 8 :, :])
    to_outer[8:, :] = jnp.where(even, code[:, 0:LANES], code[:, last:]).astype(jnp.float32)


def contract(table, beads, blocks, species, code):
    return pl.pallas_call(
        functools.partial(contract_kernel, table, beads),
        out_shape=[
            pltpu.VMEM((4 * species.shape[0], LANES), jnp.float32),
            pltpu.VMEM((4, LANES), jnp.float32),
            pltpu.VMEM((8 + code.shape[0], LANES), jnp.float32),
        ],
        in_specs=[VMEM] * (NC + 2),
        out_specs=[VMEM] * 3,
        compiler_params=PARAMS,
        cost_estimate=cost(0.2),
        name="contract",
    )(blocks[0], *(blocks[r] for r in GATHER[1]), species, code)


def masses_of(species):
    return per_species(species, MASS_TABLE)


def spring_kernel(beads, own, before, after, momenta, species, out):
    tiles = species.shape[0]
    pull = TIME_STEP * SPRING_RATE * masses_of(species[...])

    def row(ref, c, j):
        return ref[pl.ds(c * tiles * beads + j, tiles, stride=beads), :]

    def side(c, j, ref, other):
        if GATHER[0] == "turn":
            return row(ref, c, j)
        return jnp.where(at_even("bead"), row(other, c, j), row(ref, c, j))

    for c in range(3):
        for j in range(beads):
            below = row(own, c, j - 1) if j else side(c, beads - 1, before, after)
            above = row(own, c, j + 1) if j + 1 < beads else side(c, 0, after, before)
            laplace = 2.0 * row(own, c, j) - below - above
            out[pl.ds(c * tiles * beads + j, tiles, stride=beads), :] = (
                row(momenta, c, j) - pull * laplace
            )


def spring_kick(beads, own, before, after, momenta, species):
    return pl.pallas_call(
        functools.partial(spring_kernel, beads),
        out_shape=pltpu.VMEM(own.shape, jnp.float32),
        in_specs=[VMEM] * 5,
        out_specs=VMEM,
        compiler_params=PARAMS,
        cost_estimate=cost(0.8),
        name="spring_kick",
    )(own, before, after, momenta, species)


def expand_kernel(table, beads, *refs):
    forces, kicked, species = arranged(SPREAD, refs), refs[NC], refs[NC + 1]
    momenta, displacement = refs[NC + 2 :]
    tiles = species.shape[0]
    scale = TIME_STEP * beads * NC / NC
    drift = per_species(species[...], [TIME_STEP / m for m in MASS_TABLE])
    for c in range(3):
        pulls = [force[pl.ds(c, tiles, stride=4), :] for force in forces]
        for j in range(beads):
            rows = pl.ds(c * tiles * beads + j, tiles, stride=beads)
            total = kicked[rows, :]
            for r in range(NC):
                weight = share(SPREAD, r, scale * table[-r % NC, j], scale * table[r, j])
                total = total + weight * pulls[r]
            momenta[rows, :] = total
            displacement[rows, :] = drift * total


def expand(table, beads, forces, kicked, species):
    shape = jax.ShapeDtypeStruct(kicked.shape, jnp.float32)
    return pl.pallas_call(
        functools.partial(expand_kernel, table, beads),
        out_shape=[shape, shape],
        in_specs=[VMEM] * (NC + 2),
        out_specs=[VMEM] * 2,
        compiler_params=PARAMS,
        cost_estimate=cost(0.8),
        name="expand",
    )(forces[0], *(forces[r] for r in SPREAD[1]), kicked, species)


def swap_inner(block):
    count = lax.axis_size("space")
    return lax.ppermute(block, "space", [(i, i ^ 1) for i in range(count)])


def swap_outer(block):
    count = lax.axis_size("space")
    pairs = [(i, (i + 1) % count if i % 2 else (i - 1) % count) for i in range(count)]
    return lax.ppermute(block, "space", pairs)


def arranged(plan, refs):
    return [refs[0]] + [refs[1 + plan[1].index(r)] for r in range(1, NC)]


def share(plan, distance, behind, ahead):
    behind, ahead = float(behind), float(ahead)
    if plan[0] == "turn" or behind == ahead or distance == 0:
        return behind
    return jnp.where(at_even("bead"), ahead, behind)


def around(plan, block):
    count = lax.axis_size("bead")
    blocks = [block]
    for r in range(1, count):
        if plan[0] == "turn":
            pairs = [(i, (i + r) % count) for i in range(count)]
        else:
            pairs = [(i, i ^ r) for i in range(count)]
        blocks.append(lax.ppermute(block, "bead", pairs))
    return blocks


def on_device(
    positions,
    momenta,
    species,
    neighbour_index,
    neighbour_count,
    radial_rates,
    weight_input,
    embedding,
    weight_middle,
    weight_deeper,
    weight_output,
):
    bead_dev = positions.shape[0]
    atom_dev = positions.shape[2]
    bead_groups = lax.axis_size("bead")
    bead_count = bead_dev * bead_groups
    table = contraction_table(bead_count, NC)
    place = lax.axis_index("bead")
    tiles = atom_dev // LANES
    direct = bead_groups == NC and tiles > 1
    block_size = atom_dev * NC // bead_groups

    if direct:
        block_start = 0
        slots, counts = neighbour_index, neighbour_count
    else:
        block_start = (place // NC) * block_size
        slots = lax.dynamic_slice_in_dim(neighbour_index, block_start, block_size, 1)
        counts = lax.dynamic_slice_in_dim(neighbour_count, block_start, block_size, 0)
    code, kinds, pairs, rates, wout = prepare(
        atom_dev,
        lambda: 0 if direct else (lax.axis_index("bead") // NC) * block_size,
        slots,
        counts,
        species.reshape(tiles, LANES),
        weight_input,
        embedding,
        weight_middle,
        weight_deeper,
        radial_rates,
        weight_output,
    )

    if direct:
        blocks = around(GATHER, bead_rows(positions))
        own, to_inner, to_outer = contract(table, bead_dev, blocks, kinds, code)
    else:
        replica = place % NC
        everything = lax.all_gather(positions, "bead", axis=0, tiled=True)
        weights = lax.dynamic_index_in_dim(jnp.asarray(table), replica, 0, keepdims=False)
        contracted = jnp.sum(weights[:, None, None] * everything, axis=0)
        stacked = contracted.reshape(3, tiles, LANES).transpose(1, 0, 2)
        own = jnp.concatenate([stacked, kinds[:, None]], axis=1).reshape(-1, LANES)

    if direct:
        got_outer, got_inner = swap_outer(to_outer), swap_inner(to_inner)
        inner_count = max(tiles - 2, 0)
        state_inner, others = None, []
        if inner_count:
            off, kind, rad, state_inner = inner_stage(
                own, code, rates, pairs, wout, inner_count
            )
        force, to_inner, *grad_inner = outer_stage(
            [own, got_outer, got_inner], code, pairs, rates, wout, state_inner
        )
        got_inner = swap_inner(to_inner)
        if inner_count:
            others = [inner_forces(code, rates, off, kind, rad, *grad_inner)]
        forces = around(SPREAD, combine(force, others, got_inner))
        kicked = spring_kick(
            bead_dev, blocks[0], blocks[1], blocks[NC - 1], bead_rows(momenta), kinds
        )
        moved = expand(table, bead_dev, forces, kicked, kinds)
        return tuple(from_bead_rows(rows, positions.shape) for rows in moved)

    even = at_even("space")
    bottom, top = own[:4], own[4 * tiles - 4 :]
    got_inner = swap_inner(jnp.where(even, top, bottom))
    got_outer = swap_outer(jnp.where(even, bottom, top))
    window = jnp.concatenate(
        [
            jnp.where(even, got_outer, got_inner),
            own,
            jnp.where(even, got_inner, got_outer),
        ],
        axis=0,
    )
    first = block_start // LANES * 4
    groups = block_size // LANES
    window = lax.dynamic_slice_in_dim(window, first, 4 * (groups + 2), 0)
    state_inner = None
    if groups > 2:
        inside = window[4 : 4 * groups + 4]
        off, kind, rad, state_inner = inner_stage(
            inside, code, rates, pairs, wout, groups - 2
        )
    force, *grad_inner = outer_stage([window], code, pairs, rates, wout, state_inner)
    if groups > 2:
        force = force.at[4 : 4 * groups + 4].add(
            inner_forces(code, rates, off, kind, rad, *grad_inner)
        )
    partial = jnp.zeros((4 * (tiles + 2), LANES), jnp.float32)
    partial = lax.dynamic_update_slice_in_dim(partial, force, first, 0)
    chosen = (jnp.arange(NC, dtype=jnp.int32) == replica).astype(jnp.float32)
    force = lax.psum(chosen[:, None, None] * partial[None], "bead")

    lower, middle, upper = force[:, :4], force[:, 4:-4], force[:, -4:]
    got_inner = swap_inner(jnp.where(even, upper, lower))
    got_outer = swap_outer(jnp.where(even, lower, upper))
    middle = jnp.concatenate(
        [
            middle[:, :4] + jnp.where(even, got_outer, got_inner),
            middle[:, 4:-4],
            middle[:, -4:] + jnp.where(even, got_inner, got_outer),
        ],
        axis=1,
    )

    first = place * bead_dev
    below = lax.dynamic_index_in_dim(everything, (first - 1) % bead_count, 0)
    above = lax.dynamic_index_in_dim(everything, (first + bead_dev) % bead_count, 0)
    whole = middle.reshape(NC, tiles, 4, LANES).transpose(0, 2, 1, 3)[:, :3]
    whole = whole.reshape(NC, 3, atom_dev)
    columns = lax.dynamic_slice_in_dim(jnp.asarray(table), first, bead_dev, 1)
    expanded = jnp.sum(columns[:, :, None, None] * whole[:, None], axis=0)
    expanded = bead_count / NC * expanded
    masses = masses_of(species)
    cycle = jnp.concatenate([below, positions, above], axis=0)
    laplace = 2.0 * positions - cycle[:-2] - cycle[2:]
    spring = -SPRING_RATE * masses * laplace
    momenta_next = momenta + TIME_STEP * (spring + expanded)
    return (momenta_next, TIME_STEP * momenta_next / masses)


def solution(mesh):
    return jax.shard_map(
        on_device,
        mesh=mesh,
        in_specs=(
            P(("grp", "bead"), None, "space"),
            P(("grp", "bead"), None, "space"),
            P(("grp", "space")),
            P(None, ("grp", "space")),
            P(("grp", "space")),
            P(),
            P(),
            P(),
            P(),
            P(),
            P(),
        ),
        out_specs=(P(("grp", "bead"), None, "space"), P(("grp", "bead"), None, "space")),
        check_vma=False,
    )
```

```python
import functools

import jax
import jax.numpy as jnp
import numpy as np
from jax import lax
from jax.experimental import pallas as pl
from jax.experimental.pallas import tpu as pltpu
from jax.sharding import PartitionSpec as P

HALO = 128
NC = 4
SPECIES = 4
LANES = 128
DEAD = 4096
LOG2E = 1.4426950408889634

MASS_TABLE = (1.0, 0.25, 1.5, 2.0)
SPRING_RATE = 0.2
TIME_STEP = 0.5

GATHER = ("swap", (1, 3, 2))
SPREAD = ("turn", (3, 2, 1))


def contraction_table(bead_count, kept_modes):
    rows = np.arange(kept_modes)[:, None] / kept_modes
    cols = np.arange(bead_count)[None, :] / bead_count
    angles = 2.0 * np.pi * (rows - cols)
    summed = np.ones_like(angles)
    for order in range(1, kept_modes // 2):
        summed = summed + 2.0 * np.cos(order * angles)
    summed = summed + np.cos(kept_modes // 2 * angles)
    return (summed / bead_count).astype(np.float32)


def per_species(species, values):
    picked = jnp.full(species.shape, values[0], jnp.float32)
    for kind in range(1, SPECIES):
        picked = jnp.where(species == kind, values[kind], picked)
    return picked


VMEM = pl.BlockSpec(memory_space=pltpu.VMEM)
SMEM = pl.BlockSpec(memory_space=pltpu.SMEM)


PARAMS = pltpu.CompilerParams(vmem_limit_bytes=16 * 1024 * 1024)


def cost(micros):
    return pl.CostEstimate(
        flops=0, transcendentals=0, bytes_accessed=int(micros * 3_000_000)
    )


def at_even(axis):
    return jnp.bitwise_and(lax.axis_index(axis), 1) == 0


def split2(value):
    high = value.astype(jnp.bfloat16)
    low = (value - high.astype(jnp.float32)).astype(jnp.bfloat16)
    return high, low


def dot(lhs, rhs):
    return lax.dot_general(
        lhs, rhs, (((1,), (0,)), ((), ())), preferred_element_type=jnp.float32
    )


def dot_nt(lhs, rhs):
    return lax.dot_general(
        lhs, rhs, (((1,), (1,)), ((), ())), preferred_element_type=jnp.float32
    )


def prepare_kernel(slab_atoms, block_start, *refs):
    held, outs = refs[:9], refs[9:18]
    copied, sems = refs[18:27], refs[27]
    copies = [
        pltpu.make_async_copy(src, dst, sems.at[i])
        for i, (src, dst) in enumerate(zip(held, copied, strict=True))
    ]
    for copy in copies:
        copy.start()
    slots, counts, species, w1, emb, w2, w3, rates, wout = copied
    code, kinds, t1, t2, t3, l2, l3, rates_b, wout_b = outs
    for copy in copies[:3]:
        copy.wait()
    kinds[...] = species[...].astype(jnp.float32)

    slab = lax.axis_index("space")
    last = lax.axis_size("space") - 1
    lowest = jnp.where(slab == 0, HALO, 0)
    highest = jnp.where(slab == last, slab_atoms + HALO, slab_atoms + 2 * HALO)
    word = slots[...]
    slot_ids = lax.broadcasted_iota(jnp.int32, word.shape, 0)
    lane_ids = lax.broadcasted_iota(jnp.int32, word.shape, 1)
    live = (slot_ids < counts[...]) & (word >= lowest) & (word < highest)
    band = word - block_start() - jnp.bitwise_and(lane_ids, -LANES)
    code[...] = jnp.where(live, band, band + DEAD)

    for copy in copies[3:]:
        copy.wait()
    chan = w1.shape[1]
    t1[0:chan, :], t1[chan : 2 * chan, :] = split2(w1[...].T)
    e = emb[...]
    eh = e.astype(jnp.bfloat16).astype(jnp.float32)
    el = (e - eh).astype(jnp.bfloat16).astype(jnp.float32)
    rest = jnp.zeros((chan - 3 * SPECIES, e.shape[1]), jnp.float32)
    terms = jnp.concatenate([eh, el, e - eh - el, rest], axis=0)
    t1[2 * chan : 3 * chan, :] = terms.astype(jnp.bfloat16)
    for src, fwd, bwd in ((w2, t2, l2), (w3, t3, l3)):
        hid = src.shape[0]
        fwd[0:hid, :], fwd[hid : 2 * hid, :] = split2(src[...].T)
        bwd[0:hid, :], bwd[hid : 2 * hid, :] = split2(src[...])
    count = rates.shape[1]
    tall = jnp.concatenate(
        [rates[...], jnp.zeros((1, LANES - count), jnp.float32)], axis=1
    )
    rates_b[...] = jnp.broadcast_to(tall, (LANES, LANES)).T[0:count, :]
    wout_b[...] = jnp.broadcast_to(wout[...], wout_b.shape)


def prepare(slab_atoms, block_start, slots, counts, species, w1, emb, w2, w3, rates, wout):
    hid, chan = w1.shape
    shapes = [
        (3 * chan, hid),
        (2 * hid, hid),
        (2 * hid, hid),
        (2 * hid, hid),
        (2 * hid, hid),
    ]
    out_shape = [
        pltpu.VMEM(slots.shape, jnp.int32),
        pltpu.VMEM(species.shape, jnp.float32),
    ]
    out_shape += [pltpu.VMEM(s, jnp.bfloat16) for s in shapes]
    out_shape += [
        pltpu.VMEM((rates.shape[0], LANES), jnp.float32),
        pltpu.VMEM((8, hid), jnp.float32),
    ]
    operands = (
        slots,
        counts[None, :],
        species,
        w1,
        emb.T,
        w2,
        w3,
        rates[None, :],
        wout[None, :],
    )
    code, kinds, *pairs, rates_b, wout_b = pl.pallas_call(
        functools.partial(prepare_kernel, slab_atoms, block_start),
        out_shape=out_shape,
        in_specs=[pl.BlockSpec(memory_space=pltpu.HBM)] * len(operands),
        out_specs=[VMEM] * len(out_shape),
        scratch_shapes=[pltpu.VMEM(x.shape, x.dtype) for x in operands]
        + [pltpu.SemaphoreType.DMA((len(operands),))],
        cost_estimate=cost(1.2),
        name="prepare",
    )(*operands)
    return code, kinds, pairs, rates_b, wout_b


def neighbours(places, word, g, off, kind, dist):
    src = [
        [
            jnp.broadcast_to(
                places[4 * (g + q) + c : 4 * (g + q) + c + 1, :], (8, LANES)
            )
            for q in range(3)
        ]
        for c in range(4)
    ]
    for o in range(word.shape[0] // 8):
        rows = slice(8 * o, 8 * o + 8)
        lane = jnp.bitwise_and(word[rows, :], LANES - 1)
        part = jnp.bitwise_and(word[rows, :], DEAD - 1)
        is0 = part < LANES
        is1 = part < 2 * LANES
        got = []
        for c in range(4):
            x0, x1, x2 = (
                jnp.take_along_axis(src[c][q], lane, axis=1) for q in range(3)
            )
            got.append(jnp.where(is0, x0, jnp.where(is1, x1, x2)))
        total = None
        for c in range(3):
            diff = got[c] - src[c][1]
            off[c, rows, :] = diff
            total = diff * diff if total is None else total + diff * diff
        dist[rows, :] = total
        kind[rows, :] = jnp.where(word[rows, :] >= DEAD, -1.0, got[3])


def describe(kind, dist, rates, rad, desc):
    slots = kind.shape[0]
    rate_count = rates.shape[0]
    octets = rate_count // 8
    rate8 = [rates[8 * o : 8 * o + 8, :] * (-LOG2E) for o in range(octets)]
    acc = [[jnp.zeros((8, LANES), jnp.float32)] * octets for _ in range(SPECIES)]
    for n in range(slots):
        kind_n = jnp.broadcast_to(kind[n : n + 1, :], (8, LANES))
        dist_n = jnp.broadcast_to(dist[n : n + 1, :], (8, LANES))
        masks = [kind_n == float(s) for s in range(SPECIES)]
        for o in range(octets):
            radial = jnp.exp2(rate8[o] * dist_n)
            first = n * rate_count + 8 * o
            rad[first : first + 8, :] = radial
            for s in range(SPECIES):
                acc[s][o] = acc[s][o] + jnp.where(masks[s], radial, 0.0)
    for s in range(SPECIES):
        for o in range(octets):
            first = s * rate_count + 8 * o
            desc[first : first + 8, :] = acc[s][o]


def left_factor(desc, centre):
    chan = desc.shape[0]
    high, low = split2(desc[...].T)
    ids = lax.broadcasted_iota(jnp.int32, (chan, LANES), 0)
    ids = jnp.where(ids < 3 * SPECIES, jnp.bitwise_and(ids, SPECIES - 1), -1)
    onehot = jnp.where(ids.astype(jnp.float32) == centre, 1.0, 0.0)
    onehot = onehot.T.astype(jnp.bfloat16)
    return jnp.concatenate([high, high, low, onehot], axis=1)


def dense(x, pair):
    high, low = split2(x)
    rows = pair.shape[0] // 2
    right = jnp.concatenate([pair[...], pair[0:rows, :]], axis=0)
    return dot(jnp.concatenate([high, high, low], axis=1), right)


def act(x):
    sig = 0.5 + 0.5 * jnp.tanh(0.5 * x)
    value = x * sig
    return value, sig + value * (1.0 - sig)


def forward_layers(pairs, wout):
    t1, t2, t3 = pairs
    chan = t1.shape[0] // 3
    first = jnp.concatenate([t1[0 : 2 * chan, :], t1[0:chan, :], t1[2 * chan :, :]], axis=0)

    def one(left):
        return act(dot(left, first))

    def two(state):
        value, s1 = state
        return act(dense(value, t2)), s1

    def three(state):
        (value, s2), s1 = state
        return s1, s2, wout[0:1, :] * act(dense(value, t3))[1]

    return one, two, three


def backward_layers(pairs):
    t1, l2, l3 = pairs
    chan = t1.shape[0] // 3

    def three(state):
        s1, s2, grad = state
        return s1, dense(grad, l3) * s2

    def two(state):
        s1, grad = state
        return dense(grad, l2) * s1

    def one(grad):
        high, low = split2(grad)
        last = [t1[0:chan, :], t1[chan : 2 * chan, :], t1[0:chan, :]]
        return dot_nt(
            jnp.concatenate(last, axis=1), jnp.concatenate([high, high, low], axis=1)
        )

    return three, two, one


def through(layers, states):
    for layer in layers:
        states = [layer(state) for state in states]
    return states


def slot_slopes(grad, kind, rates, rad, slope):
    slots = kind.shape[0]
    rate_count = rates.shape[0]
    octets = rate_count // 8
    grads = [
        [
            grad[s * rate_count + 8 * o : s * rate_count + 8 * o + 8, :]
            * rates[8 * o : 8 * o + 8, :]
            for o in range(octets)
        ]
        for s in range(SPECIES)
    ]
    for n in range(slots):
        kind_n = jnp.broadcast_to(kind[n : n + 1, :], (8, LANES))
        masks = [kind_n == float(s) for s in range(SPECIES - 1)]
        total = None
        for o in range(octets):
            picked = grads[SPECIES - 1][o]
            for s in range(SPECIES - 1):
                picked = jnp.where(masks[s], grads[s][o], picked)
            first = n * rate_count + 8 * o
            term = picked * rad[first : first + 8, :]
            total = term if total is None else total + term
        slope[n : n + 1, :] = jnp.sum(total, axis=0, keepdims=True)


def pair_forces(word, slope, off, pair, rel):
    sums = [jnp.zeros((8, LANES), jnp.float32)] * 3
    for o in range(word.shape[0] // 8):
        rows = slice(8 * o, 8 * o + 8)
        part = jnp.bitwise_and(word[rows, :], DEAD - 1)
        rel[0, rows, :] = jnp.bitwise_and(part, 63).astype(jnp.float32)
        rel[1, rows, :] = jnp.right_shift(part, 6).astype(jnp.float32)
        twice = jnp.where(word[rows, :] >= DEAD, 0.0, 2.0 * slope[rows, :])
        for c in range(3):
            force = twice * off[c, rows, :]
            sums[c] = sums[c] + force
            high = force.astype(jnp.bfloat16).astype(jnp.float32)
            pair[2 * c, rows, :] = high
            pair[2 * c + 1, rows, :] = force - high
    return [jnp.sum(x, axis=0, keepdims=True) for x in sums]


def scatter(pair, rel, slots, out, block0, centre):
    half = jnp.bfloat16
    low_ids = lax.broadcasted_iota(jnp.int32, (64, LANES), 0).astype(half)
    high_ids = lax.broadcasted_iota(jnp.int32, (16, LANES), 0)
    high_ids = jnp.bitwise_and(high_ids, 7).astype(half)
    ones, zeros = jnp.ones((64, LANES), half), jnp.zeros((64, LANES), half)
    total = jnp.zeros((48, 64), jnp.float32)
    for n in range(0, slots, 2):
        lefts, rights = [], []
        for k in (n, n + 1):
            low = jnp.broadcast_to(rel[0, k : k + 1, :], (16, LANES)).astype(half)
            high = jnp.broadcast_to(rel[1, k : k + 1, :], (16, LANES)).astype(half)
            low = jnp.concatenate([low] * 4, axis=0)
            rights.append(jnp.where(low_ids == low, ones, zeros))
            hit = high_ids == high
            for c in range(3):
                terms = [
                    jnp.broadcast_to(pair[2 * c + i, k : k + 1, :], (8, LANES))
                    for i in range(2)
                ]
                terms = jnp.concatenate(terms, axis=0).astype(half)
                lefts.append(jnp.where(hit, terms, zeros[0:16]))
        lefts = [jnp.concatenate(lefts[0:3], axis=0), jnp.concatenate(lefts[3:6], axis=0)]
        total = total + dot_nt(
            jnp.concatenate(lefts, axis=1), jnp.concatenate(rights, axis=1)
        )
    for c in range(3):
        merged = total[16 * c : 16 * c + 8, :] + total[16 * c + 8 : 16 * c + 16, :]
        for q in range(3):
            row = 4 * (block0 + q) + c
            both = jnp.concatenate(
                [merged[2 * q : 2 * q + 1, :], merged[2 * q + 1 : 2 * q + 2, :]], axis=1
            )
            if q == 1 and centre is not None:
                both = both - centre[c]
            out[row : row + 1, :] = out[row : row + 1, :] + both


def inner_kernel(own, code, rates, t1, t2, t3, wout, off, kind, rad, state, dist, desc):
    lefts = []
    for i in range(kind.shape[0]):
        word = code[:, (i + 1) * LANES : (i + 2) * LANES]
        neighbours(own, word, i, off.at[i], kind.at[i], dist.at[i])
        describe(kind.at[i], dist.at[i], rates, rad.at[i], desc.at[i])
        row = 4 * (i + 1) + 3
        lefts.append(left_factor(desc.at[i], own[row : row + 1, :]))
    states = through(forward_layers((t1, t2, t3), wout), lefts)
    for i, values in enumerate(states):
        for j, value in enumerate(values):
            state[i, j] = value


def inner_stage(own, code, rates, pairs, wout, count):
    slots = code.shape[0]
    rate_count = rates.shape[0]
    chan = SPECIES * rate_count
    out_shape = [
        pltpu.VMEM((count, 3, slots, LANES), jnp.float32),
        pltpu.VMEM((count, slots, LANES), jnp.float32),
        pltpu.VMEM((count, slots * rate_count, LANES), jnp.float32),
        pltpu.VMEM((count, 3, LANES, wout.shape[1]), jnp.float32),
    ]
    return pl.pallas_call(
        inner_kernel,
        out_shape=out_shape,
        in_specs=[VMEM] * 7,
        out_specs=[VMEM] * 4,
        scratch_shapes=[
            pltpu.VMEM((count, slots, LANES), jnp.float32),
            pltpu.VMEM((count, chan, LANES), jnp.float32),
        ],
        compiler_params=PARAMS,
        cost_estimate=cost(1.0),
        name="inner_forward",
    )(own, code, rates, *pairs[:3], wout)


def outer_kernel(direct, inner, *refs):
    refs = list(refs)

    def take(count):
        taken = refs[:count]
        del refs[:count]
        return taken

    blocks = take(3 if direct else 1)
    code, *pairs, rates, wout = take(9 - 1)
    state_inner = take(1)[0] if inner else None
    out = take(1)[0]
    to_inner = take(1)[0] if direct else None
    grad_inner = take(1)[0] if inner else None
    places, off, kind, dist, rad, desc, grad, pair, rel, beyond, pulled = refs
    slots, block = code.shape
    groups = block // LANES
    stages = [
        (code[:, g * LANES : (g + 1) * LANES], places, g, out)
        for g in sorted({0, groups - 1})
    ]
    if direct:
        own, got_outer, got_inner = blocks
        even = at_even("space")
        first, last = own[0:4, :], own[4 * groups - 4 :, :]
        near, far = got_outer[0:4, :], got_outer[4:8, :]
        places[0:4, :] = jnp.where(even, far, got_inner[...])
        places[4 : 4 * groups + 4, :] = own[...]
        places[4 * groups + 4 :, :] = jnp.where(even, got_inner[...], near)
        beyond[0:4, :] = jnp.where(even, near, last)
        beyond[4:8, :] = jnp.where(even, far, near)
        beyond[8:12, :] = jnp.where(even, first, far)
        slab = lax.axis_index("space")
        at_end = (slab == 0) | (slab == lax.axis_size("space") - 1)
        word = got_outer[8:, :].astype(jnp.int32)
        word = jnp.where(at_end, jnp.bitwise_or(word, DEAD), word)
        stages.append((word, beyond, 0, pulled))
        pulled[...] = jnp.zeros_like(pulled)
    else:
        places[...] = blocks[0][...]
    def describe_group(i):
        word, rows, g, _ = stages[i]
        neighbours(rows, word, g, off.at[i], kind.at[i], dist.at[i])
        describe(kind.at[i], dist.at[i], rates, rad.at[i], desc.at[i])
        row = 4 * (g + 1) + 3
        return left_factor(desc.at[i], rows[row : row + 1, :])

    t1, t2, t3, l2, l3 = pairs
    layers = forward_layers((t1, t2, t3), wout)
    states = through(layers, [describe_group(i) for i in range(len(stages))])
    layers = backward_layers((t1, l2, l3))
    if inner:
        states += [[state_inner[i, j] for j in range(3)] for i in range(inner)]
    slopes = through(layers, states)
    for i in range(len(stages)):
        grad[i] = slopes[i]
    for i in range(len(stages), len(slopes)):
        grad_inner[i - len(stages)] = slopes[i]

    out[...] = jnp.zeros_like(out)
    for i, (word, rows, g, target) in enumerate(stages):
        slope = dist.at[i]
        slot_slopes(grad.at[i], kind.at[i], rates, rad.at[i], slope)
        centre = pair_forces(word, slope, off.at[i], pair.at[i], rel.at[i])
        centre = None if rows is beyond else centre
        scatter(pair.at[i], rel.at[i], slots, target, g, centre)
    if direct:
        out[4:8, :] += jnp.where(even, pulled[8:12, :], 0.0)
        out[4 * groups : 4 * groups + 4, :] += jnp.where(even, 0.0, pulled[0:4, :])
        to_inner[...] = jnp.where(even, out[4 * groups + 4 :, :], out[0:4, :])


def outer_stage(blocks, code, pairs, rates, wout, state_inner):
    slots, block = code.shape
    rate_count = rates.shape[0]
    chan = SPECIES * rate_count
    groups = block // LANES
    count = len({0, groups - 1})
    inner = groups - count
    direct = len(blocks) > 1
    f32 = jnp.float32
    out_shape = [pltpu.VMEM((4 * (groups + 2), LANES), f32)]
    operands = [*blocks, code, *pairs, rates, wout]
    if direct:
        out_shape.append(pltpu.VMEM((4, LANES), f32))
        count += 1
    if inner:
        out_shape.append(pltpu.VMEM((inner, chan, LANES), f32))
        operands.append(state_inner)
    return pl.pallas_call(
        functools.partial(outer_kernel, direct, inner),
        out_shape=out_shape,
        in_specs=[VMEM] * len(operands),
        out_specs=[VMEM] * len(out_shape),
        scratch_shapes=[
            pltpu.VMEM((4 * (groups + 2), LANES), f32),
            pltpu.VMEM((count, 3, slots, LANES), f32),
            pltpu.VMEM((count, slots, LANES), f32),
            pltpu.VMEM((count, slots, LANES), f32),
            pltpu.VMEM((count, slots * rate_count, LANES), f32),
            pltpu.VMEM((count, chan, LANES), f32),
            pltpu.VMEM((count, chan, LANES), f32),
            pltpu.VMEM((count, 6, slots, LANES), f32),
            pltpu.VMEM((count, 2, slots, LANES), jnp.float32),
            pltpu.VMEM((16, LANES), f32),
            pltpu.VMEM((16, LANES), f32),
        ],
        compiler_params=PARAMS,
        cost_estimate=cost(3.0),
        name="outer_forces",
    )(*operands)


def inner_force_kernel(code, rates, off, kind, rad, grad, out, slope, pair, rel):
    slots = code.shape[0]
    out[...] = jnp.zeros_like(out)
    for i in range(kind.shape[0]):
        word = code[:, (i + 1) * LANES : (i + 2) * LANES]
        slot_slopes(grad.at[i], kind.at[i], rates, rad.at[i], slope.at[i])
        centre = pair_forces(word, slope.at[i], off.at[i], pair.at[i], rel.at[i])
        scatter(pair.at[i], rel.at[i], slots, out, i, centre)


def inner_forces(code, rates, off, kind, rad, grad):
    slots, block = code.shape
    count = kind.shape[0]
    return pl.pallas_call(
        inner_force_kernel,
        out_shape=pltpu.VMEM((block // LANES * 4, LANES), jnp.float32),
        in_specs=[VMEM] * 6,
        out_specs=VMEM,
        scratch_shapes=[
            pltpu.VMEM((count, slots, LANES), jnp.float32),
            pltpu.VMEM((count, 6, slots, LANES), jnp.float32),
            pltpu.VMEM((count, 2, slots, LANES), jnp.float32),
        ],
        compiler_params=PARAMS,
        cost_estimate=cost(1.2),
        name="inner_forces",
    )(code, rates, off, kind, rad, grad)


def combine_kernel(inner, force, *refs):
    *rest, got_inner, out = refs
    total = force[4 : force.shape[0] - 4, :]
    if inner:
        total = total + rest[0][...]
    even = at_even("space")
    out[...] = total
    out[0:4, :] += jnp.where(even, 0.0, got_inner[...])
    out[out.shape[0] - 4 :, :] += jnp.where(even, got_inner[...], 0.0)


def combine(force, inner, got_inner):
    operands = [force, *inner, got_inner]
    return pl.pallas_call(
        functools.partial(combine_kernel, len(inner)),
        out_shape=pltpu.VMEM((force.shape[0] - 8, LANES), jnp.float32),
        in_specs=[VMEM] * len(operands),
        out_specs=VMEM,
        compiler_params=PARAMS,
        cost_estimate=cost(0.1),
        name="combine",
    )(*operands)


def bead_rows(array):
    beads, comps, atoms = array.shape
    split = array.reshape(beads, comps, atoms // LANES, LANES)
    return split.transpose(1, 2, 0, 3).reshape(-1, LANES)


def from_bead_rows(rows, shape):
    beads, comps, atoms = shape
    split = rows.reshape(comps, atoms // LANES, beads, LANES)
    return split.transpose(2, 0, 1, 3).reshape(shape)


def contract_kernel(table, beads, *refs):
    blocks, species, code = arranged(GATHER, refs), refs[NC], refs[NC + 1]
    out, to_inner, to_outer = refs[NC + 2 :]
    tiles = species.shape[0]
    weights = [
        [share(GATHER, r, table[r, j], table[-r % NC, j]) for j in range(beads)]
        for r in range(NC)
    ]
    for t in range(tiles):
        for c in range(3):
            total = None
            for r in range(NC):
                for j in range(beads):
                    row = (c * tiles + t) * beads + j
                    term = weights[r][j] * blocks[r][row : row + 1, :]
                    total = term if total is None else total + term
            out[4 * t + c : 4 * t + c + 1, :] = total
        out[4 * t + 3 : 4 * t + 4, :] = species[t : t + 1, :]
    even = at_even("space")
    last = code.shape[1] - LANES
    to_inner[...] = jnp.where(even, out[4 * tiles - 4 :, :], out[0:4, :])
    to_outer[0:8, :] = jnp.where(even, out[0:8, :], out[4 * tiles - 8 :, :])
    to_outer[8:, :] = jnp.where(even, code[:, 0:LANES], code[:, last:]).astype(jnp.float32)


def contract(table, beads, blocks, species, code):
    return pl.pallas_call(
        functools.partial(contract_kernel, table, beads),
        out_shape=[
            pltpu.VMEM((4 * species.shape[0], LANES), jnp.float32),
            pltpu.VMEM((4, LANES), jnp.float32),
            pltpu.VMEM((8 + code.shape[0], LANES), jnp.float32),
        ],
        in_specs=[VMEM] * (NC + 2),
        out_specs=[VMEM] * 3,
        compiler_params=PARAMS,
        cost_estimate=cost(0.2),
        name="contract",
    )(blocks[0], *(blocks[r] for r in GATHER[1]), species, code)


def masses_of(species):
    return per_species(species, MASS_TABLE)


def spring_kernel(beads, own, before, after, momenta, species, out):
    tiles = species.shape[0]
    pull = TIME_STEP * SPRING_RATE * masses_of(species[...])

    def side(row, ref, other):
        taken = ref[row : row + 1, :]
        if GATHER[0] == "turn":
            return taken
        return jnp.where(at_even("bead"), other[row : row + 1, :], taken)

    for m in range(3 * tiles):
        t, first, last = m % tiles, m * beads, m * beads + beads - 1
        for row in range(first, last + 1):
            here = own[row : row + 1, :]
            if row > first:
                below = own[row - 1 : row, :]
            else:
                below = side(last, before, after)
            if row < last:
                above = own[row + 1 : row + 2, :]
            else:
                above = side(first, after, before)
            laplace = 2.0 * here - below - above
            out[row : row + 1, :] = momenta[row : row + 1, :] - pull[t : t + 1, :] * laplace


def spring_kick(beads, own, before, after, momenta, species):
    return pl.pallas_call(
        functools.partial(spring_kernel, beads),
        out_shape=pltpu.VMEM(own.shape, jnp.float32),
        in_specs=[VMEM] * 5,
        out_specs=VMEM,
        compiler_params=PARAMS,
        cost_estimate=cost(0.8),
        name="spring_kick",
    )(own, before, after, momenta, species)


def expand_kernel(table, beads, *refs):
    forces, kicked, species = arranged(SPREAD, refs), refs[NC], refs[NC + 1]
    momenta, displacement = refs[NC + 2 :]
    tiles = species.shape[0]
    scale = TIME_STEP * beads * NC / NC
    weights = [
        [
            share(SPREAD, r, scale * table[-r % NC, j], scale * table[r, j])
            for j in range(beads)
        ]
        for r in range(NC)
    ]
    drift = per_species(species[...], [TIME_STEP / m for m in MASS_TABLE])
    for c in range(3):
        for t in range(tiles):
            pulls = [force[4 * t + c : 4 * t + c + 1, :] for force in forces]
            for j in range(beads):
                row = (c * tiles + t) * beads + j
                total = kicked[row : row + 1, :]
                for r in range(NC):
                    total = total + weights[r][j] * pulls[r]
                momenta[row : row + 1, :] = total
                displacement[row : row + 1, :] = drift[t : t + 1, :] * total


def expand(table, beads, forces, kicked, species):
    shape = jax.ShapeDtypeStruct(kicked.shape, jnp.float32)
    return pl.pallas_call(
        functools.partial(expand_kernel, table, beads),
        out_shape=[shape, shape],
        in_specs=[VMEM] * (NC + 2),
        out_specs=[VMEM] * 2,
        compiler_params=PARAMS,
        cost_estimate=cost(0.8),
        name="expand",
    )(forces[0], *(forces[r] for r in SPREAD[1]), kicked, species)


def swap_inner(block):
    count = lax.axis_size("space")
    return lax.ppermute(block, "space", [(i, i ^ 1) for i in range(count)])


def swap_outer(block):
    count = lax.axis_size("space")
    pairs = [(i, (i + 1) % count if i % 2 else (i - 1) % count) for i in range(count)]
    return lax.ppermute(block, "space", pairs)


def arranged(plan, refs):
    return [refs[0]] + [refs[1 + plan[1].index(r)] for r in range(1, NC)]


def share(plan, distance, behind, ahead):
    behind, ahead = float(behind), float(ahead)
    if plan[0] == "turn" or behind == ahead or distance == 0:
        return behind
    return jnp.where(at_even("bead"), ahead, behind)


def around(plan, block):
    count = lax.axis_size("bead")
    blocks = [block]
    for r in range(1, count):
        if plan[0] == "turn":
            pairs = [(i, (i + r) % count) for i in range(count)]
        else:
            pairs = [(i, i ^ r) for i in range(count)]
        blocks.append(lax.ppermute(block, "bead", pairs))
    return blocks


def on_device(
    positions,
    momenta,
    species,
    neighbour_index,
    neighbour_count,
    radial_rates,
    weight_input,
    embedding,
    weight_middle,
    weight_deeper,
    weight_output,
):
    bead_dev = positions.shape[0]
    atom_dev = positions.shape[2]
    bead_groups = lax.axis_size("bead")
    bead_count = bead_dev * bead_groups
    table = contraction_table(bead_count, NC)
    place = lax.axis_index("bead")
    tiles = atom_dev // LANES
    direct = bead_groups == NC and tiles > 1
    block_size = atom_dev * NC // bead_groups

    if direct:
        block_start = 0
        slots, counts = neighbour_index, neighbour_count
    else:
        block_start = (place // NC) * block_size
        slots = lax.dynamic_slice_in_dim(neighbour_index, block_start, block_size, 1)
        counts = lax.dynamic_slice_in_dim(neighbour_count, block_start, block_size, 0)
    code, kinds, pairs, rates, wout = prepare(
        atom_dev,
        lambda: 0 if direct else (lax.axis_index("bead") // NC) * block_size,
        slots,
        counts,
        species.reshape(tiles, LANES),
        weight_input,
        embedding,
        weight_middle,
        weight_deeper,
        radial_rates,
        weight_output,
    )

    if direct:
        blocks = around(GATHER, bead_rows(positions))
        own, to_inner, to_outer = contract(table, bead_dev, blocks, kinds, code)
    else:
        replica = place % NC
        everything = lax.all_gather(positions, "bead", axis=0, tiled=True)
        weights = lax.dynamic_index_in_dim(jnp.asarray(table), replica, 0, keepdims=False)
        contracted = jnp.sum(weights[:, None, None] * everything, axis=0)
        stacked = contracted.reshape(3, tiles, LANES).transpose(1, 0, 2)
        own = jnp.concatenate([stacked, kinds[:, None]], axis=1).reshape(-1, LANES)

    if direct:
        got_outer, got_inner = swap_outer(to_outer), swap_inner(to_inner)
        inner_count = max(tiles - 2, 0)
        state_inner, others = None, []
        if inner_count:
            off, kind, rad, state_inner = inner_stage(
                own, code, rates, pairs, wout, inner_count
            )
        force, to_inner, *grad_inner = outer_stage(
            [own, got_outer, got_inner], code, pairs, rates, wout, state_inner
        )
        got_inner = swap_inner(to_inner)
        if inner_count:
            others = [inner_forces(code, rates, off, kind, rad, *grad_inner)]
        forces = around(SPREAD, combine(force, others, got_inner))
        kicked = spring_kick(
            bead_dev, blocks[0], blocks[1], blocks[NC - 1], bead_rows(momenta), kinds
        )
        moved = expand(table, bead_dev, forces, kicked, kinds)
        return tuple(from_bead_rows(rows, positions.shape) for rows in moved)

    even = at_even("space")
    bottom, top = own[:4], own[4 * tiles - 4 :]
    got_inner = swap_inner(jnp.where(even, top, bottom))
    got_outer = swap_outer(jnp.where(even, bottom, top))
    window = jnp.concatenate(
        [
            jnp.where(even, got_outer, got_inner),
            own,
            jnp.where(even, got_inner, got_outer),
        ],
        axis=0,
    )
    first = block_start // LANES * 4
    groups = block_size // LANES
    window = lax.dynamic_slice_in_dim(window, first, 4 * (groups + 2), 0)
    state_inner = None
    if groups > 2:
        inside = window[4 : 4 * groups + 4]
        off, kind, rad, state_inner = inner_stage(
            inside, code, rates, pairs, wout, groups - 2
        )
    force, *grad_inner = outer_stage([window], code, pairs, rates, wout, state_inner)
    if groups > 2:
        force = force.at[4 : 4 * groups + 4].add(
            inner_forces(code, rates, off, kind, rad, *grad_inner)
        )
    partial = jnp.zeros((4 * (tiles + 2), LANES), jnp.float32)
    partial = lax.dynamic_update_slice_in_dim(partial, force, first, 0)
    chosen = (jnp.arange(NC, dtype=jnp.int32) == replica).astype(jnp.float32)
    force = lax.psum(chosen[:, None, None] * partial[None], "bead")

    lower, middle, upper = force[:, :4], force[:, 4:-4], force[:, -4:]
    got_inner = swap_inner(jnp.where(even, upper, lower))
    got_outer = swap_outer(jnp.where(even, lower, upper))
    middle = jnp.concatenate(
        [
            middle[:, :4] + jnp.where(even, got_outer, got_inner),
            middle[:, 4:-4],
            middle[:, -4:] + jnp.where(even, got_inner, got_outer),
        ],
        axis=1,
    )

    first = place * bead_dev
    below = lax.dynamic_index_in_dim(everything, (first - 1) % bead_count, 0)
    above = lax.dynamic_index_in_dim(everything, (first + bead_dev) % bead_count, 0)
    whole = middle.reshape(NC, tiles, 4, LANES).transpose(0, 2, 1, 3)[:, :3]
    whole = whole.reshape(NC, 3, atom_dev)
    columns = lax.dynamic_slice_in_dim(jnp.asarray(table), first, bead_dev, 1)
    expanded = jnp.sum(columns[:, :, None, None] * whole[:, None], axis=0)
    expanded = bead_count / NC * expanded
    masses = masses_of(species)
    cycle = jnp.concatenate([below, positions, above], axis=0)
    laplace = 2.0 * positions - cycle[:-2] - cycle[2:]
    spring = -SPRING_RATE * masses * laplace
    momenta_next = momenta + TIME_STEP * (spring + expanded)
    return (momenta_next, TIME_STEP * momenta_next / masses)


def solution(mesh):
    return jax.shard_map(
        on_device,
        mesh=mesh,
        in_specs=(
            P(("grp", "bead"), None, "space"),
            P(("grp", "bead"), None, "space"),
            P(("grp", "space")),
            P(None, ("grp", "space")),
            P(("grp", "space")),
            P(),
            P(),
            P(),
            P(),
            P(),
            P(),
        ),
        out_specs=(P(("grp", "bead"), None, "space"), P(("grp", "bead"), None, "space")),
        check_vma=False,
    )
```

```python
import functools

import jax
import jax.numpy as jnp
import numpy as np
from jax import lax
from jax.experimental import pallas as pl
from jax.experimental.pallas import tpu as pltpu
from jax.sharding import PartitionSpec as P

HALO = 128
NC = 4
SPECIES = 4
LANES = 128
DEAD = 4096
LOG2E = 1.4426950408889634

MASS_TABLE = (1.0, 0.25, 1.5, 2.0)
SPRING_RATE = 0.2
TIME_STEP = 0.5

GATHER = ("swap", (1, 3, 2))
SPREAD = ("turn", (3, 2, 1))


def contraction_table(bead_count, kept_modes):
    rows = np.arange(kept_modes)[:, None] / kept_modes
    cols = np.arange(bead_count)[None, :] / bead_count
    angles = 2.0 * np.pi * (rows - cols)
    summed = np.ones_like(angles)
    for order in range(1, kept_modes // 2):
        summed = summed + 2.0 * np.cos(order * angles)
    summed = summed + np.cos(kept_modes // 2 * angles)
    return (summed / bead_count).astype(np.float32)


def per_species(species, values):
    picked = jnp.full(species.shape, values[0], jnp.float32)
    for kind in range(1, SPECIES):
        picked = jnp.where(species == kind, values[kind], picked)
    return picked


VMEM = pl.BlockSpec(memory_space=pltpu.VMEM)
PARAMS = pltpu.CompilerParams(vmem_limit_bytes=16 * 1024 * 1024)


def cost(micros):
    return pl.CostEstimate(
        flops=0, transcendentals=0, bytes_accessed=int(micros * 3_000_000)
    )


def at_even(axis):
    return jnp.bitwise_and(lax.axis_index(axis), 1) == 0


def split2(value):
    high = value.astype(jnp.bfloat16)
    low = (value - high.astype(jnp.float32)).astype(jnp.bfloat16)
    return high, low


def dot(lhs, rhs):
    return lax.dot_general(
        lhs, rhs, (((1,), (0,)), ((), ())), preferred_element_type=jnp.float32
    )


def dot_nt(lhs, rhs):
    return lax.dot_general(
        lhs, rhs, (((1,), (1,)), ((), ())), preferred_element_type=jnp.float32
    )


def prepare_kernel(slab_atoms, block_start, *refs):
    held, outs = refs[:9], refs[9:18]
    copied, sems = refs[18:27], refs[27]
    copies = [
        pltpu.make_async_copy(src, dst, sems.at[i])
        for i, (src, dst) in enumerate(zip(held, copied, strict=True))
    ]
    for copy in copies:
        copy.start()
    slots, counts, species, w1, emb, w2, w3, rates, wout = copied
    code, kinds, t1, t2, t3, l2, l3, rates_b, wout_b = outs
    for copy in copies[:3]:
        copy.wait()
    kinds[...] = species[...].astype(jnp.float32)

    slab = lax.axis_index("space")
    last = lax.axis_size("space") - 1
    lowest = jnp.where(slab == 0, HALO, 0)
    highest = jnp.where(slab == last, slab_atoms + HALO, slab_atoms + 2 * HALO)
    word = slots[...]
    slot_ids = lax.broadcasted_iota(jnp.int32, word.shape, 0)
    lane_ids = lax.broadcasted_iota(jnp.int32, word.shape, 1)
    live = (slot_ids < counts[...]) & (word >= lowest) & (word < highest)
    band = word - block_start() - jnp.bitwise_and(lane_ids, -LANES)
    code[...] = jnp.where(live, band, band + DEAD)

    for copy in copies[3:]:
        copy.wait()
    chan = w1.shape[1]
    t1[0:chan, :], t1[chan : 2 * chan, :] = split2(w1[...].T)
    e = emb[...]
    eh = e.astype(jnp.bfloat16).astype(jnp.float32)
    el = (e - eh).astype(jnp.bfloat16).astype(jnp.float32)
    rest = jnp.zeros((chan - 3 * SPECIES, e.shape[1]), jnp.float32)
    terms = jnp.concatenate([eh, el, e - eh - el, rest], axis=0)
    t1[2 * chan : 3 * chan, :] = terms.astype(jnp.bfloat16)
    for src, fwd, bwd in ((w2, t2, l2), (w3, t3, l3)):
        hid = src.shape[0]
        fwd[0:hid, :], fwd[hid : 2 * hid, :] = split2(src[...].T)
        bwd[0:hid, :], bwd[hid : 2 * hid, :] = split2(src[...])
    count = rates.shape[1]
    tall = jnp.concatenate(
        [rates[...], jnp.zeros((1, LANES - count), jnp.float32)], axis=1
    )
    rates_b[...] = jnp.broadcast_to(tall, (LANES, LANES)).T[0:count, :]
    wout_b[...] = jnp.broadcast_to(wout[...], wout_b.shape)


def prepare(slab_atoms, block_start, slots, counts, species, w1, emb, w2, w3, rates, wout):
    hid, chan = w1.shape
    shapes = [
        (3 * chan, hid),
        (2 * hid, hid),
        (2 * hid, hid),
        (2 * hid, hid),
        (2 * hid, hid),
    ]
    out_shape = [
        pltpu.VMEM(slots.shape, jnp.int32),
        pltpu.VMEM(species.shape, jnp.float32),
    ]
    out_shape += [pltpu.VMEM(s, jnp.bfloat16) for s in shapes]
    out_shape += [
        pltpu.VMEM((rates.shape[0], LANES), jnp.float32),
        pltpu.VMEM((8, hid), jnp.float32),
    ]
    operands = (
        slots,
        counts[None, :],
        species,
        w1,
        emb.T,
        w2,
        w3,
        rates[None, :],
        wout[None, :],
    )
    code, kinds, *pairs, rates_b, wout_b = pl.pallas_call(
        functools.partial(prepare_kernel, slab_atoms, block_start),
        out_shape=out_shape,
        in_specs=[pl.BlockSpec(memory_space=pltpu.HBM)] * len(operands),
        out_specs=[VMEM] * len(out_shape),
        scratch_shapes=[pltpu.VMEM(x.shape, x.dtype) for x in operands]
        + [pltpu.SemaphoreType.DMA((len(operands),))],
        cost_estimate=cost(1.2),
        name="prepare",
    )(*operands)
    return code, kinds, pairs, rates_b, wout_b


def neighbours(places, word, g, off, kind, dist):
    src = [
        [
            jnp.broadcast_to(
                places[4 * (g + q) + c : 4 * (g + q) + c + 1, :], (8, LANES)
            )
            for q in range(3)
        ]
        for c in range(4)
    ]
    for o in range(word.shape[0] // 8):
        rows = slice(8 * o, 8 * o + 8)
        lane = jnp.bitwise_and(word[rows, :], LANES - 1)
        part = jnp.bitwise_and(word[rows, :], DEAD - 1)
        is0 = part < LANES
        is1 = part < 2 * LANES
        got = []
        for c in range(4):
            x0, x1, x2 = (
                jnp.take_along_axis(src[c][q], lane, axis=1) for q in range(3)
            )
            got.append(jnp.where(is0, x0, jnp.where(is1, x1, x2)))
        total = None
        for c in range(3):
            diff = got[c] - src[c][1]
            off[c, rows, :] = diff
            total = diff * diff if total is None else total + diff * diff
        dist[rows, :] = total
        kind[rows, :] = jnp.where(word[rows, :] >= DEAD, -1.0, got[3])


def describe(kind, dist, rates, rad, desc):
    slots = kind.shape[0]
    rate_count = rates.shape[0]
    octets = rate_count // 8
    rate8 = [rates[8 * o : 8 * o + 8, :] * (-LOG2E) for o in range(octets)]
    acc = [[jnp.zeros((8, LANES), jnp.float32)] * octets for _ in range(SPECIES)]
    for n in range(slots):
        kind_n = jnp.broadcast_to(kind[n : n + 1, :], (8, LANES))
        dist_n = jnp.broadcast_to(dist[n : n + 1, :], (8, LANES))
        masks = [kind_n == float(s) for s in range(SPECIES)]
        for o in range(octets):
            radial = jnp.exp2(rate8[o] * dist_n)
            first = n * rate_count + 8 * o
            rad[first : first + 8, :] = radial
            for s in range(SPECIES):
                acc[s][o] = jnp.where(masks[s], acc[s][o] + radial, acc[s][o])
    for s in range(SPECIES):
        for o in range(octets):
            first = s * rate_count + 8 * o
            desc[first : first + 8, :] = acc[s][o]


def left_factor(desc, centre):
    chan = desc.shape[0]
    high, low = split2(desc[...].T)
    ids = lax.broadcasted_iota(jnp.int32, (chan, LANES), 0)
    ids = jnp.where(ids < 3 * SPECIES, jnp.bitwise_and(ids, SPECIES - 1), -1)
    onehot = jnp.where(ids.astype(jnp.float32) == centre, 1.0, 0.0)
    onehot = onehot.T.astype(jnp.bfloat16)
    return jnp.concatenate([high, high, low, onehot], axis=1)


def dense(x, pair):
    high, low = split2(x)
    rows = pair.shape[0] // 2
    right = jnp.concatenate([pair[...], pair[0:rows, :]], axis=0)
    return dot(jnp.concatenate([high, high, low], axis=1), right)


def act(x):
    sig = 0.5 + 0.5 * jnp.tanh(0.5 * x)
    value = x * sig
    return value, sig + value * (1.0 - sig)


def forward_layers(pairs, wout):
    t1, t2, t3 = pairs
    chan = t1.shape[0] // 3
    first = jnp.concatenate([t1[0 : 2 * chan, :], t1[0:chan, :], t1[2 * chan :, :]], axis=0)

    def one(left):
        return act(dot(left, first))

    def two(state):
        value, s1 = state
        return act(dense(value, t2)), s1

    def three(state):
        (value, s2), s1 = state
        return s1, s2, wout[0:1, :] * act(dense(value, t3))[1]

    return one, two, three


def backward_layers(pairs):
    t1, l2, l3 = pairs
    chan = t1.shape[0] // 3

    def three(state):
        s1, s2, grad = state
        return s1, dense(grad, l3) * s2

    def two(state):
        s1, grad = state
        return dense(grad, l2) * s1

    def one(grad):
        high, low = split2(grad)
        last = [t1[0:chan, :], t1[chan : 2 * chan, :], t1[0:chan, :]]
        return dot_nt(
            jnp.concatenate(last, axis=1), jnp.concatenate([high, high, low], axis=1)
        )

    return three, two, one


def through(layers, states):
    for layer in layers:
        states = [layer(state) for state in states]
    return states


def slot_slopes(grad, kind, rates, rad, slope):
    slots = kind.shape[0]
    rate_count = rates.shape[0]
    octets = rate_count // 8
    grads = [
        [
            grad[s * rate_count + 8 * o : s * rate_count + 8 * o + 8, :]
            * rates[8 * o : 8 * o + 8, :]
            for o in range(octets)
        ]
        for s in range(SPECIES)
    ]
    for n in range(slots):
        kind_n = jnp.broadcast_to(kind[n : n + 1, :], (8, LANES))
        masks = [kind_n == float(s) for s in range(SPECIES - 1)]
        total = None
        for o in range(octets):
            picked = grads[SPECIES - 1][o]
            for s in range(SPECIES - 1):
                picked = jnp.where(masks[s], grads[s][o], picked)
            first = n * rate_count + 8 * o
            term = picked * rad[first : first + 8, :]
            total = term if total is None else total + term
        slope[n : n + 1, :] = jnp.sum(total, axis=0, keepdims=True)


def pair_forces(word, slope, off, pair, rel):
    sums = [jnp.zeros((8, LANES), jnp.float32)] * 3
    for o in range(word.shape[0] // 8):
        rows = slice(8 * o, 8 * o + 8)
        part = jnp.bitwise_and(word[rows, :], DEAD - 1)
        rel[0, rows, :] = jnp.bitwise_and(part, 63).astype(jnp.float32)
        rel[1, rows, :] = jnp.right_shift(part, 6).astype(jnp.float32)
        twice = jnp.where(word[rows, :] >= DEAD, 0.0, 2.0 * slope[rows, :])
        for c in range(3):
            force = twice * off[c, rows, :]
            sums[c] = sums[c] + force
            high = force.astype(jnp.bfloat16).astype(jnp.float32)
            pair[2 * c, rows, :] = high
            pair[2 * c + 1, rows, :] = force - high
    return [jnp.sum(x, axis=0, keepdims=True) for x in sums]


def scatter(pair, rel, slots, out, block0, centre):
    half = jnp.bfloat16
    low_ids = lax.broadcasted_iota(jnp.int32, (64, LANES), 0).astype(half)
    high_ids = lax.broadcasted_iota(jnp.int32, (16, LANES), 0)
    high_ids = jnp.bitwise_and(high_ids, 7).astype(half)
    ones, zeros = jnp.ones((64, LANES), half), jnp.zeros((64, LANES), half)
    total = jnp.zeros((48, 64), jnp.float32)
    for n in range(0, slots, 2):
        lefts, rights = [], []
        for k in (n, n + 1):
            low = jnp.broadcast_to(rel[0, k : k + 1, :], (16, LANES)).astype(half)
            high = jnp.broadcast_to(rel[1, k : k + 1, :], (16, LANES)).astype(half)
            low = jnp.concatenate([low] * 4, axis=0)
            rights.append(jnp.where(low_ids == low, ones, zeros))
            hit = high_ids == high
            for c in range(3):
                terms = [
                    jnp.broadcast_to(pair[2 * c + i, k : k + 1, :], (8, LANES))
                    for i in range(2)
                ]
                terms = jnp.concatenate(terms, axis=0).astype(half)
                lefts.append(jnp.where(hit, terms, zeros[0:16]))
        lefts = [jnp.concatenate(lefts[0:3], axis=0), jnp.concatenate(lefts[3:6], axis=0)]
        total = total + dot_nt(
            jnp.concatenate(lefts, axis=1), jnp.concatenate(rights, axis=1)
        )
    for c in range(3):
        merged = total[16 * c : 16 * c + 8, :] + total[16 * c + 8 : 16 * c + 16, :]
        for q in range(3):
            row = 4 * (block0 + q) + c
            both = jnp.concatenate(
                [merged[2 * q : 2 * q + 1, :], merged[2 * q + 1 : 2 * q + 2, :]], axis=1
            )
            if q == 1 and centre is not None:
                both = both - centre[c]
            out[row : row + 1, :] = out[row : row + 1, :] + both


def inner_kernel(own, code, rates, t1, t2, t3, wout, off, kind, rad, state, dist, desc):
    lefts = []
    for i in range(kind.shape[0]):
        word = code[:, (i + 1) * LANES : (i + 2) * LANES]
        neighbours(own, word, i, off.at[i], kind.at[i], dist.at[i])
        describe(kind.at[i], dist.at[i], rates, rad.at[i], desc.at[i])
        row = 4 * (i + 1) + 3
        lefts.append(left_factor(desc.at[i], own[row : row + 1, :]))
    states = through(forward_layers((t1, t2, t3), wout), lefts)
    for i, values in enumerate(states):
        for j, value in enumerate(values):
            state[i, j] = value


def inner_stage(own, code, rates, pairs, wout, count):
    slots = code.shape[0]
    rate_count = rates.shape[0]
    chan = SPECIES * rate_count
    out_shape = [
        pltpu.VMEM((count, 3, slots, LANES), jnp.float32),
        pltpu.VMEM((count, slots, LANES), jnp.float32),
        pltpu.VMEM((count, slots * rate_count, LANES), jnp.float32),
        pltpu.VMEM((count, 3, LANES, wout.shape[1]), jnp.float32),
    ]
    return pl.pallas_call(
        inner_kernel,
        out_shape=out_shape,
        in_specs=[VMEM] * 7,
        out_specs=[VMEM] * 4,
        scratch_shapes=[
            pltpu.VMEM((count, slots, LANES), jnp.float32),
            pltpu.VMEM((count, chan, LANES), jnp.float32),
        ],
        compiler_params=PARAMS,
        cost_estimate=cost(1.0),
        name="inner_forward",
    )(own, code, rates, *pairs[:3], wout)


def outer_kernel(direct, inner, *refs):
    refs = list(refs)

    def take(count):
        taken = refs[:count]
        del refs[:count]
        return taken

    blocks = take(3 if direct else 1)
    code, *pairs, rates, wout = take(9 - 1)
    state_inner = take(1)[0] if inner else None
    out = take(1)[0]
    to_inner = take(1)[0] if direct else None
    grad_inner = take(1)[0] if inner else None
    places, off, kind, dist, rad, desc, grad, pair, rel, beyond, pulled = refs
    slots, block = code.shape
    groups = block // LANES
    stages = [
        (code[:, g * LANES : (g + 1) * LANES], places, g, out)
        for g in sorted({0, groups - 1})
    ]
    if direct:
        own, got_outer, got_inner = blocks
        even = at_even("space")
        first, last = own[0:4, :], own[4 * groups - 4 :, :]
        near, far = got_outer[0:4, :], got_outer[4:8, :]
        places[0:4, :] = jnp.where(even, far, got_inner[...])
        places[4 : 4 * groups + 4, :] = own[...]
        places[4 * groups + 4 :, :] = jnp.where(even, got_inner[...], near)
        beyond[0:4, :] = jnp.where(even, near, last)
        beyond[4:8, :] = jnp.where(even, far, near)
        beyond[8:12, :] = jnp.where(even, first, far)
        slab = lax.axis_index("space")
        at_end = (slab == 0) | (slab == lax.axis_size("space") - 1)
        word = got_outer[8:, :].astype(jnp.int32)
        word = jnp.where(at_end, jnp.bitwise_or(word, DEAD), word)
        stages.append((word, beyond, 0, pulled))
        pulled[...] = jnp.zeros_like(pulled)
    else:
        places[...] = blocks[0][...]
    def describe_group(i):
        word, rows, g, _ = stages[i]
        neighbours(rows, word, g, off.at[i], kind.at[i], dist.at[i])
        describe(kind.at[i], dist.at[i], rates, rad.at[i], desc.at[i])
        row = 4 * (g + 1) + 3
        return left_factor(desc.at[i], rows[row : row + 1, :])

    t1, t2, t3, l2, l3 = pairs
    layers = forward_layers((t1, t2, t3), wout)
    states = through(layers, [describe_group(i) for i in range(len(stages))])
    layers = backward_layers((t1, l2, l3))
    if inner:
        states += [[state_inner[i, j] for j in range(3)] for i in range(inner)]
    slopes = through(layers, states)
    for i in range(len(stages)):
        grad[i] = slopes[i]
    for i in range(len(stages), len(slopes)):
        grad_inner[i - len(stages)] = slopes[i]

    out[...] = jnp.zeros_like(out)
    for i, (word, rows, g, target) in enumerate(stages):
        slope = dist.at[i]
        slot_slopes(grad.at[i], kind.at[i], rates, rad.at[i], slope)
        centre = pair_forces(word, slope, off.at[i], pair.at[i], rel.at[i])
        centre = None if rows is beyond else centre
        scatter(pair.at[i], rel.at[i], slots, target, g, centre)
    if direct:
        out[4:8, :] += jnp.where(even, pulled[8:12, :], 0.0)
        out[4 * groups : 4 * groups + 4, :] += jnp.where(even, 0.0, pulled[0:4, :])
        to_inner[...] = jnp.where(even, out[4 * groups + 4 :, :], out[0:4, :])


def outer_stage(blocks, code, pairs, rates, wout, state_inner):
    slots, block = code.shape
    rate_count = rates.shape[0]
    chan = SPECIES * rate_count
    groups = block // LANES
    count = len({0, groups - 1})
    inner = groups - count
    direct = len(blocks) > 1
    f32 = jnp.float32
    out_shape = [pltpu.VMEM((4 * (groups + 2), LANES), f32)]
    operands = [*blocks, code, *pairs, rates, wout]
    if direct:
        out_shape.append(pltpu.VMEM((4, LANES), f32))
        count += 1
    if inner:
        out_shape.append(pltpu.VMEM((inner, chan, LANES), f32))
        operands.append(state_inner)
    return pl.pallas_call(
        functools.partial(outer_kernel, direct, inner),
        out_shape=out_shape,
        in_specs=[VMEM] * len(operands),
        out_specs=[VMEM] * len(out_shape),
        scratch_shapes=[
            pltpu.VMEM((4 * (groups + 2), LANES), f32),
            pltpu.VMEM((count, 3, slots, LANES), f32),
            pltpu.VMEM((count, slots, LANES), f32),
            pltpu.VMEM((count, slots, LANES), f32),
            pltpu.VMEM((count, slots * rate_count, LANES), f32),
            pltpu.VMEM((count, chan, LANES), f32),
            pltpu.VMEM((count, chan, LANES), f32),
            pltpu.VMEM((count, 6, slots, LANES), f32),
            pltpu.VMEM((count, 2, slots, LANES), jnp.float32),
            pltpu.VMEM((16, LANES), f32),
            pltpu.VMEM((16, LANES), f32),
        ],
        compiler_params=PARAMS,
        cost_estimate=cost(3.0),
        name="outer_forces",
    )(*operands)


def inner_force_kernel(code, rates, off, kind, rad, grad, out, slope, pair, rel):
    slots = code.shape[0]
    out[...] = jnp.zeros_like(out)
    for i in range(kind.shape[0]):
        word = code[:, (i + 1) * LANES : (i + 2) * LANES]
        slot_slopes(grad.at[i], kind.at[i], rates, rad.at[i], slope.at[i])
        centre = pair_forces(word, slope.at[i], off.at[i], pair.at[i], rel.at[i])
        scatter(pair.at[i], rel.at[i], slots, out, i, centre)


def inner_forces(code, rates, off, kind, rad, grad):
    slots, block = code.shape
    count = kind.shape[0]
    return pl.pallas_call(
        inner_force_kernel,
        out_shape=pltpu.VMEM((block // LANES * 4, LANES), jnp.float32),
        in_specs=[VMEM] * 6,
        out_specs=VMEM,
        scratch_shapes=[
            pltpu.VMEM((count, slots, LANES), jnp.float32),
            pltpu.VMEM((count, 6, slots, LANES), jnp.float32),
            pltpu.VMEM((count, 2, slots, LANES), jnp.float32),
        ],
        compiler_params=PARAMS,
        cost_estimate=cost(1.2),
        name="inner_forces",
    )(code, rates, off, kind, rad, grad)


def combine_kernel(inner, force, *refs):
    *rest, got_inner, out = refs
    total = force[4 : force.shape[0] - 4, :]
    if inner:
        total = total + rest[0][...]
    even = at_even("space")
    out[...] = total
    out[0:4, :] += jnp.where(even, 0.0, got_inner[...])
    out[out.shape[0] - 4 :, :] += jnp.where(even, got_inner[...], 0.0)


def combine(force, inner, got_inner):
    operands = [force, *inner, got_inner]
    return pl.pallas_call(
        functools.partial(combine_kernel, len(inner)),
        out_shape=pltpu.VMEM((force.shape[0] - 8, LANES), jnp.float32),
        in_specs=[VMEM] * len(operands),
        out_specs=VMEM,
        compiler_params=PARAMS,
        cost_estimate=cost(0.1),
        name="combine",
    )(*operands)


def bead_rows(array):
    beads, comps, atoms = array.shape
    split = array.reshape(beads, comps, atoms // LANES, LANES)
    return split.transpose(1, 2, 0, 3).reshape(-1, LANES)


def from_bead_rows(rows, shape):
    beads, comps, atoms = shape
    split = rows.reshape(comps, atoms // LANES, beads, LANES)
    return split.transpose(2, 0, 1, 3).reshape(shape)


def contract_kernel(table, beads, *refs):
    blocks, species, code = arranged(GATHER, refs), refs[NC], refs[NC + 1]
    out, to_inner, to_outer = refs[NC + 2 :]
    tiles = species.shape[0]
    weights = [
        [share(GATHER, r, table[r, j], table[-r % NC, j]) for j in range(beads)]
        for r in range(NC)
    ]
    for t in range(tiles):
        for c in range(3):
            total = None
            for r in range(NC):
                for j in range(beads):
                    row = (c * tiles + t) * beads + j
                    term = weights[r][j] * blocks[r][row : row + 1, :]
                    total = term if total is None else total + term
            out[4 * t + c : 4 * t + c + 1, :] = total
        out[4 * t + 3 : 4 * t + 4, :] = species[t : t + 1, :]
    even = at_even("space")
    last = code.shape[1] - LANES
    to_inner[...] = jnp.where(even, out[4 * tiles - 4 :, :], out[0:4, :])
    to_outer[0:8, :] = jnp.where(even, out[0:8, :], out[4 * tiles - 8 :, :])
    to_outer[8:, :] = jnp.where(even, code[:, 0:LANES], code[:, last:]).astype(jnp.float32)


def contract(table, beads, blocks, species, code):
    return pl.pallas_call(
        functools.partial(contract_kernel, table, beads),
        out_shape=[
            pltpu.VMEM((4 * species.shape[0], LANES), jnp.float32),
            pltpu.VMEM((4, LANES), jnp.float32),
            pltpu.VMEM((8 + code.shape[0], LANES), jnp.float32),
        ],
        in_specs=[VMEM] * (NC + 2),
        out_specs=[VMEM] * 3,
        compiler_params=PARAMS,
        cost_estimate=cost(0.2),
        name="contract",
    )(blocks[0], *(blocks[r] for r in GATHER[1]), species, code)


def masses_of(species):
    return per_species(species, MASS_TABLE)


def spring_kernel(beads, own, before, after, momenta, species, out):
    tiles = species.shape[0]
    pull = TIME_STEP * SPRING_RATE * masses_of(species[...])

    def side(row, ref, other):
        taken = ref[row : row + 1, :]
        if GATHER[0] == "turn":
            return taken
        return jnp.where(at_even("bead"), other[row : row + 1, :], taken)

    for m in range(3 * tiles):
        t, first, last = m % tiles, m * beads, m * beads + beads - 1
        for row in range(first, last + 1):
            here = own[row : row + 1, :]
            if row > first:
                below = own[row - 1 : row, :]
            else:
                below = side(last, before, after)
            if row < last:
                above = own[row + 1 : row + 2, :]
            else:
                above = side(first, after, before)
            laplace = 2.0 * here - below - above
            out[row : row + 1, :] = momenta[row : row + 1, :] - pull[t : t + 1, :] * laplace


def spring_kick(beads, own, before, after, momenta, species):
    return pl.pallas_call(
        functools.partial(spring_kernel, beads),
        out_shape=pltpu.VMEM(own.shape, jnp.float32),
        in_specs=[VMEM] * 5,
        out_specs=VMEM,
        compiler_params=PARAMS,
        cost_estimate=cost(0.8),
        name="spring_kick",
    )(own, before, after, momenta, species)


def expand_kernel(table, beads, *refs):
    forces, kicked, species = arranged(SPREAD, refs), refs[NC], refs[NC + 1]
    momenta, displacement = refs[NC + 2 :]
    tiles = species.shape[0]
    scale = TIME_STEP * beads * NC / NC
    weights = [
        [
            share(SPREAD, r, scale * table[-r % NC, j], scale * table[r, j])
            for j in range(beads)
        ]
        for r in range(NC)
    ]
    drift = per_species(species[...], [TIME_STEP / m for m in MASS_TABLE])
    for c in range(3):
        for t in range(tiles):
            pulls = [force[4 * t + c : 4 * t + c + 1, :] for force in forces]
            for j in range(beads):
                row = (c * tiles + t) * beads + j
                total = kicked[row : row + 1, :]
                for r in range(NC):
                    total = total + weights[r][j] * pulls[r]
                momenta[row : row + 1, :] = total
                displacement[row : row + 1, :] = drift[t : t + 1, :] * total


def expand(table, beads, forces, kicked, species):
    shape = jax.ShapeDtypeStruct(kicked.shape, jnp.float32)
    return pl.pallas_call(
        functools.partial(expand_kernel, table, beads),
        out_shape=[shape, shape],
        in_specs=[VMEM] * (NC + 2),
        out_specs=[VMEM] * 2,
        compiler_params=PARAMS,
        cost_estimate=cost(0.8),
        name="expand",
    )(forces[0], *(forces[r] for r in SPREAD[1]), kicked, species)


def swap_inner(block):
    count = lax.axis_size("space")
    return lax.ppermute(block, "space", [(i, i ^ 1) for i in range(count)])


def swap_outer(block):
    count = lax.axis_size("space")
    pairs = [(i, (i + 1) % count if i % 2 else (i - 1) % count) for i in range(count)]
    return lax.ppermute(block, "space", pairs)


def arranged(plan, refs):
    return [refs[0]] + [refs[1 + plan[1].index(r)] for r in range(1, NC)]


def share(plan, distance, behind, ahead):
    behind, ahead = float(behind), float(ahead)
    if plan[0] == "turn" or behind == ahead or distance == 0:
        return behind
    return jnp.where(at_even("bead"), ahead, behind)


def around(plan, block):
    count = lax.axis_size("bead")
    blocks = [block]
    for r in range(1, count):
        if plan[0] == "turn":
            pairs = [(i, (i + r) % count) for i in range(count)]
        else:
            pairs = [(i, i ^ r) for i in range(count)]
        blocks.append(lax.ppermute(block, "bead", pairs))
    return blocks


def on_device(
    positions,
    momenta,
    species,
    neighbour_index,
    neighbour_count,
    radial_rates,
    weight_input,
    embedding,
    weight_middle,
    weight_deeper,
    weight_output,
):
    bead_dev = positions.shape[0]
    atom_dev = positions.shape[2]
    bead_groups = lax.axis_size("bead")
    bead_count = bead_dev * bead_groups
    table = contraction_table(bead_count, NC)
    place = lax.axis_index("bead")
    tiles = atom_dev // LANES
    direct = bead_groups == NC and tiles > 1
    block_size = atom_dev * NC // bead_groups

    if direct:
        block_start = 0
        slots, counts = neighbour_index, neighbour_count
    else:
        block_start = (place // NC) * block_size
        slots = lax.dynamic_slice_in_dim(neighbour_index, block_start, block_size, 1)
        counts = lax.dynamic_slice_in_dim(neighbour_count, block_start, block_size, 0)
    code, kinds, pairs, rates, wout = prepare(
        atom_dev,
        lambda: 0 if direct else (lax.axis_index("bead") // NC) * block_size,
        slots,
        counts,
        species.reshape(tiles, LANES),
        weight_input,
        embedding,
        weight_middle,
        weight_deeper,
        radial_rates,
        weight_output,
    )

    if direct:
        blocks = around(GATHER, bead_rows(positions))
        own, to_inner, to_outer = contract(table, bead_dev, blocks, kinds, code)
    else:
        replica = place % NC
        everything = lax.all_gather(positions, "bead", axis=0, tiled=True)
        weights = lax.dynamic_index_in_dim(jnp.asarray(table), replica, 0, keepdims=False)
        contracted = jnp.sum(weights[:, None, None] * everything, axis=0)
        stacked = contracted.reshape(3, tiles, LANES).transpose(1, 0, 2)
        own = jnp.concatenate([stacked, kinds[:, None]], axis=1).reshape(-1, LANES)

    if direct:
        got_outer, got_inner = swap_outer(to_outer), swap_inner(to_inner)
        inner_count = max(tiles - 2, 0)
        state_inner, others = None, []
        if inner_count:
            off, kind, rad, state_inner = inner_stage(
                own, code, rates, pairs, wout, inner_count
            )
        force, to_inner, *grad_inner = outer_stage(
            [own, got_outer, got_inner], code, pairs, rates, wout, state_inner
        )
        got_inner = swap_inner(to_inner)
        if inner_count:
            others = [inner_forces(code, rates, off, kind, rad, *grad_inner)]
        forces = around(SPREAD, combine(force, others, got_inner))
        kicked = spring_kick(
            bead_dev, blocks[0], blocks[1], blocks[NC - 1], bead_rows(momenta), kinds
        )
        moved = expand(table, bead_dev, forces, kicked, kinds)
        return tuple(from_bead_rows(rows, positions.shape) for rows in moved)

    even = at_even("space")
    bottom, top = own[:4], own[4 * tiles - 4 :]
    got_inner = swap_inner(jnp.where(even, top, bottom))
    got_outer = swap_outer(jnp.where(even, bottom, top))
    window = jnp.concatenate(
        [
            jnp.where(even, got_outer, got_inner),
            own,
            jnp.where(even, got_inner, got_outer),
        ],
        axis=0,
    )
    first = block_start // LANES * 4
    groups = block_size // LANES
    window = lax.dynamic_slice_in_dim(window, first, 4 * (groups + 2), 0)
    state_inner = None
    if groups > 2:
        inside = window[4 : 4 * groups + 4]
        off, kind, rad, state_inner = inner_stage(
            inside, code, rates, pairs, wout, groups - 2
        )
    force, *grad_inner = outer_stage([window], code, pairs, rates, wout, state_inner)
    if groups > 2:
        force = force.at[4 : 4 * groups + 4].add(
            inner_forces(code, rates, off, kind, rad, *grad_inner)
        )
    partial = jnp.zeros((4 * (tiles + 2), LANES), jnp.float32)
    partial = lax.dynamic_update_slice_in_dim(partial, force, first, 0)
    chosen = (jnp.arange(NC, dtype=jnp.int32) == replica).astype(jnp.float32)
    force = lax.psum(chosen[:, None, None] * partial[None], "bead")

    lower, middle, upper = force[:, :4], force[:, 4:-4], force[:, -4:]
    got_inner = swap_inner(jnp.where(even, upper, lower))
    got_outer = swap_outer(jnp.where(even, lower, upper))
    middle = jnp.concatenate(
        [
            middle[:, :4] + jnp.where(even, got_outer, got_inner),
            middle[:, 4:-4],
            middle[:, -4:] + jnp.where(even, got_inner, got_outer),
        ],
        axis=1,
    )

    first = place * bead_dev
    below = lax.dynamic_index_in_dim(everything, (first - 1) % bead_count, 0)
    above = lax.dynamic_index_in_dim(everything, (first + bead_dev) % bead_count, 0)
    whole = middle.reshape(NC, tiles, 4, LANES).transpose(0, 2, 1, 3)[:, :3]
    whole = whole.reshape(NC, 3, atom_dev)
    columns = lax.dynamic_slice_in_dim(jnp.asarray(table), first, bead_dev, 1)
    expanded = jnp.sum(columns[:, :, None, None] * whole[:, None], axis=0)
    expanded = bead_count / NC * expanded
    masses = masses_of(species)
    cycle = jnp.concatenate([below, positions, above], axis=0)
    laplace = 2.0 * positions - cycle[:-2] - cycle[2:]
    spring = -SPRING_RATE * masses * laplace
    momenta_next = momenta + TIME_STEP * (spring + expanded)
    return (momenta_next, TIME_STEP * momenta_next / masses)


def solution(mesh):
    return jax.shard_map(
        on_device,
        mesh=mesh,
        in_specs=(
            P(("grp", "bead"), None, "space"),
            P(("grp", "bead"), None, "space"),
            P(("grp", "space")),
            P(None, ("grp", "space")),
            P(("grp", "space")),
            P(),
            P(),
            P(),
            P(),
            P(),
            P(),
        ),
        out_specs=(P(("grp", "bead"), None, "space"), P(("grp", "bead"), None, "space")),
        check_vma=False,
    )
```

```python
import functools

import jax
import jax.numpy as jnp
import numpy as np
from jax import lax
from jax.experimental import pallas as pl
from jax.experimental.pallas import tpu as pltpu
from jax.sharding import PartitionSpec as P

HALO = 128
NC = 4
SPECIES = 4
LANES = 128
DEAD = 4096
LOG2E = 1.4426950408889634

MASS_TABLE = (1.0, 0.25, 1.5, 2.0)
SPRING_RATE = 0.2
TIME_STEP = 0.5

GATHER = ("swap", (1, 3, 2))
SPREAD = ("turn", (3, 2, 1))


def contraction_table(bead_count, kept_modes):
    rows = np.arange(kept_modes)[:, None] / kept_modes
    cols = np.arange(bead_count)[None, :] / bead_count
    angles = 2.0 * np.pi * (rows - cols)
    summed = np.ones_like(angles)
    for order in range(1, kept_modes // 2):
        summed = summed + 2.0 * np.cos(order * angles)
    summed = summed + np.cos(kept_modes // 2 * angles)
    return (summed / bead_count).astype(np.float32)


def per_species(species, values):
    picked = jnp.full(species.shape, values[0], jnp.float32)
    for kind in range(1, SPECIES):
        picked = jnp.where(species == kind, values[kind], picked)
    return picked


VMEM = pl.BlockSpec(memory_space=pltpu.VMEM)
PARAMS = pltpu.CompilerParams(vmem_limit_bytes=16 * 1024 * 1024)


def cost(micros):
    return pl.CostEstimate(
        flops=0, transcendentals=0, bytes_accessed=int(micros * 3_000_000)
    )


def at_even(axis):
    return jnp.bitwise_and(lax.axis_index(axis), 1) == 0


def split2(value):
    high = value.astype(jnp.bfloat16)
    low = (value - high.astype(jnp.float32)).astype(jnp.bfloat16)
    return high, low


def dot(lhs, rhs):
    return lax.dot_general(
        lhs, rhs, (((1,), (0,)), ((), ())), preferred_element_type=jnp.float32
    )


def dot_nt(lhs, rhs):
    return lax.dot_general(
        lhs, rhs, (((1,), (1,)), ((), ())), preferred_element_type=jnp.float32
    )


def prepare_kernel(slab_atoms, block_start, *refs):
    held, outs = refs[:9], refs[9:18]
    copied, sems = refs[18:27], refs[27]
    copies = [
        pltpu.make_async_copy(src, dst, sems.at[i])
        for i, (src, dst) in enumerate(zip(held, copied, strict=True))
    ]
    for copy in copies:
        copy.start()
    slots, counts, species, w1, emb, w2, w3, rates, wout = copied
    code, kinds, t1, t2, t3, l2, l3, rates_b, wout_b = outs
    for copy in copies[:3]:
        copy.wait()
    kinds[...] = species[...].astype(jnp.float32)

    slab = lax.axis_index("space")
    last = lax.axis_size("space") - 1
    lowest = jnp.where(slab == 0, HALO, 0)
    highest = jnp.where(slab == last, slab_atoms + HALO, slab_atoms + 2 * HALO)
    word = slots[...]
    slot_ids = lax.broadcasted_iota(jnp.int32, word.shape, 0)
    lane_ids = lax.broadcasted_iota(jnp.int32, word.shape, 1)
    live = (slot_ids < counts[...]) & (word >= lowest) & (word < highest)
    band = word - block_start() - jnp.bitwise_and(lane_ids, -LANES)
    code[...] = jnp.where(live, band, band + DEAD)

    for copy in copies[3:]:
        copy.wait()
    chan = w1.shape[1]
    t1[0:chan, :], t1[chan : 2 * chan, :] = split2(w1[...].T)
    e = emb[...]
    eh = e.astype(jnp.bfloat16).astype(jnp.float32)
    el = (e - eh).astype(jnp.bfloat16).astype(jnp.float32)
    rest = jnp.zeros((chan - 3 * SPECIES, e.shape[1]), jnp.float32)
    terms = jnp.concatenate([eh, el, e - eh - el, rest], axis=0)
    t1[2 * chan : 3 * chan, :] = terms.astype(jnp.bfloat16)
    for src, fwd, bwd in ((w2, t2, l2), (w3, t3, l3)):
        hid = src.shape[0]
        fwd[0:hid, :], fwd[hid : 2 * hid, :] = split2(src[...].T)
        bwd[0:hid, :], bwd[hid : 2 * hid, :] = split2(src[...])
    count = rates.shape[1]
    tall = jnp.concatenate(
        [rates[...], jnp.zeros((1, LANES - count), jnp.float32)], axis=1
    )
    rates_b[...] = jnp.broadcast_to(tall, (LANES, LANES)).T[0:count, :]
    wout_b[...] = jnp.broadcast_to(wout[...], wout_b.shape)


def prepare(slab_atoms, block_start, slots, counts, species, w1, emb, w2, w3, rates, wout):
    hid, chan = w1.shape
    shapes = [
        (3 * chan, hid),
        (2 * hid, hid),
        (2 * hid, hid),
        (2 * hid, hid),
        (2 * hid, hid),
    ]
    out_shape = [
        pltpu.VMEM(slots.shape, jnp.int32),
        pltpu.VMEM(species.shape, jnp.float32),
    ]
    out_shape += [pltpu.VMEM(s, jnp.bfloat16) for s in shapes]
    out_shape += [
        pltpu.VMEM((rates.shape[0], LANES), jnp.float32),
        pltpu.VMEM((8, hid), jnp.float32),
    ]
    operands = (
        slots,
        counts[None, :],
        species,
        w1,
        emb.T,
        w2,
        w3,
        rates[None, :],
        wout[None, :],
    )
    code, kinds, *pairs, rates_b, wout_b = pl.pallas_call(
        functools.partial(prepare_kernel, slab_atoms, block_start),
        out_shape=out_shape,
        in_specs=[pl.BlockSpec(memory_space=pltpu.HBM)] * len(operands),
        out_specs=[VMEM] * len(out_shape),
        scratch_shapes=[pltpu.VMEM(x.shape, x.dtype) for x in operands]
        + [pltpu.SemaphoreType.DMA((len(operands),))],
        cost_estimate=cost(1.2),
        name="prepare",
    )(*operands)
    return code, kinds, pairs, rates_b, wout_b


def neighbours(places, word, g, off, kind, dist):
    src = [
        [
            jnp.broadcast_to(
                places[4 * (g + q) + c : 4 * (g + q) + c + 1, :], (8, LANES)
            )
            for q in range(3)
        ]
        for c in range(4)
    ]
    for o in range(word.shape[0] // 8):
        rows = slice(8 * o, 8 * o + 8)
        lane = jnp.bitwise_and(word[rows, :], LANES - 1)
        part = jnp.bitwise_and(word[rows, :], DEAD - 1)
        is0 = part < LANES
        is1 = part < 2 * LANES
        got = []
        for c in range(4):
            x0, x1, x2 = (
                jnp.take_along_axis(src[c][q], lane, axis=1) for q in range(3)
            )
            got.append(jnp.where(is0, x0, jnp.where(is1, x1, x2)))
        total = None
        for c in range(3):
            diff = got[c] - src[c][1]
            off[c, rows, :] = diff
            total = diff * diff if total is None else total + diff * diff
        dist[rows, :] = total
        kind[rows, :] = jnp.where(word[rows, :] >= DEAD, -1.0, got[3])


def describe(kind, dist, rates, rad, desc):
    slots = kind.shape[0]
    rate_count = rates.shape[0]
    octets = rate_count // 8
    rate8 = [rates[8 * o : 8 * o + 8, :] * (-LOG2E) for o in range(octets)]
    acc = [[jnp.zeros((8, LANES), jnp.float32)] * octets for _ in range(SPECIES)]
    for n in range(slots):
        kind_n = jnp.broadcast_to(kind[n : n + 1, :], (8, LANES))
        dist_n = jnp.broadcast_to(dist[n : n + 1, :], (8, LANES))
        masks = [kind_n == float(s) for s in range(SPECIES)]
        for o in range(octets):
            radial = jnp.exp2(rate8[o] * dist_n)
            first = n * rate_count + 8 * o
            rad[first : first + 8, :] = radial
            for s in range(SPECIES):
                acc[s][o] = jnp.where(masks[s], acc[s][o] + radial, acc[s][o])
    for s in range(SPECIES):
        for o in range(octets):
            first = s * rate_count + 8 * o
            desc[first : first + 8, :] = acc[s][o]


def centre_factor(centre, chan):
    ids = lax.broadcasted_iota(jnp.int32, (chan, LANES), 0)
    ids = jnp.where(ids < 3 * SPECIES, jnp.bitwise_and(ids, SPECIES - 1), -1)
    onehot = jnp.where(ids.astype(jnp.float32) == centre, 1.0, 0.0)
    return onehot.T.astype(jnp.bfloat16)


def left_factor(desc, centre):
    high, low = split2(desc[...].T)
    return jnp.concatenate([high, high, low, centre], axis=1)


def dense(x, pair):
    high, low = split2(x)
    rows = pair.shape[0] // 2
    right = jnp.concatenate([pair[...], pair[0:rows, :]], axis=0)
    return dot(jnp.concatenate([high, high, low], axis=1), right)


def act(x):
    sig = 0.5 + 0.5 * jnp.tanh(0.5 * x)
    value = x * sig
    return value, sig + value * (1.0 - sig)


def forward_layers(pairs, wout):
    t1, t2, t3 = pairs
    chan = t1.shape[0] // 3
    first = jnp.concatenate([t1[0 : 2 * chan, :], t1[0:chan, :], t1[2 * chan :, :]], axis=0)

    def one(left):
        return act(dot(left, first))

    def two(state):
        value, s1 = state
        return act(dense(value, t2)), s1

    def three(state):
        (value, s2), s1 = state
        return s1, s2, wout[0:1, :] * act(dense(value, t3))[1]

    return one, two, three


def backward_layers(pairs):
    t1, l2, l3 = pairs
    chan = t1.shape[0] // 3

    def three(state):
        s1, s2, grad = state
        return s1, dense(grad, l3) * s2

    def two(state):
        s1, grad = state
        return dense(grad, l2) * s1

    def one(grad):
        high, low = split2(grad)
        last = [t1[0:chan, :], t1[chan : 2 * chan, :], t1[0:chan, :]]
        return dot_nt(
            jnp.concatenate(last, axis=1), jnp.concatenate([high, high, low], axis=1)
        )

    return three, two, one


def through(layers, states):
    for layer in layers:
        states = [layer(state) for state in states]
    return states


def slot_slopes(grad, kind, rates, rad, slope):
    slots = kind.shape[0]
    rate_count = rates.shape[0]
    octets = rate_count // 8
    grads = [
        [
            grad[s * rate_count + 8 * o : s * rate_count + 8 * o + 8, :]
            * rates[8 * o : 8 * o + 8, :]
            for o in range(octets)
        ]
        for s in range(SPECIES)
    ]
    for n in range(slots):
        kind_n = jnp.broadcast_to(kind[n : n + 1, :], (8, LANES))
        masks = [kind_n == float(s) for s in range(SPECIES - 1)]
        total = None
        for o in range(octets):
            picked = grads[SPECIES - 1][o]
            for s in range(SPECIES - 1):
                picked = jnp.where(masks[s], grads[s][o], picked)
            first = n * rate_count + 8 * o
            term = picked * rad[first : first + 8, :]
            total = term if total is None else total + term
        slope[n : n + 1, :] = jnp.sum(total, axis=0, keepdims=True)


def pair_forces(word, slope, off, pair, rel):
    sums = [jnp.zeros((8, LANES), jnp.float32)] * 3
    for o in range(word.shape[0] // 8):
        rows = slice(8 * o, 8 * o + 8)
        part = jnp.bitwise_and(word[rows, :], DEAD - 1)
        rel[0, rows, :] = jnp.bitwise_and(part, 63).astype(jnp.float32)
        rel[1, rows, :] = jnp.right_shift(part, 6).astype(jnp.float32)
        twice = jnp.where(word[rows, :] >= DEAD, 0.0, 2.0 * slope[rows, :])
        for c in range(3):
            force = twice * off[c, rows, :]
            sums[c] = sums[c] + force
            high = force.astype(jnp.bfloat16).astype(jnp.float32)
            pair[2 * c, rows, :] = high
            pair[2 * c + 1, rows, :] = force - high
    return [jnp.sum(x, axis=0, keepdims=True) for x in sums]


def scatter(pair, rel, slots, out, block0, centre):
    half = jnp.bfloat16
    low_ids = lax.broadcasted_iota(jnp.int32, (64, LANES), 0).astype(half)
    high_ids = lax.broadcasted_iota(jnp.int32, (16, LANES), 0)
    high_ids = jnp.bitwise_and(high_ids, 7).astype(half)
    ones, zeros = jnp.ones((64, LANES), half), jnp.zeros((64, LANES), half)
    total = jnp.zeros((48, 64), jnp.float32)
    for n in range(0, slots, 2):
        lefts, rights = [], []
        for k in (n, n + 1):
            low = jnp.broadcast_to(rel[0, k : k + 1, :], (16, LANES)).astype(half)
            high = jnp.broadcast_to(rel[1, k : k + 1, :], (16, LANES)).astype(half)
            low = jnp.concatenate([low] * 4, axis=0)
            rights.append(jnp.where(low_ids == low, ones, zeros))
            hit = high_ids == high
            for c in range(3):
                terms = [
                    jnp.broadcast_to(pair[2 * c + i, k : k + 1, :], (8, LANES))
                    for i in range(2)
                ]
                terms = jnp.concatenate(terms, axis=0).astype(half)
                lefts.append(jnp.where(hit, terms, zeros[0:16]))
        lefts = [jnp.concatenate(lefts[0:3], axis=0), jnp.concatenate(lefts[3:6], axis=0)]
        total = total + dot_nt(
            jnp.concatenate(lefts, axis=1), jnp.concatenate(rights, axis=1)
        )
    for c in range(3):
        merged = total[16 * c : 16 * c + 8, :] + total[16 * c + 8 : 16 * c + 16, :]
        for q in range(3):
            row = 4 * (block0 + q) + c
            both = jnp.concatenate(
                [merged[2 * q : 2 * q + 1, :], merged[2 * q + 1 : 2 * q + 2, :]], axis=1
            )
            if q == 1 and centre is not None:
                both = both - centre[c]
            out[row : row + 1, :] = out[row : row + 1, :] + both


def inner_kernel(
    own, code, rates, t1, t2, t3, wout, off, kind, rad, state, centres, dist, desc
):
    chan = desc.shape[1]
    for i, g in enumerate((0, kind.shape[0] + 1)):
        centres[i] = centre_factor(own[4 * g + 3 : 4 * g + 4, :], chan)
    lefts = []
    for i in range(kind.shape[0]):
        word = code[:, (i + 1) * LANES : (i + 2) * LANES]
        neighbours(own, word, i, off.at[i], kind.at[i], dist.at[i])
        describe(kind.at[i], dist.at[i], rates, rad.at[i], desc.at[i])
        row = 4 * (i + 1) + 3
        centre = centre_factor(own[row : row + 1, :], chan)
        lefts.append(left_factor(desc.at[i], centre))
    states = through(forward_layers((t1, t2, t3), wout), lefts)
    for i, values in enumerate(states):
        for j, value in enumerate(values):
            state[i, j] = value


def inner_stage(own, code, rates, pairs, wout, count):
    slots = code.shape[0]
    rate_count = rates.shape[0]
    chan = SPECIES * rate_count
    out_shape = [
        pltpu.VMEM((count, 3, slots, LANES), jnp.float32),
        pltpu.VMEM((count, slots, LANES), jnp.float32),
        pltpu.VMEM((count, slots * rate_count, LANES), jnp.float32),
        pltpu.VMEM((count, 3, LANES, wout.shape[1]), jnp.float32),
        pltpu.VMEM((2, LANES, chan), jnp.bfloat16),
    ]
    return pl.pallas_call(
        inner_kernel,
        out_shape=out_shape,
        in_specs=[VMEM] * 7,
        out_specs=[VMEM] * 5,
        scratch_shapes=[
            pltpu.VMEM((count, slots, LANES), jnp.float32),
            pltpu.VMEM((count, chan, LANES), jnp.float32),
        ],
        compiler_params=PARAMS,
        cost_estimate=cost(1.0),
        name="inner_forward",
    )(own, code, rates, *pairs[:3], wout)


def outer_kernel(direct, inner, *refs):
    refs = list(refs)

    def take(count):
        taken = refs[:count]
        del refs[:count]
        return taken

    blocks = take(3 if direct else 1)
    code, *pairs, rates, wout = take(9 - 1)
    state_inner, centres = take(2) if inner else (None, None)
    out = take(1)[0]
    to_inner = take(1)[0] if direct else None
    grad_inner = take(1)[0] if inner else None
    places, off, kind, dist, rad, desc, grad, pair, rel, beyond, pulled = refs
    slots, block = code.shape
    groups = block // LANES
    stages = [
        (code[:, g * LANES : (g + 1) * LANES], places, g, out)
        for g in sorted({0, groups - 1})
    ]
    if direct:
        own, got_outer, got_inner = blocks
        even = at_even("space")
        first, last = own[0:4, :], own[4 * groups - 4 :, :]
        near, far = got_outer[0:4, :], got_outer[4:8, :]
        places[0:4, :] = jnp.where(even, far, got_inner[...])
        places[4 : 4 * groups + 4, :] = own[...]
        places[4 * groups + 4 :, :] = jnp.where(even, got_inner[...], near)
        beyond[0:4, :] = jnp.where(even, near, last)
        beyond[4:8, :] = jnp.where(even, far, near)
        beyond[8:12, :] = jnp.where(even, first, far)
        slab = lax.axis_index("space")
        at_end = (slab == 0) | (slab == lax.axis_size("space") - 1)
        word = got_outer[8:, :].astype(jnp.int32)
        word = jnp.where(at_end, jnp.bitwise_or(word, DEAD), word)
        stages.append((word, beyond, 0, pulled))
        pulled[...] = jnp.zeros_like(pulled)
    else:
        places[...] = blocks[0][...]
    def describe_group(i):
        word, rows, g, _ = stages[i]
        neighbours(rows, word, g, off.at[i], kind.at[i], dist.at[i])
        describe(kind.at[i], dist.at[i], rates, rad.at[i], desc.at[i])
        row = 4 * (g + 1) + 3
        if inner and rows is places:
            centre = centres[i]
        else:
            centre = centre_factor(rows[row : row + 1, :], desc.shape[1])
        return left_factor(desc.at[i], centre)

    t1, t2, t3, l2, l3 = pairs
    layers = forward_layers((t1, t2, t3), wout)
    states = through(layers, [describe_group(i) for i in range(len(stages))])
    layers = backward_layers((t1, l2, l3))
    if inner:
        states += [[state_inner[i, j] for j in range(3)] for i in range(inner)]
    slopes = through(layers, states)
    for i in range(len(stages)):
        grad[i] = slopes[i]
    for i in range(len(stages), len(slopes)):
        grad_inner[i - len(stages)] = slopes[i]

    out[...] = jnp.zeros_like(out)
    for i, (word, rows, g, target) in enumerate(stages):
        slope = dist.at[i]
        slot_slopes(grad.at[i], kind.at[i], rates, rad.at[i], slope)
        centre = pair_forces(word, slope, off.at[i], pair.at[i], rel.at[i])
        centre = None if rows is beyond else centre
        scatter(pair.at[i], rel.at[i], slots, target, g, centre)
    if direct:
        out[4:8, :] += jnp.where(even, pulled[8:12, :], 0.0)
        out[4 * groups : 4 * groups + 4, :] += jnp.where(even, 0.0, pulled[0:4, :])
        to_inner[...] = jnp.where(even, out[4 * groups + 4 :, :], out[0:4, :])


def outer_stage(blocks, code, pairs, rates, wout, state_inner):
    slots, block = code.shape
    rate_count = rates.shape[0]
    chan = SPECIES * rate_count
    groups = block // LANES
    count = len({0, groups - 1})
    inner = groups - count
    direct = len(blocks) > 1
    f32 = jnp.float32
    out_shape = [pltpu.VMEM((4 * (groups + 2), LANES), f32)]
    operands = [*blocks, code, *pairs, rates, wout]
    if direct:
        out_shape.append(pltpu.VMEM((4, LANES), f32))
        count += 1
    if inner:
        out_shape.append(pltpu.VMEM((inner, chan, LANES), f32))
        operands += state_inner
    return pl.pallas_call(
        functools.partial(outer_kernel, direct, inner),
        out_shape=out_shape,
        in_specs=[VMEM] * len(operands),
        out_specs=[VMEM] * len(out_shape),
        scratch_shapes=[
            pltpu.VMEM((4 * (groups + 2), LANES), f32),
            pltpu.VMEM((count, 3, slots, LANES), f32),
            pltpu.VMEM((count, slots, LANES), f32),
            pltpu.VMEM((count, slots, LANES), f32),
            pltpu.VMEM((count, slots * rate_count, LANES), f32),
            pltpu.VMEM((count, chan, LANES), f32),
            pltpu.VMEM((count, chan, LANES), f32),
            pltpu.VMEM((count, 6, slots, LANES), f32),
            pltpu.VMEM((count, 2, slots, LANES), jnp.float32),
            pltpu.VMEM((16, LANES), f32),
            pltpu.VMEM((16, LANES), f32),
        ],
        compiler_params=PARAMS,
        cost_estimate=cost(3.0),
        name="outer_forces",
    )(*operands)


def inner_force_kernel(code, rates, off, kind, rad, grad, out, slope, pair, rel):
    slots = code.shape[0]
    out[...] = jnp.zeros_like(out)
    for i in range(kind.shape[0]):
        word = code[:, (i + 1) * LANES : (i + 2) * LANES]
        slot_slopes(grad.at[i], kind.at[i], rates, rad.at[i], slope.at[i])
        centre = pair_forces(word, slope.at[i], off.at[i], pair.at[i], rel.at[i])
        scatter(pair.at[i], rel.at[i], slots, out, i, centre)


def inner_forces(code, rates, off, kind, rad, grad):
    slots, block = code.shape
    count = kind.shape[0]
    return pl.pallas_call(
        inner_force_kernel,
        out_shape=pltpu.VMEM((block // LANES * 4, LANES), jnp.float32),
        in_specs=[VMEM] * 6,
        out_specs=VMEM,
        scratch_shapes=[
            pltpu.VMEM((count, slots, LANES), jnp.float32),
            pltpu.VMEM((count, 6, slots, LANES), jnp.float32),
            pltpu.VMEM((count, 2, slots, LANES), jnp.float32),
        ],
        compiler_params=PARAMS,
        cost_estimate=cost(1.2),
        name="inner_forces",
    )(code, rates, off, kind, rad, grad)


def combine_kernel(inner, force, *refs):
    *rest, got_inner, out = refs
    total = force[4 : force.shape[0] - 4, :]
    if inner:
        total = total + rest[0][...]
    even = at_even("space")
    out[...] = total
    out[0:4, :] += jnp.where(even, 0.0, got_inner[...])
    out[out.shape[0] - 4 :, :] += jnp.where(even, got_inner[...], 0.0)


def combine(force, inner, got_inner):
    operands = [force, *inner, got_inner]
    return pl.pallas_call(
        functools.partial(combine_kernel, len(inner)),
        out_shape=pltpu.VMEM((force.shape[0] - 8, LANES), jnp.float32),
        in_specs=[VMEM] * len(operands),
        out_specs=VMEM,
        compiler_params=PARAMS,
        cost_estimate=cost(0.1),
        name="combine",
    )(*operands)


def bead_rows(array):
    beads, comps, atoms = array.shape
    split = array.reshape(beads, comps, atoms // LANES, LANES)
    return split.transpose(1, 2, 0, 3).reshape(-1, LANES)


def from_bead_rows(rows, shape):
    beads, comps, atoms = shape
    split = rows.reshape(comps, atoms // LANES, beads, LANES)
    return split.transpose(2, 0, 1, 3).reshape(shape)


def contract_kernel(table, beads, *refs):
    blocks, species, code = arranged(GATHER, refs), refs[NC], refs[NC + 1]
    out, to_inner, to_outer = refs[NC + 2 :]
    tiles = species.shape[0]
    weights = [
        [share(GATHER, r, table[r, j], table[-r % NC, j]) for j in range(beads)]
        for r in range(NC)
    ]
    for t in range(tiles):
        for c in range(3):
            total = None
            for r in range(NC):
                for j in range(beads):
                    row = (c * tiles + t) * beads + j
                    term = weights[r][j] * blocks[r][row : row + 1, :]
                    total = term if total is None else total + term
            out[4 * t + c : 4 * t + c + 1, :] = total
        out[4 * t + 3 : 4 * t + 4, :] = species[t : t + 1, :]
    even = at_even("space")
    last = code.shape[1] - LANES
    to_inner[...] = jnp.where(even, out[4 * tiles - 4 :, :], out[0:4, :])
    to_outer[0:8, :] = jnp.where(even, out[0:8, :], out[4 * tiles - 8 :, :])
    to_outer[8:, :] = jnp.where(even, code[:, 0:LANES], code[:, last:]).astype(jnp.float32)


def contract(table, beads, blocks, species, code):
    return pl.pallas_call(
        functools.partial(contract_kernel, table, beads),
        out_shape=[
            pltpu.VMEM((4 * species.shape[0], LANES), jnp.float32),
            pltpu.VMEM((4, LANES), jnp.float32),
            pltpu.VMEM((8 + code.shape[0], LANES), jnp.float32),
        ],
        in_specs=[VMEM] * (NC + 2),
        out_specs=[VMEM] * 3,
        compiler_params=PARAMS,
        cost_estimate=cost(0.2),
        name="contract",
    )(blocks[0], *(blocks[r] for r in GATHER[1]), species, code)


def masses_of(species):
    return per_species(species, MASS_TABLE)


def spring_kernel(beads, own, before, after, momenta, species, out):
    tiles = species.shape[0]
    pull = TIME_STEP * SPRING_RATE * masses_of(species[...])

    def side(row, ref, other):
        taken = ref[row : row + 1, :]
        if GATHER[0] == "turn":
            return taken
        return jnp.where(at_even("bead"), other[row : row + 1, :], taken)

    for m in range(3 * tiles):
        t, first, last = m % tiles, m * beads, m * beads + beads - 1
        for row in range(first, last + 1):
            here = own[row : row + 1, :]
            if row > first:
                below = own[row - 1 : row, :]
            else:
                below = side(last, before, after)
            if row < last:
                above = own[row + 1 : row + 2, :]
            else:
                above = side(first, after, before)
            laplace = 2.0 * here - below - above
            out[row : row + 1, :] = momenta[row : row + 1, :] - pull[t : t + 1, :] * laplace


def spring_kick(beads, own, before, after, momenta, species):
    return pl.pallas_call(
        functools.partial(spring_kernel, beads),
        out_shape=pltpu.VMEM(own.shape, jnp.float32),
        in_specs=[VMEM] * 5,
        out_specs=VMEM,
        compiler_params=PARAMS,
        cost_estimate=cost(0.8),
        name="spring_kick",
    )(own, before, after, momenta, species)


def expand_kernel(table, beads, *refs):
    forces, kicked, species = arranged(SPREAD, refs), refs[NC], refs[NC + 1]
    momenta, displacement = refs[NC + 2 :]
    tiles = species.shape[0]
    scale = TIME_STEP * beads * NC / NC
    weights = [
        [
            share(SPREAD, r, scale * table[-r % NC, j], scale * table[r, j])
            for j in range(beads)
        ]
        for r in range(NC)
    ]
    drift = per_species(species[...], [TIME_STEP / m for m in MASS_TABLE])
    for c in range(3):
        for t in range(tiles):
            pulls = [force[4 * t + c : 4 * t + c + 1, :] for force in forces]
            for j in range(beads):
                row = (c * tiles + t) * beads + j
                total = kicked[row : row + 1, :]
                for r in range(NC):
                    total = total + weights[r][j] * pulls[r]
                momenta[row : row + 1, :] = total
                displacement[row : row + 1, :] = drift[t : t + 1, :] * total


def expand(table, beads, forces, kicked, species):
    shape = jax.ShapeDtypeStruct(kicked.shape, jnp.float32)
    return pl.pallas_call(
        functools.partial(expand_kernel, table, beads),
        out_shape=[shape, shape],
        in_specs=[VMEM] * (NC + 2),
        out_specs=[VMEM] * 2,
        compiler_params=PARAMS,
        cost_estimate=cost(0.8),
        name="expand",
    )(forces[0], *(forces[r] for r in SPREAD[1]), kicked, species)


def swap_inner(block):
    count = lax.axis_size("space")
    return lax.ppermute(block, "space", [(i, i ^ 1) for i in range(count)])


def swap_outer(block):
    count = lax.axis_size("space")
    pairs = [(i, (i + 1) % count if i % 2 else (i - 1) % count) for i in range(count)]
    return lax.ppermute(block, "space", pairs)


def arranged(plan, refs):
    return [refs[0]] + [refs[1 + plan[1].index(r)] for r in range(1, NC)]


def share(plan, distance, behind, ahead):
    behind, ahead = float(behind), float(ahead)
    if plan[0] == "turn" or behind == ahead or distance == 0:
        return behind
    return jnp.where(at_even("bead"), ahead, behind)


def around(plan, block):
    count = lax.axis_size("bead")
    blocks = [block]
    for r in range(1, count):
        if plan[0] == "turn":
            pairs = [(i, (i + r) % count) for i in range(count)]
        else:
            pairs = [(i, i ^ r) for i in range(count)]
        blocks.append(lax.ppermute(block, "bead", pairs))
    return blocks


def on_device(
    positions,
    momenta,
    species,
    neighbour_index,
    neighbour_count,
    radial_rates,
    weight_input,
    embedding,
    weight_middle,
    weight_deeper,
    weight_output,
):
    bead_dev = positions.shape[0]
    atom_dev = positions.shape[2]
    bead_groups = lax.axis_size("bead")
    bead_count = bead_dev * bead_groups
    table = contraction_table(bead_count, NC)
    place = lax.axis_index("bead")
    tiles = atom_dev // LANES
    direct = bead_groups == NC and tiles > 1
    block_size = atom_dev * NC // bead_groups

    if direct:
        block_start = 0
        slots, counts = neighbour_index, neighbour_count
    else:
        block_start = (place // NC) * block_size
        slots = lax.dynamic_slice_in_dim(neighbour_index, block_start, block_size, 1)
        counts = lax.dynamic_slice_in_dim(neighbour_count, block_start, block_size, 0)
    code, kinds, pairs, rates, wout = prepare(
        atom_dev,
        lambda: 0 if direct else (lax.axis_index("bead") // NC) * block_size,
        slots,
        counts,
        species.reshape(tiles, LANES),
        weight_input,
        embedding,
        weight_middle,
        weight_deeper,
        radial_rates,
        weight_output,
    )

    if direct:
        blocks = around(GATHER, bead_rows(positions))
        own, to_inner, to_outer = contract(table, bead_dev, blocks, kinds, code)
    else:
        replica = place % NC
        everything = lax.all_gather(positions, "bead", axis=0, tiled=True)
        weights = lax.dynamic_index_in_dim(jnp.asarray(table), replica, 0, keepdims=False)
        contracted = jnp.sum(weights[:, None, None] * everything, axis=0)
        stacked = contracted.reshape(3, tiles, LANES).transpose(1, 0, 2)
        own = jnp.concatenate([stacked, kinds[:, None]], axis=1).reshape(-1, LANES)

    if direct:
        got_outer, got_inner = swap_outer(to_outer), swap_inner(to_inner)
        inner_count = max(tiles - 2, 0)
        state_inner, others = None, []
        if inner_count:
            off, kind, rad, *state_inner = inner_stage(
                own, code, rates, pairs, wout, inner_count
            )
        force, to_inner, *grad_inner = outer_stage(
            [own, got_outer, got_inner], code, pairs, rates, wout, state_inner
        )
        got_inner = swap_inner(to_inner)
        if inner_count:
            others = [inner_forces(code, rates, off, kind, rad, *grad_inner)]
        forces = around(SPREAD, combine(force, others, got_inner))
        kicked = spring_kick(
            bead_dev, blocks[0], blocks[1], blocks[NC - 1], bead_rows(momenta), kinds
        )
        moved = expand(table, bead_dev, forces, kicked, kinds)
        return tuple(from_bead_rows(rows, positions.shape) for rows in moved)

    even = at_even("space")
    bottom, top = own[:4], own[4 * tiles - 4 :]
    got_inner = swap_inner(jnp.where(even, top, bottom))
    got_outer = swap_outer(jnp.where(even, bottom, top))
    window = jnp.concatenate(
        [
            jnp.where(even, got_outer, got_inner),
            own,
            jnp.where(even, got_inner, got_outer),
        ],
        axis=0,
    )
    first = block_start // LANES * 4
    groups = block_size // LANES
    window = lax.dynamic_slice_in_dim(window, first, 4 * (groups + 2), 0)
    state_inner = None
    if groups > 2:
        inside = window[4 : 4 * groups + 4]
        off, kind, rad, *state_inner = inner_stage(
            inside, code, rates, pairs, wout, groups - 2
        )
    force, *grad_inner = outer_stage([window], code, pairs, rates, wout, state_inner)
    if groups > 2:
        force = force.at[4 : 4 * groups + 4].add(
            inner_forces(code, rates, off, kind, rad, *grad_inner)
        )
    partial = jnp.zeros((4 * (tiles + 2), LANES), jnp.float32)
    partial = lax.dynamic_update_slice_in_dim(partial, force, first, 0)
    chosen = (jnp.arange(NC, dtype=jnp.int32) == replica).astype(jnp.float32)
    force = lax.psum(chosen[:, None, None] * partial[None], "bead")

    lower, middle, upper = force[:, :4], force[:, 4:-4], force[:, -4:]
    got_inner = swap_inner(jnp.where(even, upper, lower))
    got_outer = swap_outer(jnp.where(even, lower, upper))
    middle = jnp.concatenate(
        [
            middle[:, :4] + jnp.where(even, got_outer, got_inner),
            middle[:, 4:-4],
            middle[:, -4:] + jnp.where(even, got_inner, got_outer),
        ],
        axis=1,
    )

    first = place * bead_dev
    below = lax.dynamic_index_in_dim(everything, (first - 1) % bead_count, 0)
    above = lax.dynamic_index_in_dim(everything, (first + bead_dev) % bead_count, 0)
    whole = middle.reshape(NC, tiles, 4, LANES).transpose(0, 2, 1, 3)[:, :3]
    whole = whole.reshape(NC, 3, atom_dev)
    columns = lax.dynamic_slice_in_dim(jnp.asarray(table), first, bead_dev, 1)
    expanded = jnp.sum(columns[:, :, None, None] * whole[:, None], axis=0)
    expanded = bead_count / NC * expanded
    masses = masses_of(species)
    cycle = jnp.concatenate([below, positions, above], axis=0)
    laplace = 2.0 * positions - cycle[:-2] - cycle[2:]
    spring = -SPRING_RATE * masses * laplace
    momenta_next = momenta + TIME_STEP * (spring + expanded)
    return (momenta_next, TIME_STEP * momenta_next / masses)


def solution(mesh):
    return jax.shard_map(
        on_device,
        mesh=mesh,
        in_specs=(
            P(("grp", "bead"), None, "space"),
            P(("grp", "bead"), None, "space"),
            P(("grp", "space")),
            P(None, ("grp", "space")),
            P(("grp", "space")),
            P(),
            P(),
            P(),
            P(),
            P(),
            P(),
        ),
        out_specs=(P(("grp", "bead"), None, "space"), P(("grp", "bead"), None, "space")),
        check_vma=False,
    )
```
